256 devices in a mesh: row: 32 (over z_hi, x, y), col: 8 (over z_lo, core).
Axes of the slice: x: 4, y: 4, z: 8 (z_hi: 2, z_lo: 4; z = z_hi * 4 + z_lo), core: 2. Of those that a mesh axis runs over, the one named last changes fastest.
Arguments:
- covariance: float32 [16384, 16384], P('row', 'col'), may hold values from -1.2 to 7.2, as said below
- classes: int32 [8192], replicated, may hold values from 0 to 15
- feed_rate: float32 [16], replicated, may hold values from 0.7 to 2
- conversion_rate: float32 [16], replicated, may hold values from 0.5 to 3
- diffusion: float32 [2], replicated, may hold values from 0.3 to 2
Outputs:
- advanced: float32 [16384, 16384], P('row', 'col')
The draws below stay inside these ranges and needn't reach their ends.
Inputs may be any that keep to these rules, and one draw needn't show every extreme that they name: covariance is symmetric: entry (r, c) equals entry (c, r) exactly.
All inputs are finite; a program needn't handle non-finite values.
Results may differ from the reference program's by a relative error of at most 0.00002.
Values sent between devices are 32-bit elements; how exact they have to be, the bound alone decides.
A program may use at most 128 MiB of HBM per device.

```python
import math
import jax
import jax.numpy as jnp

VOXELS = 8192
CLASSES = 16
ORDER = 16384


def draw_covariance(key, part):
    key = jax.random.fold_in(key, 11)
    first_key, second_key = jax.random.split(key, 2)
    raw_draw = jnp.clip(0.6 * jax.random.normal(first_key, (ORDER, ORDER), jnp.float32), -1.2, 1.2)
    symmetric = 0.5 * (raw_draw + raw_draw.T)
    diag_part = jax.random.uniform(second_key, (ORDER,), jnp.float32, 2.0, 6.0)
    positions = jnp.arange(ORDER, dtype=jnp.int32)
    return symmetric.at[positions, positions].add(diag_part)


def with_ends(array, rng, smallest, high):
    spot = [jax.random.randint(jax.random.fold_in(rng, axis), (), 0, length) for axis, length in enumerate(array.shape)]
    main_axis = array.shape.index(max(array.shape))
    next_to = spot[:main_axis] + [(spot[main_axis] + 1) % array.shape[main_axis]] + spot[main_axis + 1:]
    return array.at[tuple(spot)].set(smallest).at[tuple(next_to)].set(high)


def setup_inputs(seed: int = 0) -> dict:
    streams_of = jax.random.split(jax.random.key(seed), 6)
    return {
        "covariance": draw_covariance(jax.random.fold_in(streams_of[5], 71), 0),
        "classes": with_ends(jax.random.randint(streams_of[1], (VOXELS,), 0, CLASSES), jax.random.fold_in(streams_of[1], 1), 0, CLASSES - 1).astype(jnp.int32),
        "feed_rate": jnp.clip(jnp.exp(jax.random.uniform(streams_of[2], (CLASSES,), jnp.float32, math.log(0.7), math.log(2.0))), 0.7, 2.0),
        "conversion_rate": jnp.clip(jnp.exp(jax.random.uniform(streams_of[3], (CLASSES,), jnp.float32, math.log(0.5), math.log(3.0))), 0.5, 3.0),
        "diffusion": jnp.clip(jnp.exp(jax.random.uniform(streams_of[4], (2,), jnp.float32, math.log(0.3), math.log(2.0))), 0.3, 2.0),
    }


step_size = 0.04


def lookup(row_class, rate_table):
    class_ids = jnp.arange(rate_table.shape[0], dtype=jnp.int32)
    return jnp.sum(jnp.where(row_class[:, None] == class_ids[None, :], rate_table[None, :], 0.0), axis=1)


def coefficients(row_class, positions, feed_rate, conversion_rate, diffusion, voxels):
    feed_here = lookup(row_class, feed_rate)
    conv_here = lookup(row_class, conversion_rate)
    voxel_ids = positions // 2
    is_even = positions % 2 == 0
    neighbours = 2.0 - (voxel_ids == 0).astype(feed_here.dtype) - (voxel_ids == voxels - 1).astype(feed_here.dtype)
    diff_coef = jnp.where(is_even, diffusion[0], diffusion[1])
    square_feed = feed_here * feed_here
    self_coef = jnp.where(is_even, conv_here - 1.0, -square_feed) - diff_coef * neighbours
    cross_coef = jnp.where(is_even, square_feed, -conv_here)
    product_rate = feed_here * conv_here
    noise_same = jnp.where(is_even, 2.0 * feed_here + 2.0 * product_rate, 2.0 * product_rate)
    noise_cross = -2.0 * product_rate
    return self_coef, cross_coef, diff_coef, noise_same, noise_cross


def stencil_rows(padded, self_coef, cross_coef, diff_coef, is_even):
    centre = padded[2:-2]
    partner = jnp.where(is_even[:, None], padded[3:-1], padded[1:-3])
    return self_coef[:, None] * centre + cross_coef[:, None] * partner + diff_coef[:, None] * (padded[:-4] + padded[4:])


def stencil_cols(padded, self_coef, cross_coef, diff_coef, is_even):
    centre = padded[:, 2:-2]
    partner = jnp.where(is_even[None, :], padded[:, 3:-1], padded[:, 1:-3])
    return self_coef[None, :] * centre + cross_coef[None, :] * partner + diff_coef[None, :] * (padded[:, :-4] + padded[:, 4:])


def reference(covariance, classes, feed_rate, conversion_rate, diffusion):
    matrix_order = covariance.shape[0]
    positions = jnp.arange(matrix_order, dtype=jnp.int32)
    row_class = classes[positions // 2]
    self_coef, cross_coef, diff_coef, noise_same, noise_cross = coefficients(
        row_class, positions, feed_rate, conversion_rate, diffusion, VOXELS)
    is_even = positions % 2 == 0
    partner_ids = (positions + 1 - 2 * (positions % 2)).astype(jnp.int32)

    def rate_of(field):
        forward = stencil_rows(jnp.pad(field, ((2, 2), (0, 0))), self_coef, cross_coef, diff_coef, is_even)
        backward = stencil_cols(jnp.pad(field, ((0, 0), (2, 2))), self_coef, cross_coef, diff_coef, is_even)
        total = forward + backward
        total = total.at[positions, positions].add(noise_same)
        total = total.at[positions, partner_ids].add(noise_cross)
        return total

    first_rate = rate_of(covariance)
    section_cov = covariance + step_size * first_rate
    second_rate = rate_of(section_cov)
    return covariance + (0.5 * step_size) * (first_rate + second_rate)
```

```python
import functools

import jax
import jax.numpy as jnp
from jax import lax
from jax.experimental import pallas as pl
from jax.experimental.pallas import tpu as pltpu
from jax.sharding import PartitionSpec as P

STEP = 0.04
LANES = 128
PAD = 8
F32, BF16 = jnp.float32, jnp.bfloat16
MESH = pl.DeviceIdType.MESH
SIDES = [(dr, dc) for dr in (-1, 0, 1) for dc in (-1, 0, 1) if (dr, dc) != (0, 0)]


def split(value):
    high = value.astype(BF16)
    return high, (value - high.astype(F32)).astype(BF16)


def iota(shape, dim):
    return lax.broadcasted_iota(jnp.int32, shape, dim)


def advance_kernel(
    rows, panels, voxels, grid_rows, grid_cols,
    cov, classes, feed, conv, diff,
    u_ref, ge, go, full,
    vx, high, low, whi, wlo, code, half, noise, feed_of, conv_of, ext_s, ext_x, ext_a, ext_b, col,
    send_row, send_col, got_row, got_col, got_corner, tile_g,
    load_sem, edge_sem, send_sem, recv_sem,
):
    row, cols_at = lax.axis_index("row"), lax.axis_index("col")
    groups = rows // 16
    half_rows = rows // 2
    d0, d1 = diff[0] * STEP, diff[1] * STEP

    def there(dr, dc):
        ok = None
        for at, step, size in ((row, dr, grid_rows), (cols_at, dc, grid_cols)):
            if step:
                one = (at + step >= 0) & (at + step < size)
                ok = one if ok is None else ok & one
        return ok

    barrier = pltpu.get_barrier_semaphore()
    count = jnp.int32(0)
    for dr, dc in SIDES:
        ok = there(dr, dc)
        count += ok.astype(jnp.int32)

        @pl.when(ok)
        def _(dr=dr, dc=dc):
            pl.semaphore_signal(barrier, inc=1, device_id=(row + dr, cols_at + dc), device_id_type=MESH)

    def load(p):
        return pltpu.make_async_copy(
            cov.at[:, pl.ds(pl.multiple_of(p * LANES, LANES), LANES)],
            vx.at[p + 1, pl.ds(PAD, rows), :],
            load_sem.at[p],
        )

    load(0).start()
    load(panels - 1).start()

    def start_load(p, _):
        load(p).start()
        return 0

    lax.fori_loop(1, panels - 1, start_load, 0)

    zero = jnp.zeros((8, LANES), F32)
    for p in range(panels):
        vx[p + 1, 0:PAD, :] = zero
        vx[p + 1, PAD + rows : 2 * PAD + rows, :] = zero
    for i, (step, at) in enumerate(((1, 0), (-1, grid_rows - 1))):
        @pl.when(row == at)
        def _(i=i):
            got_row[i] = jnp.zeros(got_row.shape[1:], F32)
    for i, at in enumerate((0, grid_cols - 1)):
        @pl.when(cols_at == at)
        def _(i=i):
            got_col[i] = jnp.zeros(got_col.shape[1:], F32)
    for i, (dr, dc) in enumerate(((-1, -1), (-1, 1), (1, -1), (1, 1))):
        @pl.when(jnp.logical_not(there(dr, dc)))
        def _(i=i):
            got_corner[i] = zero

    ids = classes[...]
    a_all, b_all = jnp.zeros(ids.shape, F32), jnp.zeros(ids.shape, F32)
    for k in range(feed.shape[0]):
        a_all = jnp.where(ids == k, feed[k], a_all)
        b_all = jnp.where(ids == k, conv[k], b_all)
    feed_of[...] = a_all
    conv_of[...] = b_all
    class_rows = voxels // LANES

    lane8 = iota((8, LANES), 1)
    row_at = row * (half_rows // LANES)
    for t in range(half_rows // LANES):
        a = jnp.broadcast_to(feed_of[pl.ds(row_at + t, 1), :], (LANES, LANES)).T
        b = jnp.broadcast_to(conv_of[pl.ds(row_at + t, 1), :], (LANES, LANES)).T
        voxel = row * half_rows + t * LANES + iota((LANES, LANES), 0)
        near = 2.0 - (voxel == 0).astype(F32) - (voxel == voxels - 1).astype(F32)
        here = pl.ds(t * LANES, LANES)
        a2, ab = a * a, a * b
        values = (
            STEP * (b - 1.0) - d0 * near, -STEP * a2 - d1 * near, STEP * a2, -STEP * b,
        )
        for i, value in enumerate(values):
            full[i, here, :] = value
            half[i, here, :] = 0.5 * value
        noise[0, here, :] = STEP * (2.0 * a + 2.0 * ab)
        noise[1, here, :] = STEP * (2.0 * ab)
        noise[2, here, :] = STEP * (-2.0 * ab)

    first = cols_at * (panels // 2)
    lane = iota((panels // 2, LANES), 1)
    for t in range(2):
        pick = lane // 2 + (LANES // 2) * t
        for source, target in ((feed_of, ext_a), (conv_of, ext_b)):
            value = source[pl.ds(pl.multiple_of(first, panels // 2), panels // 2), :]
            target[pl.ds(8 + t, panels // 2, stride=2), :] = jnp.take_along_axis(value, pick, axis=1)
    before, after = jnp.maximum(first - 1, 0), jnp.minimum(first + panels // 2, class_rows - 1)
    for source, target in ((feed_of, ext_a), (conv_of, ext_b)):
        value = jnp.broadcast_to(source[pl.ds(before, 1), :], (8, LANES))
        target[0:8, :] = jnp.take_along_axis(value, lane8 // 2 + LANES // 2, axis=1)
        value = jnp.broadcast_to(source[pl.ds(after, 1), :], (8, LANES))
        target[8 + panels : 16 + panels, :] = jnp.take_along_axis(value, lane8 // 2, axis=1)
    shape = ext_a.shape
    lane_e = iota(shape, 1)
    even_e = lane_e % 2 == 0
    a, b = ext_a[...], ext_b[...]
    voxel = cols_at * (panels * LANES // 2) + (iota(shape, 0) - 8) * (LANES // 2) + lane_e // 2
    near = 2.0 - (voxel == 0).astype(F32) - (voxel == voxels - 1).astype(F32)
    d_e = jnp.where(even_e, d0, d1)
    ext_s[...] = STEP * jnp.where(even_e, b - 1.0, -a * a) - d_e * near
    ext_x[...] = STEP * jnp.where(even_e, a * a, -b)

    mid = slice(8, 8 + panels)
    lane = iota((panels, LANES), 1)
    even = lane % 2 == 0
    near, a, b = near[mid], a[mid], b[mid]
    d = jnp.where(even, d0, d1)
    other_d = jnp.where(even, d1, d0)

    def shifted(ref):
        here = ref[mid, :]
        left = pltpu.roll(jnp.where(lane >= LANES - 2, ref[7 : 7 + panels, :], here), 2, 1)
        right = pltpu.roll(jnp.where(lane < 2, ref[9 : 9 + panels, :], here), LANES - 2, 1)
        mate = jnp.where(even, pltpu.roll(here, LANES - 1, 1), pltpu.roll(here, 1, 1))
        return here, mate, jnp.where(even, right, left), jnp.where(even, left, right)

    s, s_mate, s_fore, s_back = shifted(ext_s)
    x, x_mate, x_fore, x_back = shifted(ext_x)
    col[0] = s
    col[1] = x
    col[2] = d
    col[3] = 1.0 + s + 0.5 * (s * s + x * x_mate + d * d * near)
    col[4] = x + 0.5 * x * (s + s_mate)
    col[5] = d + 0.5 * d * (s + s_fore)
    col[6] = d + 0.5 * d * (s + s_back)
    col[7] = 0.5 * d * d
    col[8] = 0.5 * (x * other_d + d * x_fore)
    col[9] = 0.5 * (x * other_d + d * x_back)
    ab = a * b
    same, cross = STEP * (jnp.where(even, 2.0 * a, 0.0) + 2.0 * ab), STEP * (-2.0 * ab)
    col[10] = jnp.where(even, same, cross)
    col[11] = jnp.where(even, cross, same)

    at = iota(code.shape, 1)
    code[...] = (iota(code.shape, 0) - 16 - at) * (1 - 2 * (at % 2))

    def weights(p, _):
        c = [jnp.broadcast_to(col[i, pl.ds(p, 1), :], (16, LANES)) for i in range(10)]
        none = jnp.zeros((16, LANES), F32)
        blank = jnp.zeros((96, 2 * LANES), BF16)
        whi[p, LANES + 16 : 2 * LANES - 16, :] = blank
        wlo[p, LANES + 16 : 2 * LANES - 16, :] = blank
        for i in range(10):
            k = code[16 * i : 16 * i + 16, :]
            z = k == 0, k == 1, k == 2, k == -2
            u = jnp.where(jnp.abs(k) == 4, c[7], none)
            u = jnp.where(k == 3, c[8], u)
            u = jnp.where(k == -1, c[9], u)
            u = jnp.where(z[0], c[3], jnp.where(z[1], c[4], jnp.where(z[2], c[5], jnp.where(z[3], c[6], u))))
            w = jnp.where(z[0], c[0], jnp.where(z[1], c[1], jnp.where(z[2] | z[3], c[2], none)))
            to = 2 * LANES - 16 if i == 0 else LANES if i == 9 else 16 * (i - 1)
            for value, lanes in ((u, slice(0, LANES)), (w, slice(LANES, 2 * LANES))):
                hi, lo = split(value)
                whi[p, to : to + 16, lanes] = hi
                wlo[p, to : to + 16, lanes] = lo
        return 0

    lax.fori_loop(0, panels, weights, 0)

    load(0).wait()
    load(panels - 1).wait()
    lane8 = iota((8, LANES), 1)
    sub8 = iota((8, LANES), 0)
    lane16 = iota((16, LANES), 1)
    for side, panel, start in ((0, 1, 0), (1, panels, LANES - 4)):
        packed = jnp.zeros((16, LANES), F32)
        for g in range(groups):
            piece = vx[panel, PAD + 16 * g : PAD + 16 * g + 16, :]
            turn = (4 * g - start) % LANES
            piece = pltpu.roll(piece, turn, 1) if turn else piece
            packed = jnp.where((lane16 >= 4 * g) & (lane16 < 4 * g + 4), piece, packed)
        send_col[side] = packed

    def wait_load(p, _):
        load(p).wait()
        return 0

    lax.fori_loop(1, panels - 1, wait_load, 0)
    for k in range(panels // 2):
        one, two = 2 * k + 1, 2 * k + 2
        send_row[0, 8 * k : 8 * k + 8, :] = jnp.where(sub8 < 4, vx[one, PAD : PAD + 8, :], vx[two, PAD - 4 : PAD + 4, :])
        end = PAD + rows
        send_row[1, 8 * k : 8 * k + 8, :] = jnp.where(sub8 < 4, vx[one, end - 4 : end + 4, :], vx[two, end - 8 : end, :])

    pl.semaphore_wait(barrier, count)
    tile_rows = 4 * panels

    def remote(i):
        dr, dc = SIDES[i]
        if dc == 0:
            side = 0 if dr < 0 else 1
            source, target = send_row.at[side], got_row.at[1 - side, pl.ds(8, tile_rows), :]
        elif dr == 0:
            side = 0 if dc < 0 else 1
            source, target = send_col.at[side], got_col.at[1 - side]
        else:
            panel = 1 if dc < 0 else panels
            at = PAD if dr < 0 else PAD + rows - 8
            corner = (2 if dr < 0 else 0) + (1 if dc < 0 else 0)
            source, target = vx.at[panel, pl.ds(at, 8), :], got_corner.at[corner]
        return pltpu.make_async_remote_copy(
            src_ref=source, dst_ref=target, send_sem=send_sem.at[i], recv_sem=recv_sem.at[i],
            device_id=(row + dr, cols_at + dc), device_id_type=MESH,
        )

    for i, (dr, dc) in enumerate(SIDES):
        @pl.when(there(dr, dc))
        def _(i=i):
            remote(i).start()

    def split_panel(p):
        for g in range(groups):
            e = vx[p, pl.ds(PAD + 16 * g, 8, stride=2), :]
            o = vx[p, pl.ds(PAD + 16 * g + 1, 8, stride=2), :]
            hi, lo = split(jnp.concatenate([e, o], axis=0))
            high[p, 16 * g : 16 * g + 16, :] = hi
            low[p, 16 * g : 16 * g + 16, :] = lo

    chunk = 128
    left_half = iota((chunk, LANES), 1) < LANES // 2

    def panel_step(p):
        rhs = jnp.concatenate([whi[p - 1], whi[p - 1], wlo[p - 1]], axis=0)
        for q in range(rows // chunk):
            here = pl.ds(chunk * q, chunk)
            hi, lo = high[p, here, :], low[p, here, :]
            edge_hi = jnp.where(left_half, high[p + 1, here, :], high[p - 1, here, :])
            edge_lo = jnp.where(left_half, low[p + 1, here, :], low[p - 1, here, :])
            lhs = jnp.concatenate([hi, edge_hi, lo, edge_lo, hi, edge_hi], axis=1)
            both = jnp.dot(lhs, rhs, preferred_element_type=F32)
            u_ref[p - 1, here, :] = both[:, :LANES]
            w = both[:, LANES:]
            for i in range(chunk // 16):
                g = q * (chunk // 16) + i
                at = PAD + 16 * g
                e, o = vx[p, pl.ds(at, 8, stride=2), :], vx[p, pl.ds(at + 1, 8, stride=2), :]
                e_sum = vx[p, pl.ds(at - 2, 8, stride=2), :] + vx[p, pl.ds(at + 2, 8, stride=2), :]
                o_sum = vx[p, pl.ds(at - 1, 8, stride=2), :] + vx[p, pl.ds(at + 3, 8, stride=2), :]
                c = [half[n, 8 * g : 8 * g + 8, :] for n in range(4)]
                ge[p - 1, PAD + 8 * g : PAD + 8 * g + 8, :] = (
                    e + w[16 * i : 16 * i + 8] + ((c[0] * e + c[2] * o) + (0.5 * d0) * e_sum)
                )
                go[p - 1, PAD + 8 * g : PAD + 8 * g + 8, :] = (
                    o + w[16 * i + 8 : 16 * i + 16] + ((c[1] * o + c[3] * e) + (0.5 * d1) * o_sum)
                )

    split_panel(1)
    split_panel(2)

    def middle(p, _):
        split_panel(p + 1)
        panel_step(p)
        return 0

    lax.fori_loop(2, panels, middle, 0)

    def wait_recv(dr, dc):
        @pl.when(there(-dr, -dc))
        def _():
            remote(SIDES.index((dr, dc))).wait_recv()

    wait_recv(0, 1)
    wait_recv(0, -1)
    for side, panel, start in ((0, 0, LANES - 4), (1, panels + 1, 0)):
        packed = got_col[side]
        for g in range(groups):
            turn = (start - 4 * g) % LANES
            vx[panel, PAD + 16 * g : PAD + 16 * g + 16, :] = pltpu.roll(packed, turn, 1) if turn else packed
        split_panel(panel)

    def outer(i, _):
        panel_step(1 + i * (panels - 1))
        return 0

    lax.fori_loop(0, 2, outer, 0)

    for dr, dc in SIDES:
        if dr:
            wait_recv(dr, dc)
    for side in (0, 1):
        left, right = got_corner[2 * side], got_corner[2 * side + 1]
        if side == 0:
            tile_g[0:8, :] = right
            got_row[side, 0:8, :] = left
            got_row[side, 8 + tile_rows : 16 + tile_rows, :] = tile_g[4:12, :]
        else:
            tile_g[8:16, :] = left
            got_row[side, 0:8, :] = tile_g[4:12, :]
            got_row[side, 8 + tile_rows : 16 + tile_rows, :] = right
    even8 = lane8 % 2 == 0
    upper = sub8 < 4
    species = sub8 % 2 == 0
    for side in (0, 1):
        ok = there(-1, 0) if side == 0 else there(1, 0)
        voxel = jnp.clip(row * half_rows + (-1 if side == 0 else half_rows), 0, voxels - 1)
        pick = lane8 * 0 + voxel % LANES
        a = jnp.broadcast_to(feed_of[pl.ds(voxel // LANES, 1), :], (8, LANES))
        b = jnp.broadcast_to(conv_of[pl.ds(voxel // LANES, 1), :], (8, LANES))
        a = jnp.sum(jnp.where(lane8 == pick, a, 0.0), axis=1, keepdims=True)
        b = jnp.sum(jnp.where(lane8 == pick, b, 0.0), axis=1, keepdims=True)
        end = (voxel == 0) | (voxel == voxels - 1)
        near = jnp.where(end, 1.0, 2.0)
        d_r = jnp.where(species, d0, d1)
        s_r = STEP * jnp.where(species, b - 1.0, -a * a) - d_r * near
        x_r = STEP * jnp.where(species, a * a, -b)
        for k in range(panels // 2):
            at = 8 + 8 * k
            one, two = 2 * k + 1, 2 * k + 2
            tile, left, right = (got_row[side, at + t : at + t + 8, :] for t in (0, -4, 4))
            c_s, c_x, c_d = (
                jnp.where(upper, col[i, 2 * k : 2 * k + 1, :], col[i, 2 * k + 1 : 2 * k + 2, :]) for i in range(3)
            )
            mate = jnp.where(even8, pltpu.roll(tile, LANES - 1, 1), pltpu.roll(tile, 1, 1))
            far = pltpu.roll(jnp.where(lane8 >= LANES - 2, left, tile), 2, 1) + pltpu.roll(
                jnp.where(lane8 < 2, right, tile), LANES - 2, 1
            )
            w = c_s * tile + c_x * mate + c_d * far
            row_mate = jnp.where(species, got_row[side, at + 1 : at + 9, :], got_row[side, at - 1 : at + 7, :])
            if side == 0:
                out = got_row[side, at - 2 : at + 6, :]
                inn = jnp.where(upper, vx[one, PAD - 2 : PAD + 6, :], vx[two, PAD - 6 : PAD + 2, :])
            else:
                out = got_row[side, at + 2 : at + 10, :]
                e = PAD + rows
                inn = jnp.where(upper, vx[one, e - 2 : e + 6, :], vx[two, e - 6 : e + 2, :])
            g = tile + w + 0.5 * (s_r * tile + x_r * row_mate + d_r * (out + inn))
            tile_g[8 + 8 * k : 16 + 8 * k, :] = jnp.where(ok, g, 0.0)
        for k in range(panels // 2):
            for t in (0, 1):
                p, at = 2 * k + t, 8 + 8 * k + 4 * t
                for ref, o, dd in ((ge, 0, d0), (go, 1, d1)):
                    if side == 0:
                        ref[p, 0:8, :] = tile_g[at + 2 + o - 7 : at + 2 + o + 1, :]
                        here, sub, from_ = slice(PAD, PAD + 8), 0, at + 2 + o
                    else:
                        end = PAD + half_rows
                        ref[p, end : end + 8, :] = tile_g[at + o : at + o + 8, :]
                        here, sub, from_ = slice(end - 8, end), 7, at + o - 7
                    ref[p, here, :] += jnp.where(sub8 == sub, (0.5 * dd) * got_row[side, from_ : from_ + 8, :], 0.0)

    row_voxel = row * half_rows
    col_voxel = cols_at * (panels * LANES // 2)

    def add_noise(g, t):
        c = [col[i, pl.ds(t, 1), :] for i in (0, 1, 2, 10, 11)]
        here = pl.ds(pl.multiple_of(8 * g, 8), 8)
        f = [full[i, here, :] for i in range(4)]
        n_e, n_o, n_x = (noise[i, here, :] for i in range(3))
        gap = (col_voxel + t * (LANES // 2) + lane8 // 2) - (row_voxel + 8 * g + sub8)
        on, beside = gap == 0, jnp.abs(gap) == 1
        at = pl.multiple_of(16 * g, 16)
        for start, s_r, x_r, d_r, one, two, mine, mate in (
            (at, f[0], f[2], d0, c[3], c[4], jnp.where(even8, n_e, n_x), jnp.where(even8, n_x, n_e)),
            (at + 8, f[1], f[3], d1, c[4], c[3], jnp.where(even8, n_x, n_o), jnp.where(even8, n_o, n_x)),
        ):
            centre = mine + 0.5 * ((s_r * one + x_r * two) + (c[0] * mine + c[1] * mate))
            side = 0.5 * (d_r * one + c[2] * mine)
            u_ref[t, pl.ds(start, 8), :] += jnp.where(on, centre, jnp.where(beside, side, 0.0))

    near_diagonal = (row_voxel + half_rows >= col_voxel) & (row_voxel <= col_voxel + panels * LANES // 2)

    @pl.when(near_diagonal)
    def _():
        def step(g, _):
            voxel = row_voxel + 8 * g - col_voxel
            t = (voxel + LANES) // (LANES // 2) - 2
            inside = voxel % (LANES // 2)
            for move, ok in ((0, True), (-1, inside == 0), (1, inside == LANES // 2 - 8)):
                @pl.when(ok & (t + move >= 0) & (t + move < panels))
                def _(move=move):
                    add_noise(g, t + move)
            return 0

        lax.fori_loop(0, groups, step, 0)

    for i, (dr, dc) in enumerate(SIDES):
        @pl.when(there(dr, dc))
        def _(i=i):
            remote(i).wait_send()


def finish_kernel(rows, panels, u_ref, ge, go, full, diff, out, stage, sem):
    d0, d1 = diff[0] * STEP, diff[1] * STEP
    groups = rows // 16
    wide = 2

    def store(p):
        return pltpu.make_async_copy(
            stage.at[p], out.at[:, pl.ds(pl.multiple_of(p * LANES, LANES), LANES)], sem.at[p]
        )

    def step(n, _):
        for g in range(groups):
            c = [full[i, 8 * g : 8 * g + 8, :] for i in range(4)]
            for t in range(wide):
                p = n * wide + t
                at = PAD + 8 * g
                e, o = ge[p, at : at + 8, :], go[p, at : at + 8, :]
                e_sum = ge[p, at - 1 : at + 7, :] + ge[p, at + 1 : at + 9, :]
                o_sum = go[p, at - 1 : at + 7, :] + go[p, at + 1 : at + 9, :]
                u_e, u_o = u_ref[p, 16 * g : 16 * g + 8, :], u_ref[p, 16 * g + 8 : 16 * g + 16, :]
                stage[p, pl.ds(16 * g, 8, stride=2), :] = u_e + ((c[0] * e + c[2] * o) + d0 * e_sum)
                stage[p, pl.ds(16 * g + 1, 8, stride=2), :] = u_o + ((c[1] * o + c[3] * e) + d1 * o_sum)
        for t in range(wide):
            store(n * wide + t).start()
        return 0

    lax.fori_loop(0, panels // wide, step, 0)

    def drain(p, _):
        store(p).wait()
        return 0

    lax.fori_loop(0, panels, drain, 0)


def body(covariance, classes, feed_rate, conversion_rate, diffusion):
    rows, cols = covariance.shape
    panels = cols // LANES
    voxels = classes.shape[0]
    half_rows = rows // 2
    vmem = pl.BlockSpec(memory_space=pltpu.VMEM)
    smem = pl.BlockSpec(memory_space=pltpu.SMEM)
    hbm = pl.BlockSpec(memory_space=pl.ANY)
    sizes = (lax.axis_size("row"), lax.axis_size("col"))
    results = [
        pltpu.VMEM((panels, rows, LANES), F32),
        pltpu.VMEM((panels, half_rows + 2 * PAD, LANES), F32),
        pltpu.VMEM((panels, half_rows + 2 * PAD, LANES), F32),
        pltpu.VMEM((4, half_rows, LANES), F32),
    ]
    u, ge, go, full = pl.pallas_call(
        functools.partial(advance_kernel, rows, panels, voxels, *sizes),
        out_shape=results,
        in_specs=[pl.BlockSpec(memory_space=pltpu.HBM), vmem, smem, smem, smem],
        out_specs=[vmem] * 4,
        scratch_shapes=[
            pltpu.VMEM((panels + 2, rows + 2 * PAD, LANES), F32),
            pltpu.VMEM((panels + 2, rows, LANES), BF16),
            pltpu.VMEM((panels + 2, rows, LANES), BF16),
            pltpu.VMEM((panels, 2 * LANES, 2 * LANES), BF16),
            pltpu.VMEM((panels, 2 * LANES, 2 * LANES), BF16),
            pltpu.VMEM((160, LANES), jnp.int32),
            pltpu.VMEM((4, half_rows, LANES), F32),
            pltpu.VMEM((3, half_rows, LANES), F32),
            pltpu.VMEM((voxels // LANES, LANES), F32),
            pltpu.VMEM((voxels // LANES, LANES), F32),
            pltpu.VMEM((panels + 16, LANES), F32),
            pltpu.VMEM((panels + 16, LANES), F32),
            pltpu.VMEM((panels + 16, LANES), F32),
            pltpu.VMEM((panels + 16, LANES), F32),
            pltpu.VMEM((12, panels, LANES), F32),
            pltpu.VMEM((2, 4 * panels, LANES), F32),
            pltpu.VMEM((2, 16, LANES), F32),
            pltpu.VMEM((2, 4 * panels + 16, LANES), F32),
            pltpu.VMEM((2, 16, LANES), F32),
            pltpu.VMEM((4, 8, LANES), F32),
            pltpu.VMEM((4 * panels + 16, LANES), F32),
            pltpu.SemaphoreType.DMA((panels,)),
            pltpu.SemaphoreType.DMA((4,)),
            pltpu.SemaphoreType.DMA((8,)),
            pltpu.SemaphoreType.DMA((8,)),
        ],
        compiler_params=pltpu.CompilerParams(
            collective_id=0, has_side_effects=True, vmem_limit_bytes=24 << 20
        ),
        name="halo_and_columns",
    )(covariance, classes.reshape(voxels // LANES, LANES), feed_rate, conversion_rate, diffusion)
    return pl.pallas_call(
        functools.partial(finish_kernel, rows, panels),
        out_shape=jax.ShapeDtypeStruct((rows, cols), F32),
        in_specs=[vmem] * 4 + [smem],
        out_specs=hbm,
        scratch_shapes=[
            pltpu.VMEM((panels, rows, LANES), F32),
            pltpu.SemaphoreType.DMA((panels,)),
        ],
        compiler_params=pltpu.CompilerParams(vmem_limit_bytes=24 << 20),
        name="rows",
    )(u, ge, go, full, diffusion)


def solution(mesh):
    in_specs = (P("row", "col"), P(), P(), P(), P())
    return jax.shard_map(body, mesh=mesh, in_specs=in_specs, out_specs=P("row", "col"), check_vma=False)
```

```python
import functools

import jax
import jax.numpy as jnp
from jax import lax
from jax.experimental import pallas as pl
from jax.experimental.pallas import tpu as pltpu
from jax.sharding import PartitionSpec as P

STEP = 0.04
LANES = 128
PAD = 8
F32, BF16 = jnp.float32, jnp.bfloat16
MESH = pl.DeviceIdType.MESH
SIDES = [(dr, dc) for dr in (-1, 0, 1) for dc in (-1, 0, 1) if (dr, dc) != (0, 0)]


def split(value):
    high = value.astype(BF16)
    return high, (value - high.astype(F32)).astype(BF16)


def iota(shape, dim):
    return lax.broadcasted_iota(jnp.int32, shape, dim)


def advance_kernel(
    rows, panels, voxels, grid_rows, grid_cols,
    cov, classes_in, feed_in, conv_in, diff_in,
    u_ref, ge, go, full, spread,
    vx, high, low, whi, wlo, w_one, w_two, half, noise, feed_of, conv_of, ext_s, ext_x, ext_a, ext_b, col,
    classes, feed, conv, diff, edge, send_row, send_col, got_row, got_col, got_corner, tile_g,
    load_sem, small_sem, send_sem, recv_sem,
):
    row, cols_at = lax.axis_index("row"), lax.axis_index("col")
    groups = rows // 16
    half_rows = rows // 2
    def there(dr, dc):
        ok = None
        for at, step, size in ((row, dr, grid_rows), (cols_at, dc, grid_cols)):
            if step:
                one = (at + step >= 0) & (at + step < size)
                ok = one if ok is None else ok & one
        return ok

    small = [
        pltpu.make_async_copy(a, b, small_sem.at[n])
        for n, (a, b) in enumerate((
            (classes_in, classes), (feed_in, feed), (conv_in, conv), (diff_in, diff),
            (cov.at[pl.ds(0, 8), :], edge.at[0]), (cov.at[pl.ds(rows - 8, 8), :], edge.at[1]),
        ))
    ]
    for copy in small:
        copy.start()
    def load(p):
        return pltpu.make_async_copy(
            cov.at[:, pl.ds(pl.multiple_of(p * LANES, LANES), LANES)],
            vx.at[p + 1, pl.ds(PAD, rows), :],
            load_sem.at[p],
        )

    load(0).start()
    load(panels - 1).start()

    def start_load(p, _):
        load(p).start()
        return 0

    lax.fori_loop(1, panels - 1, start_load, 0)

    barrier = pltpu.get_barrier_semaphore()
    count = jnp.int32(0)
    for dr, dc in SIDES:
        ok = there(dr, dc)
        count += ok.astype(jnp.int32)

        @pl.when(ok)
        def _(dr=dr, dc=dc):
            pl.semaphore_signal(barrier, inc=1, device_id=(row + dr, cols_at + dc), device_id_type=MESH)

    zero = jnp.zeros((8, LANES), F32)
    for p in range(panels):
        vx[p + 1, 0:PAD, :] = zero
        vx[p + 1, PAD + rows : 2 * PAD + rows, :] = zero
    for i, (step, at) in enumerate(((1, 0), (-1, grid_rows - 1))):
        @pl.when(row == at)
        def _(i=i):
            got_row[i] = jnp.zeros(got_row.shape[1:], F32)
    for i, at in enumerate((0, grid_cols - 1)):
        @pl.when(cols_at == at)
        def _(i=i):
            got_col[i] = jnp.zeros(got_col.shape[1:], F32)
    for i, (dr, dc) in enumerate(((-1, -1), (-1, 1), (1, -1), (1, 1))):
        @pl.when(jnp.logical_not(there(dr, dc)))
        def _(i=i):
            got_corner[i] = zero

    for copy in small[:4]:
        copy.wait()
    d0, d1 = diff[0] * STEP, diff[1] * STEP
    spread[0] = jnp.full((8, LANES), d0, F32)
    spread[1] = jnp.full((8, LANES), d1, F32)
    ids = classes[...]
    a_all, b_all = jnp.zeros(ids.shape, F32), jnp.zeros(ids.shape, F32)
    for k in range(feed.shape[0]):
        a_all = jnp.where(ids == k, feed[k], a_all)
        b_all = jnp.where(ids == k, conv[k], b_all)
    feed_of[...] = a_all
    conv_of[...] = b_all
    class_rows = voxels // LANES

    lane8 = iota((8, LANES), 1)
    row_at = row * (half_rows // LANES)
    for t in range(half_rows // LANES):
        a = jnp.broadcast_to(feed_of[pl.ds(row_at + t, 1), :], (LANES, LANES)).T
        b = jnp.broadcast_to(conv_of[pl.ds(row_at + t, 1), :], (LANES, LANES)).T
        voxel = row * half_rows + t * LANES + iota((LANES, LANES), 0)
        near = 2.0 - (voxel == 0).astype(F32) - (voxel == voxels - 1).astype(F32)
        here = pl.ds(t * LANES, LANES)
        a2, ab = a * a, a * b
        values = (
            STEP * (b - 1.0) - d0 * near, -STEP * a2 - d1 * near, STEP * a2, -STEP * b,
        )
        for i, value in enumerate(values):
            full[i, here, :] = value
            half[i, here, :] = 0.5 * value
        noise[0, here, :] = STEP * (2.0 * a + 2.0 * ab)
        noise[1, here, :] = STEP * (2.0 * ab)
        noise[2, here, :] = STEP * (-2.0 * ab)

    first = cols_at * (panels // 2)
    lane = iota((panels // 2, LANES), 1)
    for t in range(2):
        pick = lane // 2 + (LANES // 2) * t
        for source, target in ((feed_of, ext_a), (conv_of, ext_b)):
            value = source[pl.ds(pl.multiple_of(first, panels // 2), panels // 2), :]
            target[pl.ds(8 + t, panels // 2, stride=2), :] = jnp.take_along_axis(value, pick, axis=1)
    before, after = jnp.maximum(first - 1, 0), jnp.minimum(first + panels // 2, class_rows - 1)
    for source, target in ((feed_of, ext_a), (conv_of, ext_b)):
        value = jnp.broadcast_to(source[pl.ds(before, 1), :], (8, LANES))
        target[0:8, :] = jnp.take_along_axis(value, lane8 // 2 + LANES // 2, axis=1)
        value = jnp.broadcast_to(source[pl.ds(after, 1), :], (8, LANES))
        target[8 + panels : 16 + panels, :] = jnp.take_along_axis(value, lane8 // 2, axis=1)
    shape = ext_a.shape
    lane_e = iota(shape, 1)
    even_e = lane_e % 2 == 0
    a, b = ext_a[...], ext_b[...]
    voxel = cols_at * (panels * LANES // 2) + (iota(shape, 0) - 8) * (LANES // 2) + lane_e // 2
    near = 2.0 - (voxel == 0).astype(F32) - (voxel == voxels - 1).astype(F32)
    d_e = jnp.where(even_e, d0, d1)
    ext_s[...] = STEP * jnp.where(even_e, b - 1.0, -a * a) - d_e * near
    ext_x[...] = STEP * jnp.where(even_e, a * a, -b)

    mid = slice(8, 8 + panels)
    lane = iota((panels, LANES), 1)
    even = lane % 2 == 0
    near, a, b = near[mid], a[mid], b[mid]
    d = jnp.where(even, d0, d1)
    other_d = jnp.where(even, d1, d0)

    def shifted(ref):
        here = ref[mid, :]
        left = pltpu.roll(jnp.where(lane >= LANES - 2, ref[7 : 7 + panels, :], here), 2, 1)
        right = pltpu.roll(jnp.where(lane < 2, ref[9 : 9 + panels, :], here), LANES - 2, 1)
        mate = jnp.where(even, pltpu.roll(here, LANES - 1, 1), pltpu.roll(here, 1, 1))
        return here, mate, jnp.where(even, right, left), jnp.where(even, left, right)

    s, s_mate, s_fore, s_back = shifted(ext_s)
    x, x_mate, x_fore, x_back = shifted(ext_x)
    col[0] = s
    col[1] = x
    col[2] = d
    col[3] = 1.0 + s + 0.5 * (s * s + x * x_mate + d * d * near)
    col[4] = x + 0.5 * x * (s + s_mate)
    col[5] = d + 0.5 * d * (s + s_fore)
    col[6] = d + 0.5 * d * (s + s_back)
    col[7] = 0.5 * d * d
    col[8] = 0.5 * (x * other_d + d * x_fore)
    col[9] = 0.5 * (x * other_d + d * x_back)
    ab = a * b
    same, cross = STEP * (jnp.where(even, 2.0 * a, 0.0) + 2.0 * ab), STEP * (-2.0 * ab)
    col[10] = jnp.where(even, same, cross)
    col[11] = jnp.where(even, cross, same)

    load(0).wait()
    load(panels - 1).wait()
    lane8 = iota((8, LANES), 1)
    sub8 = iota((8, LANES), 0)
    lane16 = iota((16, LANES), 1)
    for side, panel, start in ((0, 1, 0), (1, panels, LANES - 4)):
        packed = jnp.zeros((16, LANES), F32)
        for g in range(groups):
            piece = vx[panel, PAD + 16 * g : PAD + 16 * g + 16, :]
            turn = (4 * g - start) % LANES
            piece = pltpu.roll(piece, turn, 1) if turn else piece
            packed = jnp.where((lane16 >= 4 * g) & (lane16 < 4 * g + 4), piece, packed)
        send_col[side] = packed

    small[4].wait()
    small[5].wait()
    for k in range(panels // 2):
        one, two = (slice(LANES * (2 * k + t), LANES * (2 * k + t + 1)) for t in (0, 1))
        send_row[0, 8 * k : 8 * k + 8, :] = jnp.where(sub8 < 4, edge[0, :, one], pltpu.roll(edge[0, :, two], 4, 0))
        send_row[1, 8 * k : 8 * k + 8, :] = jnp.where(sub8 < 4, pltpu.roll(edge[1, :, one], 4, 0), edge[1, :, two])

    pl.semaphore_wait(barrier, count)
    tile_rows = 4 * panels

    def remote(i):
        dr, dc = SIDES[i]
        if dc == 0:
            side = 0 if dr < 0 else 1
            source, target = send_row.at[side], got_row.at[1 - side, pl.ds(8, tile_rows), :]
        elif dr == 0:
            side = 0 if dc < 0 else 1
            source, target = send_col.at[side], got_col.at[1 - side]
        else:
            lanes = pl.ds(0 if dc < 0 else (panels - 1) * LANES, LANES)
            corner = (2 if dr < 0 else 0) + (1 if dc < 0 else 0)
            source, target = edge.at[0 if dr < 0 else 1, :, lanes], got_corner.at[corner]
        return pltpu.make_async_remote_copy(
            src_ref=source, dst_ref=target, send_sem=send_sem.at[i], recv_sem=recv_sem.at[i],
            device_id=(row + dr, cols_at + dc), device_id_type=MESH,
        )

    for i, (dr, dc) in enumerate(SIDES):
        @pl.when(there(dr, dc))
        def _(i=i):
            remote(i).start()

    at16 = iota((16, LANES), 1)
    in16 = iota((16, LANES), 0)
    owner = (at16 + 4) // 32, (at16 + 20) // 32
    codes = [
        (16 * tile + in16 - at16) * (1 - 2 * (at16 % 2)) for tile in (2 * owner[0], 2 * owner[1] - 1)
    ]
    wide_at = iota((16, 2 * LANES), 1) % LANES
    wide_owner = (wide_at + 4) // 32, (wide_at + 20) // 32
    blank = jnp.zeros((16, 2 * LANES), BF16)

    def weights(p, _):
        c = [jnp.broadcast_to(col[i, pl.ds(p, 1), :], (16, LANES)) for i in range(10)]
        none = jnp.zeros((16, LANES), F32)
        pairs = []
        for k in codes:
            z = k == 0, k == 1, k == 2, k == -2
            u = jnp.where(jnp.abs(k) == 4, c[7], none)
            u = jnp.where(k == 3, c[8], u)
            u = jnp.where(k == -1, c[9], u)
            u = jnp.where(z[0], c[3], jnp.where(z[1], c[4], jnp.where(z[2], c[5], jnp.where(z[3], c[6], u))))
            w = jnp.where(z[0], c[0], jnp.where(z[1], c[1], jnp.where(z[2] | z[3], c[2], none)))
            pairs.append(split(jnp.concatenate([u, w], axis=1)))

        def tile(i, part):
            odd = i % 2
            return jnp.where(wide_owner[odd] == (i + odd) // 2, pairs[odd][part], blank)

        for i in range(8):
            whi[p, 16 * i : 16 * i + 16, :] = tile(i, 0)
            wlo[p, 16 * i : 16 * i + 16, :] = tile(i, 1)
        before, after = [tile(-1, part) for part in (0, 1)], [tile(8, part) for part in (0, 1)]
        for i, value in enumerate((after[0], before[0], after[0], before[1], after[1], blank, blank, before[0])):
            wlo[p, LANES + 16 * i : LANES + 16 * i + 16, :] = value
        return 0

    lax.fori_loop(0, panels, weights, 0)

    def split_panel(p):
        for g in range(groups):
            e = vx[p, pl.ds(PAD + 16 * g, 8, stride=2), :]
            o = vx[p, pl.ds(PAD + 16 * g + 1, 8, stride=2), :]
            hi, lo = split(jnp.concatenate([e, o], axis=0))
            high[p, 16 * g : 16 * g + 16, :] = hi
            low[p, 16 * g : 16 * g + 16, :] = lo

    split_panel(1)
    split_panel(panels)

    def next_panel(p, _):
        load(p - 1).wait()
        split_panel(p)
        return 0

    lax.fori_loop(2, panels, next_panel, 0)

    at_rows = iota((rows, LANES), 1)
    next_lanes = at_rows < LANES // 2
    low_lanes = (at_rows >= 16) & (at_rows < 48)
    again_lanes = (at_rows >= 48) & (at_rows < 80)

    def columns(p, w_ref):
        hi, lo = high[p], low[p]
        edge_hi = jnp.where(next_lanes, high[p + 1], high[p - 1])
        edge_lo = jnp.where(next_lanes, low[p + 1], low[p - 1])
        edges = jnp.where(
            low_lanes, pltpu.roll(edge_lo, 32, 1), jnp.where(again_lanes, pltpu.roll(edge_hi, 64, 1), edge_hi)
        )
        lhs = jnp.concatenate([hi, lo, hi, edges], axis=1)
        rhs = jnp.concatenate([whi[p - 1], whi[p - 1], wlo[p - 1]], axis=0)
        both = jnp.dot(lhs, rhs, preferred_element_type=F32)
        u_ref[p - 1] = both[:, :LANES]
        w_ref[...] = both[:, LANES:]

    def own_rows(p, w_ref):
        for g in range(groups):
            at = PAD + 16 * g
            e, o = vx[p, pl.ds(at, 8, stride=2), :], vx[p, pl.ds(at + 1, 8, stride=2), :]
            e_sum = vx[p, pl.ds(at - 2, 8, stride=2), :] + vx[p, pl.ds(at + 2, 8, stride=2), :]
            o_sum = vx[p, pl.ds(at - 1, 8, stride=2), :] + vx[p, pl.ds(at + 3, 8, stride=2), :]
            c = [half[n, 8 * g : 8 * g + 8, :] for n in range(4)]
            ge[p - 1, PAD + 8 * g : PAD + 8 * g + 8, :] = (
                e + w_ref[16 * g : 16 * g + 8, :] + ((c[0] * e + c[2] * o) + (0.5 * d0) * e_sum)
            )
            go[p - 1, PAD + 8 * g : PAD + 8 * g + 8, :] = (
                o + w_ref[16 * g + 8 : 16 * g + 16, :] + ((c[1] * o + c[3] * e) + (0.5 * d1) * o_sum)
            )

    columns(2, w_one)

    def middle(i, _):
        p = 3 + 2 * i
        own_rows(p - 1, w_one)
        columns(p, w_two)
        own_rows(p, w_two)
        columns(p + 1, w_one)
        return 0

    lax.fori_loop(0, (panels - 4) // 2, middle, 0)
    own_rows(panels - 2, w_one)
    columns(panels - 1, w_two)

    def wait_recv(dr, dc):
        @pl.when(there(-dr, -dc))
        def _():
            remote(SIDES.index((dr, dc))).wait_recv()

    wait_recv(0, 1)
    wait_recv(0, -1)
    for side, panel, start in ((0, 0, LANES - 4), (1, panels + 1, 0)):
        packed = got_col[side]
        for g in range(groups):
            turn = (start - 4 * g) % LANES
            vx[panel, PAD + 16 * g : PAD + 16 * g + 16, :] = pltpu.roll(packed, turn, 1) if turn else packed
        split_panel(panel)

    own_rows(panels - 1, w_two)
    columns(1, w_one)
    own_rows(1, w_one)
    columns(panels, w_two)
    own_rows(panels, w_two)

    for dr, dc in SIDES:
        if dr:
            wait_recv(dr, dc)
    for side in (0, 1):
        left, right = got_corner[2 * side], got_corner[2 * side + 1]
        if side == 0:
            tile_g[0:8, :] = right
            got_row[side, 0:8, :] = left
            got_row[side, 8 + tile_rows : 16 + tile_rows, :] = tile_g[4:12, :]
        else:
            tile_g[8:16, :] = left
            got_row[side, 0:8, :] = tile_g[4:12, :]
            got_row[side, 8 + tile_rows : 16 + tile_rows, :] = right
    even8 = lane8 % 2 == 0
    upper = sub8 < 4
    species = sub8 % 2 == 0
    for side in (0, 1):
        ok = there(-1, 0) if side == 0 else there(1, 0)
        voxel = jnp.clip(row * half_rows + (-1 if side == 0 else half_rows), 0, voxels - 1)
        pick = lane8 * 0 + voxel % LANES
        a = jnp.broadcast_to(feed_of[pl.ds(voxel // LANES, 1), :], (8, LANES))
        b = jnp.broadcast_to(conv_of[pl.ds(voxel // LANES, 1), :], (8, LANES))
        a = jnp.sum(jnp.where(lane8 == pick, a, 0.0), axis=1, keepdims=True)
        b = jnp.sum(jnp.where(lane8 == pick, b, 0.0), axis=1, keepdims=True)
        end = (voxel == 0) | (voxel == voxels - 1)
        near = jnp.where(end, 1.0, 2.0)
        d_r = jnp.where(species, d0, d1)
        s_r = STEP * jnp.where(species, b - 1.0, -a * a) - d_r * near
        x_r = STEP * jnp.where(species, a * a, -b)
        for k in range(panels // 2):
            at = 8 + 8 * k
            one, two = 2 * k + 1, 2 * k + 2
            tile, left, right = (got_row[side, at + t : at + t + 8, :] for t in (0, -4, 4))
            c_s, c_x, c_d = (
                jnp.where(upper, col[i, 2 * k : 2 * k + 1, :], col[i, 2 * k + 1 : 2 * k + 2, :]) for i in range(3)
            )
            mate = jnp.where(even8, pltpu.roll(tile, LANES - 1, 1), pltpu.roll(tile, 1, 1))
            far = pltpu.roll(jnp.where(lane8 >= LANES - 2, left, tile), 2, 1) + pltpu.roll(
                jnp.where(lane8 < 2, right, tile), LANES - 2, 1
            )
            w = c_s * tile + c_x * mate + c_d * far
            row_mate = jnp.where(species, got_row[side, at + 1 : at + 9, :], got_row[side, at - 1 : at + 7, :])
            if side == 0:
                out = got_row[side, at - 2 : at + 6, :]
                inn = jnp.where(upper, vx[one, PAD - 2 : PAD + 6, :], vx[two, PAD - 6 : PAD + 2, :])
            else:
                out = got_row[side, at + 2 : at + 10, :]
                e = PAD + rows
                inn = jnp.where(upper, vx[one, e - 2 : e + 6, :], vx[two, e - 6 : e + 2, :])
            g = tile + w + 0.5 * (s_r * tile + x_r * row_mate + d_r * (out + inn))
            tile_g[8 + 8 * k : 16 + 8 * k, :] = jnp.where(ok, g, 0.0)
        for k in range(panels // 2):
            for t in (0, 1):
                p, at = 2 * k + t, 8 + 8 * k + 4 * t
                for ref, o, dd in ((ge, 0, d0), (go, 1, d1)):
                    if side == 0:
                        ref[p, 0:8, :] = tile_g[at + 2 + o - 7 : at + 2 + o + 1, :]
                        here, sub, from_ = slice(PAD, PAD + 8), 0, at + 2 + o
                    else:
                        end = PAD + half_rows
                        ref[p, end : end + 8, :] = tile_g[at + o : at + o + 8, :]
                        here, sub, from_ = slice(end - 8, end), 7, at + o - 7
                    ref[p, here, :] += jnp.where(sub8 == sub, (0.5 * dd) * got_row[side, from_ : from_ + 8, :], 0.0)

    per_panel = LANES // 16

    def add_noise(g, t, move):
        c = [col[i, pl.ds(t, 1), :] for i in (0, 1, 2, 10, 11)]
        here = slice(8 * g, 8 * g + 8)
        f = [full[i, here, :] for i in range(4)]
        n_e, n_o, n_x = (noise[i, here, :] for i in range(3))
        gap = (move * (LANES // 2) + lane8 // 2) - (8 * (g % per_panel) + sub8)
        on, beside = gap == 0, jnp.abs(gap) == 1
        for start, s_r, x_r, d_r, one, two, mine, mate in (
            (16 * g, f[0], f[2], d0, c[3], c[4], jnp.where(even8, n_e, n_x), jnp.where(even8, n_x, n_e)),
            (16 * g + 8, f[1], f[3], d1, c[4], c[3], jnp.where(even8, n_x, n_o), jnp.where(even8, n_o, n_x)),
        ):
            centre = mine + 0.5 * ((s_r * one + x_r * two) + (c[0] * mine + c[1] * mate))
            side = 0.5 * (d_r * one + c[2] * mine)
            u_ref[t, start : start + 8, :] += jnp.where(on, centre, jnp.where(beside, side, 0.0))

    ratio = panels * LANES // rows
    first_panel = (row - cols_at * ratio) * (rows // LANES)

    @pl.when((first_panel >= 0) & (first_panel < panels))
    def _():
        for g in range(groups):
            t = first_panel + g // per_panel
            add_noise(g, t, 0)
            if g % per_panel == 0 and g:
                add_noise(g, t - 1, -1)
            if g % per_panel == per_panel - 1 and g < groups - 1:
                add_noise(g, t + 1, 1)

    @pl.when((first_panel >= 1) & (first_panel <= panels))
    def _():
        add_noise(0, first_panel - 1, -1)

    @pl.when((first_panel + rows // LANES >= 0) & (first_panel + rows // LANES < panels))
    def _():
        add_noise(groups - 1, first_panel + rows // LANES, 1)

    for i, (dr, dc) in enumerate(SIDES):
        @pl.when(there(dr, dc))
        def _(i=i):
            remote(i).wait_send()


def finish_kernel(rows, panels, u_ref, ge, go, full, spread, out, stage, sem):
    d0, d1 = spread[0], spread[1]
    groups = rows // 16
    wide = 4

    def store(p):
        return pltpu.make_async_copy(
            stage.at[p], out.at[:, pl.ds(pl.multiple_of(p * LANES, LANES), LANES)], sem.at[p]
        )

    def step(n, _):
        for g in range(groups):
            c = [full[i, 8 * g : 8 * g + 8, :] for i in range(4)]
            for t in range(wide):
                p = n * wide + t
                at = PAD + 8 * g
                e, o = ge[p, at : at + 8, :], go[p, at : at + 8, :]
                e_sum = ge[p, at - 1 : at + 7, :] + ge[p, at + 1 : at + 9, :]
                o_sum = go[p, at - 1 : at + 7, :] + go[p, at + 1 : at + 9, :]
                u_e, u_o = u_ref[p, 16 * g : 16 * g + 8, :], u_ref[p, 16 * g + 8 : 16 * g + 16, :]
                stage[p, pl.ds(16 * g, 8, stride=2), :] = u_e + ((c[0] * e + c[2] * o) + d0 * e_sum)
                stage[p, pl.ds(16 * g + 1, 8, stride=2), :] = u_o + ((c[1] * o + c[3] * e) + d1 * o_sum)
        for t in range(wide):
            store(n * wide + t).start()
        return 0

    lax.fori_loop(0, panels // wide, step, 0)

    def drain(p, _):
        store(p).wait()
        return 0

    lax.fori_loop(0, panels, drain, 0)


def body(covariance, classes, feed_rate, conversion_rate, diffusion):
    rows, cols = covariance.shape
    panels = cols // LANES
    voxels = classes.shape[0]
    half_rows = rows // 2
    vmem = pl.BlockSpec(memory_space=pltpu.VMEM)
    hbm = pl.BlockSpec(memory_space=pl.ANY)
    sizes = (lax.axis_size("row"), lax.axis_size("col"))
    inputs = (covariance, classes.reshape(voxels // LANES, LANES), feed_rate, conversion_rate, diffusion)
    results = pl.pallas_call(
        functools.partial(advance_kernel, rows, panels, voxels, *sizes),
        out_shape=[
            pltpu.VMEM((panels, rows, LANES), F32),
            pltpu.VMEM((panels, half_rows + 2 * PAD, LANES), F32),
            pltpu.VMEM((panels, half_rows + 2 * PAD, LANES), F32),
            pltpu.VMEM((4, half_rows, LANES), F32),
            pltpu.VMEM((2, 8, LANES), F32),
        ],
        in_specs=[hbm] * 5,
        out_specs=[vmem] * 5,
        scratch_shapes=[
            pltpu.VMEM((panels + 2, rows + 2 * PAD, LANES), F32),
            pltpu.VMEM((panels + 2, rows, LANES), BF16),
            pltpu.VMEM((panels + 2, rows, LANES), BF16),
            pltpu.VMEM((panels, LANES, 2 * LANES), BF16),
            pltpu.VMEM((panels, 2 * LANES, 2 * LANES), BF16),
            pltpu.VMEM((rows, LANES), F32),
            pltpu.VMEM((rows, LANES), F32),
            pltpu.VMEM((4, half_rows, LANES), F32),
            pltpu.VMEM((3, half_rows, LANES), F32),
            pltpu.VMEM((voxels // LANES, LANES), F32),
            pltpu.VMEM((voxels // LANES, LANES), F32),
            pltpu.VMEM((panels + 16, LANES), F32),
            pltpu.VMEM((panels + 16, LANES), F32),
            pltpu.VMEM((panels + 16, LANES), F32),
            pltpu.VMEM((panels + 16, LANES), F32),
            pltpu.VMEM((12, panels, LANES), F32),
            pltpu.VMEM((voxels // LANES, LANES), jnp.int32),
            pltpu.SMEM(feed_rate.shape, F32),
            pltpu.SMEM(conversion_rate.shape, F32),
            pltpu.SMEM(diffusion.shape, F32),
            pltpu.VMEM((2, 8, cols), F32),
            pltpu.VMEM((2, 4 * panels, LANES), F32),
            pltpu.VMEM((2, 16, LANES), F32),
            pltpu.VMEM((2, 4 * panels + 16, LANES), F32),
            pltpu.VMEM((2, 16, LANES), F32),
            pltpu.VMEM((4, 8, LANES), F32),
            pltpu.VMEM((4 * panels + 16, LANES), F32),
            pltpu.SemaphoreType.DMA((panels,)),
            pltpu.SemaphoreType.DMA((6,)),
            pltpu.SemaphoreType.DMA((8,)),
            pltpu.SemaphoreType.DMA((8,)),
        ],
        compiler_params=pltpu.CompilerParams(
            collective_id=0, has_side_effects=True, vmem_limit_bytes=32 << 20
        ),
        name="halo_and_columns",
    )(*(pltpu.with_memory_space_constraint(x, pltpu.HBM) for x in inputs))
    return pl.pallas_call(
        functools.partial(finish_kernel, rows, panels),
        out_shape=jax.ShapeDtypeStruct((rows, cols), F32),
        in_specs=[vmem] * 5,
        out_specs=hbm,
        scratch_shapes=[
            pltpu.VMEM((panels, rows, LANES), F32),
            pltpu.SemaphoreType.DMA((panels,)),
        ],
        compiler_params=pltpu.CompilerParams(vmem_limit_bytes=24 << 20),
        name="rows",
    )(*results)


def solution(mesh):
    in_specs = (P("row", "col"), P(), P(), P(), P())
    return jax.shard_map(body, mesh=mesh, in_specs=in_specs, out_specs=P("row", "col"), check_vma=False)
```

```python
import functools

import jax
import jax.numpy as jnp
from jax import lax
from jax.experimental import pallas as pl
from jax.experimental.pallas import tpu as pltpu
from jax.sharding import PartitionSpec as P

STEP = 0.04
LANES = 128
PAD = 8
F32, BF16 = jnp.float32, jnp.bfloat16
MESH = pl.DeviceIdType.MESH
SIDES = [(dr, dc) for dr in (-1, 0, 1) for dc in (-1, 0, 1) if (dr, dc) != (0, 0)]


def split(value):
    high = value.astype(BF16)
    return high, (value - high.astype(F32)).astype(BF16)


def iota(shape, dim):
    return lax.broadcasted_iota(jnp.int32, shape, dim)


def advance_kernel(
    rows, panels, voxels, grid_rows, grid_cols,
    cov, classes_in, feed_in, conv_in, diff_in,
    stage, u_edge, ge, go, full, spread, halo, inner, halo_col, halo_row,
    vx, high, low, whi, wlo, w_one, w_two, half, noise, feed_of, conv_of, ext_s, ext_x, ext_a, ext_b, col,
    classes, feed, conv, diff, edge, send_row, send_col, got_row, got_col, got_corner,
    load_sem, small_sem, send_sem, recv_sem,
):
    row, cols_at = lax.axis_index("row"), lax.axis_index("col")
    groups = rows // 16
    half_rows = rows // 2
    def there(dr, dc):
        ok = None
        for at, step, size in ((row, dr, grid_rows), (cols_at, dc, grid_cols)):
            if step:
                one = (at + step >= 0) & (at + step < size)
                ok = one if ok is None else ok & one
        return ok

    barrier = pltpu.get_barrier_semaphore()
    count = jnp.int32(0)
    for dr, dc in SIDES:
        ok = there(dr, dc)
        count += ok.astype(jnp.int32)

        @pl.when(ok)
        def _(dr=dr, dc=dc):
            pl.semaphore_signal(barrier, inc=1, device_id=(row + dr, cols_at + dc), device_id_type=MESH)

    distant = (row == grid_rows // 2 - 1) | (row == grid_rows // 2)

    small = [
        pltpu.make_async_copy(a, b, small_sem.at[n])
        for n, (a, b) in enumerate((
            (classes_in, classes), (feed_in, feed), (conv_in, conv), (diff_in, diff),
            (cov.at[pl.ds(0, 8), :], edge.at[0]), (cov.at[pl.ds(rows - 8, 8), :], edge.at[1]),
        ))
    ]
    for copy in small:
        copy.start()
    def load(p):
        return pltpu.make_async_copy(
            cov.at[:, pl.ds(pl.multiple_of(p * LANES, LANES), LANES)],
            vx.at[p + 1, pl.ds(PAD, rows), :],
            load_sem.at[p],
        )

    load(0).start()
    load(panels - 1).start()

    def start_load(p, _):
        load(p).start()
        return 0

    lax.fori_loop(1, panels - 1, start_load, 0)

    zero = jnp.zeros((8, LANES), F32)
    for p in range(panels):
        vx[p + 1, 0:PAD, :] = zero
        vx[p + 1, PAD + rows : 2 * PAD + rows, :] = zero
    for i, at in enumerate((0, grid_cols - 1)):
        @pl.when(cols_at == at)
        def _(i=i):
            got_col[i] = jnp.zeros(got_col.shape[1:], F32)
            got_corner[i] = zero
            got_corner[2 + i] = zero

    for copy in small[:4]:
        copy.wait()
    d0, d1 = diff[0] * STEP, diff[1] * STEP
    spread[0] = jnp.full((8, LANES), d0, F32)
    spread[1] = jnp.full((8, LANES), d1, F32)
    ids = classes[...]
    a_all, b_all = jnp.zeros(ids.shape, F32), jnp.zeros(ids.shape, F32)
    for k in range(feed.shape[0]):
        a_all = jnp.where(ids == k, feed[k], a_all)
        b_all = jnp.where(ids == k, conv[k], b_all)
    feed_of[...] = a_all
    conv_of[...] = b_all
    class_rows = voxels // LANES

    lane8 = iota((8, LANES), 1)
    row_at = row * (half_rows // LANES)
    for t in range(half_rows // LANES):
        a = jnp.broadcast_to(feed_of[pl.ds(row_at + t, 1), :], (LANES, LANES)).T
        b = jnp.broadcast_to(conv_of[pl.ds(row_at + t, 1), :], (LANES, LANES)).T
        voxel = row * half_rows + t * LANES + iota((LANES, LANES), 0)
        near = 2.0 - (voxel == 0).astype(F32) - (voxel == voxels - 1).astype(F32)
        here = pl.ds(t * LANES, LANES)
        a2, ab = a * a, a * b
        values = (
            STEP * (b - 1.0) - d0 * near, -STEP * a2 - d1 * near, STEP * a2, -STEP * b,
        )
        for i, value in enumerate(values):
            full[i, here, :] = value
            half[i, here, :] = 0.5 * value
        noise[0, here, :] = STEP * (2.0 * a + 2.0 * ab)
        noise[1, here, :] = STEP * (2.0 * ab)
        noise[2, here, :] = STEP * (-2.0 * ab)

    first = cols_at * (panels // 2)
    lane = iota((panels // 2, LANES), 1)
    for t in range(2):
        pick = lane // 2 + (LANES // 2) * t
        for source, target in ((feed_of, ext_a), (conv_of, ext_b)):
            value = source[pl.ds(pl.multiple_of(first, panels // 2), panels // 2), :]
            target[pl.ds(8 + t, panels // 2, stride=2), :] = jnp.take_along_axis(value, pick, axis=1)
    before, after = jnp.maximum(first - 1, 0), jnp.minimum(first + panels // 2, class_rows - 1)
    for source, target in ((feed_of, ext_a), (conv_of, ext_b)):
        value = jnp.broadcast_to(source[pl.ds(before, 1), :], (8, LANES))
        target[0:8, :] = jnp.take_along_axis(value, lane8 // 2 + LANES // 2, axis=1)
        value = jnp.broadcast_to(source[pl.ds(after, 1), :], (8, LANES))
        target[8 + panels : 16 + panels, :] = jnp.take_along_axis(value, lane8 // 2, axis=1)
    shape = ext_a.shape
    lane_e = iota(shape, 1)
    even_e = lane_e % 2 == 0
    a, b = ext_a[...], ext_b[...]
    voxel = cols_at * (panels * LANES // 2) + (iota(shape, 0) - 8) * (LANES // 2) + lane_e // 2
    near = 2.0 - (voxel == 0).astype(F32) - (voxel == voxels - 1).astype(F32)
    d_e = jnp.where(even_e, d0, d1)
    ext_s[...] = STEP * jnp.where(even_e, b - 1.0, -a * a) - d_e * near
    ext_x[...] = STEP * jnp.where(even_e, a * a, -b)

    mid = slice(8, 8 + panels)
    lane = iota((panels, LANES), 1)
    even = lane % 2 == 0
    near, a, b = near[mid], a[mid], b[mid]
    d = jnp.where(even, d0, d1)
    other_d = jnp.where(even, d1, d0)

    def shifted(ref):
        here = ref[mid, :]
        left = pltpu.roll(jnp.where(lane >= LANES - 2, ref[7 : 7 + panels, :], here), 2, 1)
        right = pltpu.roll(jnp.where(lane < 2, ref[9 : 9 + panels, :], here), LANES - 2, 1)
        mate = jnp.where(even, pltpu.roll(here, LANES - 1, 1), pltpu.roll(here, 1, 1))
        return here, mate, jnp.where(even, right, left), jnp.where(even, left, right)

    s, s_mate, s_fore, s_back = shifted(ext_s)
    x, x_mate, x_fore, x_back = shifted(ext_x)
    col[0] = s
    col[1] = x
    col[2] = d
    col[3] = 1.0 + s + 0.5 * (s * s + x * x_mate + d * d * near)
    col[4] = x + 0.5 * x * (s + s_mate)
    col[5] = d + 0.5 * d * (s + s_fore)
    col[6] = d + 0.5 * d * (s + s_back)
    col[7] = 0.5 * d * d
    col[8] = 0.5 * (x * other_d + d * x_fore)
    col[9] = 0.5 * (x * other_d + d * x_back)
    ab = a * b
    same, cross = STEP * (jnp.where(even, 2.0 * a, 0.0) + 2.0 * ab), STEP * (-2.0 * ab)
    col[10] = jnp.where(even, same, cross)
    col[11] = jnp.where(even, cross, same)

    load(0).wait()
    load(panels - 1).wait()
    lane8 = iota((8, LANES), 1)
    sub8 = iota((8, LANES), 0)
    lane16 = iota((16, LANES), 1)
    for side, panel, start in ((0, 1, 0), (1, panels, LANES - 4)):
        packed = jnp.zeros((16, LANES), F32)
        for g in range(groups):
            piece = vx[panel, PAD + 16 * g : PAD + 16 * g + 16, :]
            turn = (4 * g - start) % LANES
            piece = pltpu.roll(piece, turn, 1) if turn else piece
            packed = jnp.where((lane16 >= 4 * g) & (lane16 < 4 * g + 4), piece, packed)
        send_col[side] = packed

    small[4].wait()
    small[5].wait()
    for k in range(panels // 2):
        one, two = (slice(LANES * (2 * k + t), LANES * (2 * k + t + 1)) for t in (0, 1))
        send_row[0, 8 * k : 8 * k + 8, :] = jnp.where(sub8 < 4, edge[0, :, one], pltpu.roll(edge[0, :, two], 4, 0))
        send_row[1, 8 * k : 8 * k + 8, :] = jnp.where(sub8 < 4, pltpu.roll(edge[1, :, one], 4, 0), edge[1, :, two])

    tile_rows = 4 * panels

    def landing(i):
        dr, dc = SIDES[i]
        if dc == 0:
            return got_row.at[0 if dr > 0 else 1, pl.ds(8, tile_rows), :]
        if dr == 0:
            return got_col.at[0 if dc > 0 else 1]
        return got_corner.at[(2 if dr < 0 else 0) + (1 if dc < 0 else 0)]

    def remote(i):
        dr, dc = SIDES[i]
        if dc == 0:
            source = send_row.at[0 if dr < 0 else 1]
        elif dr == 0:
            source = send_col.at[0 if dc < 0 else 1]
        else:
            source = edge.at[0 if dr < 0 else 1, :, pl.ds(0 if dc < 0 else (panels - 1) * LANES, LANES)]
        return pltpu.make_async_remote_copy(
            src_ref=source, dst_ref=landing(i), send_sem=send_sem.at[i], recv_sem=recv_sem.at[i],
            device_id=(row + dr, cols_at + dc), device_id_type=MESH,
        )

    def send():
        pl.semaphore_wait(barrier, count)
        for i, (dr, dc) in enumerate(SIDES):
            @pl.when(there(dr, dc))
            def _(i=i):
                remote(i).start()

    at16 = iota((16, LANES), 1)
    in16 = iota((16, LANES), 0)
    owner = (at16 + 4) // 32, (at16 + 20) // 32
    codes = [
        (16 * tile + in16 - at16) * (1 - 2 * (at16 % 2)) for tile in (2 * owner[0], 2 * owner[1] - 1)
    ]
    wide_at = iota((16, 2 * LANES), 1) % LANES
    wide_owner = (wide_at + 4) // 32, (wide_at + 20) // 32
    blank = jnp.zeros((16, 2 * LANES), BF16)

    def weights(p, _):
        c = [jnp.broadcast_to(col[i, pl.ds(p, 1), :], (16, LANES)) for i in range(10)]
        none = jnp.zeros((16, LANES), F32)
        pairs = []
        for k in codes:
            z = k == 0, k == 1, k == 2, k == -2
            u = jnp.where(jnp.abs(k) == 4, c[7], none)
            u = jnp.where(k == 3, c[8], u)
            u = jnp.where(k == -1, c[9], u)
            u = jnp.where(z[0], c[3], jnp.where(z[1], c[4], jnp.where(z[2], c[5], jnp.where(z[3], c[6], u))))
            w = jnp.where(z[0], c[0], jnp.where(z[1], c[1], jnp.where(z[2] | z[3], c[2], none)))
            pairs.append(split(jnp.concatenate([u, w], axis=1)))

        def tile(i, part):
            odd = i % 2
            return jnp.where(wide_owner[odd] == (i + odd) // 2, pairs[odd][part], blank)

        for i in range(8):
            whi[p, 16 * i : 16 * i + 16, :] = tile(i, 0)
            wlo[p, 16 * i : 16 * i + 16, :] = tile(i, 1)
        before, after = [tile(-1, part) for part in (0, 1)], [tile(8, part) for part in (0, 1)]
        for i, value in enumerate((after[0], before[0], after[0], before[1], after[1], blank, blank, before[0])):
            wlo[p, LANES + 16 * i : LANES + 16 * i + 16, :] = value
        return 0

    lax.fori_loop(0, panels, weights, 0)

    def split_panel(p):
        for g in range(groups):
            e = vx[p, pl.ds(PAD + 16 * g, 8, stride=2), :]
            o = vx[p, pl.ds(PAD + 16 * g + 1, 8, stride=2), :]
            hi, lo = split(jnp.concatenate([e, o], axis=0))
            high[p, 16 * g : 16 * g + 16, :] = hi
            low[p, 16 * g : 16 * g + 16, :] = lo

    split_panel(1)
    split_panel(panels)

    def next_panel(p, _):
        load(p - 1).wait()
        split_panel(p)
        return 0

    lax.fori_loop(2, panels, next_panel, 0)
    pl.when(jnp.logical_not(distant))(send)

    at_rows = iota((rows, LANES), 1)
    next_lanes = at_rows < LANES // 2
    low_lanes = (at_rows >= 16) & (at_rows < 48)
    again_lanes = (at_rows >= 48) & (at_rows < 80)

    def columns(p, w_ref):
        hi, lo = high[p], low[p]
        edge_hi = jnp.where(next_lanes, high[p + 1], high[p - 1])
        edge_lo = jnp.where(next_lanes, low[p + 1], low[p - 1])
        edges = jnp.where(
            low_lanes, pltpu.roll(edge_lo, 32, 1), jnp.where(again_lanes, pltpu.roll(edge_hi, 64, 1), edge_hi)
        )
        lhs = jnp.concatenate([hi, lo, hi, edges], axis=1)
        rhs = jnp.concatenate([whi[p - 1], whi[p - 1], wlo[p - 1]], axis=0)
        both = jnp.dot(lhs, rhs, preferred_element_type=F32)
        w_ref[...] = both
        u_edge[p - 1, 0:16, :] = both[0:16, :LANES]
        u_edge[p - 1, 16:32, :] = both[rows - 16 :, :LANES]

    def own_rows(p, w_ref):
        for g in range(groups):
            at = PAD + 16 * g
            e, o = vx[p, pl.ds(at, 8, stride=2), :], vx[p, pl.ds(at + 1, 8, stride=2), :]
            e_sum = vx[p, pl.ds(at - 2, 8, stride=2), :] + vx[p, pl.ds(at + 2, 8, stride=2), :]
            o_sum = vx[p, pl.ds(at - 1, 8, stride=2), :] + vx[p, pl.ds(at + 3, 8, stride=2), :]
            c = [half[n, 8 * g : 8 * g + 8, :] for n in range(4)]
            ge[p - 1, PAD + 8 * g : PAD + 8 * g + 8, :] = (
                e + w_ref[16 * g : 16 * g + 8, LANES:] + ((c[0] * e + c[2] * o) + (0.5 * d0) * e_sum)
            )
            go[p - 1, PAD + 8 * g : PAD + 8 * g + 8, :] = (
                o + w_ref[16 * g + 8 : 16 * g + 16, LANES:] + ((c[1] * o + c[3] * e) + (0.5 * d1) * o_sum)
            )
        for g in range(1, groups - 1):
            at = PAD + 8 * g
            e, o = ge[p - 1, at : at + 8, :], go[p - 1, at : at + 8, :]
            e_sum = ge[p - 1, at - 1 : at + 7, :] + ge[p - 1, at + 1 : at + 9, :]
            o_sum = go[p - 1, at - 1 : at + 7, :] + go[p - 1, at + 1 : at + 9, :]
            c = [full[n, 8 * g : 8 * g + 8, :] for n in range(4)]
            stage[p - 1, pl.ds(16 * g, 8, stride=2), :] = (
                w_ref[16 * g : 16 * g + 8, :LANES] + ((c[0] * e + c[2] * o) + d0 * e_sum)
            )
            stage[p - 1, pl.ds(16 * g + 1, 8, stride=2), :] = (
                w_ref[16 * g + 8 : 16 * g + 16, :LANES] + ((c[1] * o + c[3] * e) + d1 * o_sum)
            )

    columns(2, w_one)

    steps = (panels - 4) // 2
    early = 1

    def middle(i, _):
        pl.when(distant & (i == early))(send)
        p = 3 + 2 * i
        own_rows(p - 1, w_one)
        columns(p, w_two)
        own_rows(p, w_two)
        columns(p + 1, w_one)
        return 0

    lax.fori_loop(0, steps, middle, 0)
    own_rows(panels - 2, w_one)
    columns(panels - 1, w_two)

    def wait_recv(dr, dc):
        @pl.when(there(-dr, -dc))
        def _():
            remote(SIDES.index((dr, dc))).wait_recv()

    wait_recv(0, 1)
    wait_recv(0, -1)
    for side, panel, start in ((0, 0, LANES - 4), (1, panels + 1, 0)):
        packed = got_col[side]
        for g in range(groups):
            turn = (start - 4 * g) % LANES
            vx[panel, PAD + 16 * g : PAD + 16 * g + 16, :] = pltpu.roll(packed, turn, 1) if turn else packed
        split_panel(panel)

    own_rows(panels - 1, w_two)
    columns(1, w_one)
    own_rows(1, w_one)
    columns(panels, w_two)
    own_rows(panels, w_two)

    per_panel = LANES // 16
    even_lane = lane8 % 2 == 0

    def add_noise(g, t, move):
        c = [col[i, pl.ds(t, 1), :] for i in (0, 1, 2, 10, 11)]
        here = slice(8 * g, 8 * g + 8)
        f = [full[i, here, :] for i in range(4)]
        n_e, n_o, n_x = (noise[i, here, :] for i in range(3))
        gap = (move * (LANES // 2) + lane8 // 2) - (8 * (g % per_panel) + sub8)
        on, beside = gap == 0, jnp.abs(gap) == 1
        for odd, s_r, x_r, d_r, one, two, mine, mate in (
            (0, f[0], f[2], d0, c[3], c[4], jnp.where(even_lane, n_e, n_x), jnp.where(even_lane, n_x, n_e)),
            (1, f[1], f[3], d1, c[4], c[3], jnp.where(even_lane, n_x, n_o), jnp.where(even_lane, n_o, n_x)),
        ):
            centre = mine + 0.5 * ((s_r * one + x_r * two) + (c[0] * mine + c[1] * mate))
            side = 0.5 * (d_r * one + c[2] * mine)
            value = jnp.where(on, centre, jnp.where(beside, side, 0.0))
            if g in (0, groups - 1):
                at = 8 * odd + (16 if g else 0)
                u_edge[t, at : at + 8, :] += value
            else:
                stage[t, pl.ds(16 * g + odd, 8, stride=2), :] += value

    ratio = panels * LANES // rows
    first_panel = (row - cols_at * ratio) * (rows // LANES)

    @pl.when((first_panel >= 0) & (first_panel < panels))
    def _():
        for g in range(groups):
            t = first_panel + g // per_panel
            add_noise(g, t, 0)
            if g % per_panel == 0 and g:
                add_noise(g, t - 1, -1)
            if g % per_panel == per_panel - 1 and g < groups - 1:
                add_noise(g, t + 1, 1)

    @pl.when((first_panel >= 1) & (first_panel <= panels))
    def _():
        add_noise(0, first_panel - 1, -1)

    @pl.when((first_panel + rows // LANES >= 0) & (first_panel + rows // LANES < panels))
    def _():
        add_noise(groups - 1, first_panel + rows // LANES, 1)

    upper = sub8 < 4
    species = sub8 % 2 == 0
    for k in range(panels // 2):
        here = slice(8 * k, 8 * k + 8)
        one, two = 2 * k + 1, 2 * k + 2
        e = PAD + rows
        inner[0, here, :] = jnp.where(upper, vx[one, PAD - 2 : PAD + 6, :], vx[two, PAD - 6 : PAD + 2, :])
        inner[1, here, :] = jnp.where(upper, vx[one, e - 2 : e + 6, :], vx[two, e - 6 : e + 2, :])
        for i in range(3):
            halo_col[i, here, :] = jnp.where(upper, col[i, 2 * k : 2 * k + 1, :], col[i, 2 * k + 1 : 2 * k + 2, :])
    for side in (0, 1):
        voxel = jnp.clip(row * half_rows + (-1 if side == 0 else half_rows), 0, voxels - 1)
        pick = lane8 * 0 + voxel % LANES
        a = jnp.broadcast_to(feed_of[pl.ds(voxel // LANES, 1), :], (8, LANES))
        b = jnp.broadcast_to(conv_of[pl.ds(voxel // LANES, 1), :], (8, LANES))
        a = jnp.sum(jnp.where(lane8 == pick, a, 0.0), axis=1, keepdims=True)
        b = jnp.sum(jnp.where(lane8 == pick, b, 0.0), axis=1, keepdims=True)
        end = (voxel == 0) | (voxel == voxels - 1)
        near = jnp.where(end, 1.0, 2.0)
        d_r = jnp.where(species, d0, d1)
        halo_row[side, 0] = jnp.broadcast_to(STEP * jnp.where(species, b - 1.0, -a * a) - d_r * near, (8, LANES))
        halo_row[side, 1] = jnp.broadcast_to(STEP * jnp.where(species, a * a, -b), (8, LANES))
        halo_row[side, 2] = jnp.broadcast_to(d_r, (8, LANES))
        ok = there(-1, 0) if side == 0 else there(1, 0)
        halo_row[side, 3] = jnp.full((8, LANES), ok.astype(F32))

    for dr, dc in SIDES:
        if dr:
            wait_recv(dr, dc)
    for side in (0, 1):
        halo[side, 8 : 8 + tile_rows, :] = got_row[side, 8 : 8 + tile_rows, :]
        halo[side, 0:8, :] = got_corner[2 * side] if side == 0 else pltpu.roll(got_corner[2 * side], 4, 0)
        right = got_corner[2 * side + 1]
        halo[side, 8 + tile_rows : 16 + tile_rows, :] = pltpu.roll(right, 4, 0) if side == 0 else right

    for i, (dr, dc) in enumerate(SIDES):
        @pl.when(there(dr, dc))
        def _(i=i):
            remote(i).wait_send()


def finish_kernel(
    rows, panels,
    stage, u_edge, ge, go, full, spread, halo, inner, halo_col, halo_row,
    out, tile_g, near_g, ends, wide, sem,
):
    d0, d1 = spread[0], spread[1]
    groups = rows // 16
    half_rows = rows // 2

    def store(p):
        return pltpu.make_async_copy(
            stage.at[p, pl.ds(16, rows - 32), :],
            out.at[pl.ds(16, rows - 32), pl.ds(p * LANES, LANES)],
            sem.at[p],
        )

    def store_end(side):
        return pltpu.make_async_copy(
            wide.at[side], out.at[pl.ds(side * (rows - 16), 16), :], sem.at[panels + side]
        )

    for p in range(panels):
        store(p).start()

    lane8 = iota((8, LANES), 1)
    sub8 = iota((8, LANES), 0)
    even8 = lane8 % 2 == 0
    species = sub8 % 2 == 0
    for side in (0, 1):
        s_r, x_r, d_r = halo_row[side, 0], halo_row[side, 1], halo_row[side, 2]
        ok = halo_row[side, 3] > 0.5
        for k in range(panels // 2):
            at = 8 + 8 * k
            here = slice(8 * k, 8 * k + 8)
            tile, left, right = (halo[side, at + t : at + t + 8, :] for t in (0, -4, 4))
            mate = jnp.where(even8, pltpu.roll(tile, LANES - 1, 1), pltpu.roll(tile, 1, 1))
            beside = pltpu.roll(jnp.where(lane8 >= LANES - 2, left, tile), 2, 1) + pltpu.roll(
                jnp.where(lane8 < 2, right, tile), LANES - 2, 1
            )
            w = halo_col[0, here, :] * tile + halo_col[1, here, :] * mate + halo_col[2, here, :] * beside
            row_mate = jnp.where(species, halo[side, at + 1 : at + 9, :], halo[side, at - 1 : at + 7, :])
            away = halo[side, at - 2 : at + 6, :] if side == 0 else halo[side, at + 2 : at + 10, :]
            g = tile + w + 0.5 * (s_r * tile + x_r * row_mate + d_r * (away + inner[side, here, :]))
            tile_g[side, at : at + 8, :] = jnp.where(ok, g, 0.0)

        first = 0 if side == 0 else half_rows - 8
        c = [full[i, first : first + 8, :] for i in range(4)]
        for p in range(panels):
            at = 8 + 8 * (p // 2) + 4 * (p % 2)
            for o, ref, dd in ((0, ge, d0), (1, go, d1)):
                mine = ref[p, PAD + first : PAD + first + 8, :]
                if side == 0:
                    fix = halo[side, at + 2 + o : at + 10 + o, :]
                    near_g[o, 0:8, :] = tile_g[side, at + o - 5 : at + o + 3, :]
                    near_g[o, 16:24, :] = ref[p, PAD + 8 : PAD + 16, :]
                else:
                    fix = halo[side, at + o - 7 : at + o + 1, :]
                    near_g[o, 0:8, :] = ref[p, PAD + first - 8 : PAD + first, :]
                    near_g[o, 16:24, :] = tile_g[side, at + o : at + o + 8, :]
                fix = jnp.where(ok & (sub8 == (0 if side == 0 else 7)), (0.5 * dd) * fix, 0.0)
                near_g[o, 8:16, :] = mine + fix
            e, o = near_g[0, 8:16, :], near_g[1, 8:16, :]
            e_sum = near_g[0, 7:15, :] + near_g[0, 9:17, :]
            o_sum = near_g[1, 7:15, :] + near_g[1, 9:17, :]
            u = 16 * side
            ends[p, pl.ds(0, 8, stride=2), :] = u_edge[p, u : u + 8, :] + ((c[0] * e + c[2] * o) + d0 * e_sum)
            ends[p, pl.ds(1, 8, stride=2), :] = u_edge[p, u + 8 : u + 16, :] + ((c[1] * o + c[3] * e) + d1 * o_sum)
            wide[side, :, LANES * p : LANES * p + LANES] = ends[p]
        store_end(side).start()

    for p in range(panels):
        store(p).wait()
    for side in (0, 1):
        store_end(side).wait()


def body(covariance, classes, feed_rate, conversion_rate, diffusion):
    rows, cols = covariance.shape
    panels = cols // LANES
    voxels = classes.shape[0]
    half_rows = rows // 2
    vmem = pl.BlockSpec(memory_space=pltpu.VMEM)
    hbm = pl.BlockSpec(memory_space=pl.ANY)
    sizes = (lax.axis_size("row"), lax.axis_size("col"))
    inputs = (covariance, classes.reshape(voxels // LANES, LANES), feed_rate, conversion_rate, diffusion)
    results = pl.pallas_call(
        functools.partial(advance_kernel, rows, panels, voxels, *sizes),
        out_shape=[
            pltpu.VMEM((panels, rows, LANES), F32),
            pltpu.VMEM((panels, 32, LANES), F32),
            pltpu.VMEM((panels, half_rows + 2 * PAD, LANES), F32),
            pltpu.VMEM((panels, half_rows + 2 * PAD, LANES), F32),
            pltpu.VMEM((4, half_rows, LANES), F32),
            pltpu.VMEM((2, 8, LANES), F32),
            pltpu.VMEM((2, 4 * panels + 16, LANES), F32),
            pltpu.VMEM((2, 4 * panels, LANES), F32),
            pltpu.VMEM((3, 4 * panels, LANES), F32),
            pltpu.VMEM((2, 4, 8, LANES), F32),
        ],
        in_specs=[hbm] * 5,
        out_specs=[vmem] * 10,
        scratch_shapes=[
            pltpu.VMEM((panels + 2, rows + 2 * PAD, LANES), F32),
            pltpu.VMEM((panels + 2, rows, LANES), BF16),
            pltpu.VMEM((panels + 2, rows, LANES), BF16),
            pltpu.VMEM((panels, LANES, 2 * LANES), BF16),
            pltpu.VMEM((panels, 2 * LANES, 2 * LANES), BF16),
            pltpu.VMEM((rows, 2 * LANES), F32),
            pltpu.VMEM((rows, 2 * LANES), F32),
            pltpu.VMEM((4, half_rows, LANES), F32),
            pltpu.VMEM((3, half_rows, LANES), F32),
            pltpu.VMEM((voxels // LANES, LANES), F32),
            pltpu.VMEM((voxels // LANES, LANES), F32),
            pltpu.VMEM((panels + 16, LANES), F32),
            pltpu.VMEM((panels + 16, LANES), F32),
            pltpu.VMEM((panels + 16, LANES), F32),
            pltpu.VMEM((panels + 16, LANES), F32),
            pltpu.VMEM((12, panels, LANES), F32),
            pltpu.VMEM((voxels // LANES, LANES), jnp.int32),
            pltpu.SMEM(feed_rate.shape, F32),
            pltpu.SMEM(conversion_rate.shape, F32),
            pltpu.SMEM(diffusion.shape, F32),
            pltpu.VMEM((2, 8, cols), F32),
            pltpu.VMEM((2, 4 * panels, LANES), F32),
            pltpu.VMEM((2, 16, LANES), F32),
            pltpu.VMEM((2, 4 * panels + 16, LANES), F32),
            pltpu.VMEM((2, 16, LANES), F32),
            pltpu.VMEM((4, 8, LANES), F32),
            pltpu.SemaphoreType.DMA((panels,)),
            pltpu.SemaphoreType.DMA((6,)),
            pltpu.SemaphoreType.DMA((8,)),
            pltpu.SemaphoreType.DMA((8,)),
        ],
        compiler_params=pltpu.CompilerParams(
            collective_id=0, has_side_effects=True, vmem_limit_bytes=32 << 20
        ),
        name="halo_and_columns",
    )(*(pltpu.with_memory_space_constraint(x, pltpu.HBM) for x in inputs))
    return pl.pallas_call(
        functools.partial(finish_kernel, rows, panels),
        out_shape=jax.ShapeDtypeStruct((rows, cols), F32),
        in_specs=[vmem] * 10,
        out_specs=hbm,
        scratch_shapes=[
            pltpu.VMEM((2, 4 * panels + 16, LANES), F32),
            pltpu.VMEM((2, 24, LANES), F32),
            pltpu.VMEM((panels, 16, LANES), F32),
            pltpu.VMEM((2, 16, cols), F32),
            pltpu.SemaphoreType.DMA((panels + 2,)),
        ],
        compiler_params=pltpu.CompilerParams(vmem_limit_bytes=24 << 20),
        name="rows",
    )(*results)


def solution(mesh):
    in_specs = (P("row", "col"), P(), P(), P(), P())
    return jax.shard_map(body, mesh=mesh, in_specs=in_specs, out_specs=P("row", "col"), check_vma=False)
```

```python
import functools

import jax
import jax.numpy as jnp
from jax import lax
from jax.experimental import pallas as pl
from jax.experimental.pallas import tpu as pltpu
from jax.sharding import PartitionSpec as P

STEP = 0.04
LANES = 128
PAD = 8
F32, BF16 = jnp.float32, jnp.bfloat16
MESH = pl.DeviceIdType.MESH
SIDES = [(dr, dc) for dr in (-1, 0, 1) for dc in (-1, 0, 1) if (dr, dc) != (0, 0)]


def split(value):
    high = value.astype(BF16)
    return high, (value - high.astype(F32)).astype(BF16)


def iota(shape, dim):
    return lax.broadcasted_iota(jnp.int32, shape, dim)


def advance_kernel(
    rows, panels, voxels, grid_rows, grid_cols,
    cov, classes_in, feed_in, conv_in, diff_in,
    stage, u_edge, ge, go, full, spread, halo, inner, halo_col, halo_row,
    vx, high, low, whi, wlo, w_one, w_two, half, noise, feed_of, conv_of, ext_s, ext_x, ext_a, ext_b, col,
    classes, feed, conv, diff, edge, send_row, send_col, got_row, got_col, got_corner,
    load_sem, small_sem, send_sem, recv_sem,
):
    row, cols_at = lax.axis_index("row"), lax.axis_index("col")
    groups = rows // 16
    half_rows = rows // 2
    def there(dr, dc):
        ok = None
        for at, step, size in ((row, dr, grid_rows), (cols_at, dc, grid_cols)):
            if step:
                one = (at + step >= 0) & (at + step < size)
                ok = one if ok is None else ok & one
        return ok

    barrier = pltpu.get_barrier_semaphore()
    count = jnp.int32(0)
    across = {1: row == grid_rows // 2 - 1, -1: row == grid_rows // 2}
    distant = across[1] | across[-1]

    def each_side(act):
        for dr in (1, -1):
            @pl.when(across[dr])
            def _(dr=dr):
                for dc in (0, 1, -1):
                    pl.when(there(dr, dc))(lambda dc=dc: act(dr, dc))
        for dr, dc in SIDES:
            ok = there(dr, dc)
            pl.when(ok & jnp.logical_not(across[dr]) if dr else ok)(lambda dr=dr, dc=dc: act(dr, dc))

    for dr, dc in SIDES:
        count += there(dr, dc).astype(jnp.int32)
    each_side(lambda dr, dc: pl.semaphore_signal(
        barrier, inc=1, device_id=(row + dr, cols_at + dc), device_id_type=MESH
    ))

    small = [
        pltpu.make_async_copy(a, b, small_sem.at[n])
        for n, (a, b) in enumerate((
            (classes_in, classes), (feed_in, feed), (conv_in, conv), (diff_in, diff),
            (cov.at[pl.ds(0, 8), :], edge.at[0]), (cov.at[pl.ds(rows - 8, 8), :], edge.at[1]),
        ))
    ]
    for copy in small:
        copy.start()
    def load(p):
        return pltpu.make_async_copy(
            cov.at[:, pl.ds(pl.multiple_of(p * LANES, LANES), LANES)],
            vx.at[p + 1, pl.ds(PAD, rows), :],
            load_sem.at[p],
        )

    load(0).start()
    load(panels - 1).start()

    def start_load(p, _):
        load(p).start()
        return 0

    lax.fori_loop(1, panels - 1, start_load, 0)

    zero = jnp.zeros((8, LANES), F32)
    for p in range(panels):
        vx[p + 1, 0:PAD, :] = zero
        vx[p + 1, PAD + rows : 2 * PAD + rows, :] = zero
    for i, at in enumerate((0, grid_cols - 1)):
        @pl.when(cols_at == at)
        def _(i=i):
            got_col[i] = jnp.zeros(got_col.shape[1:], F32)
            got_corner[i] = zero
            got_corner[2 + i] = zero

    for copy in small[:4]:
        copy.wait()
    d0, d1 = diff[0] * STEP, diff[1] * STEP
    spread[0] = jnp.full((8, LANES), d0, F32)
    spread[1] = jnp.full((8, LANES), d1, F32)
    ids = classes[...]
    a_all, b_all = jnp.zeros(ids.shape, F32), jnp.zeros(ids.shape, F32)
    for k in range(feed.shape[0]):
        a_all = jnp.where(ids == k, feed[k], a_all)
        b_all = jnp.where(ids == k, conv[k], b_all)
    feed_of[...] = a_all
    conv_of[...] = b_all
    class_rows = voxels // LANES

    lane8 = iota((8, LANES), 1)
    row_at = row * (half_rows // LANES)
    for t in range(half_rows // LANES):
        a = jnp.broadcast_to(feed_of[pl.ds(row_at + t, 1), :], (LANES, LANES)).T
        b = jnp.broadcast_to(conv_of[pl.ds(row_at + t, 1), :], (LANES, LANES)).T
        voxel = row * half_rows + t * LANES + iota((LANES, LANES), 0)
        near = 2.0 - (voxel == 0).astype(F32) - (voxel == voxels - 1).astype(F32)
        here = pl.ds(t * LANES, LANES)
        a2, ab = a * a, a * b
        values = (
            STEP * (b - 1.0) - d0 * near, -STEP * a2 - d1 * near, STEP * a2, -STEP * b,
        )
        for i, value in enumerate(values):
            full[i, here, :] = value
            half[i, here, :] = 0.5 * value
        noise[0, here, :] = STEP * (2.0 * a + 2.0 * ab)
        noise[1, here, :] = STEP * (2.0 * ab)
        noise[2, here, :] = STEP * (-2.0 * ab)

    first = cols_at * (panels // 2)
    lane = iota((panels // 2, LANES), 1)
    for t in range(2):
        pick = lane // 2 + (LANES // 2) * t
        for source, target in ((feed_of, ext_a), (conv_of, ext_b)):
            value = source[pl.ds(pl.multiple_of(first, panels // 2), panels // 2), :]
            target[pl.ds(8 + t, panels // 2, stride=2), :] = jnp.take_along_axis(value, pick, axis=1)
    before, after = jnp.maximum(first - 1, 0), jnp.minimum(first + panels // 2, class_rows - 1)
    for source, target in ((feed_of, ext_a), (conv_of, ext_b)):
        value = jnp.broadcast_to(source[pl.ds(before, 1), :], (8, LANES))
        target[0:8, :] = jnp.take_along_axis(value, lane8 // 2 + LANES // 2, axis=1)
        value = jnp.broadcast_to(source[pl.ds(after, 1), :], (8, LANES))
        target[8 + panels : 16 + panels, :] = jnp.take_along_axis(value, lane8 // 2, axis=1)
    shape = ext_a.shape
    lane_e = iota(shape, 1)
    even_e = lane_e % 2 == 0
    a, b = ext_a[...], ext_b[...]
    voxel = cols_at * (panels * LANES // 2) + (iota(shape, 0) - 8) * (LANES // 2) + lane_e // 2
    near = 2.0 - (voxel == 0).astype(F32) - (voxel == voxels - 1).astype(F32)
    d_e = jnp.where(even_e, d0, d1)
    ext_s[...] = STEP * jnp.where(even_e, b - 1.0, -a * a) - d_e * near
    ext_x[...] = STEP * jnp.where(even_e, a * a, -b)

    mid = slice(8, 8 + panels)
    lane = iota((panels, LANES), 1)
    even = lane % 2 == 0
    near, a, b = near[mid], a[mid], b[mid]
    d = jnp.where(even, d0, d1)
    other_d = jnp.where(even, d1, d0)

    def shifted(ref):
        here = ref[mid, :]
        left = pltpu.roll(jnp.where(lane >= LANES - 2, ref[7 : 7 + panels, :], here), 2, 1)
        right = pltpu.roll(jnp.where(lane < 2, ref[9 : 9 + panels, :], here), LANES - 2, 1)
        mate = jnp.where(even, pltpu.roll(here, LANES - 1, 1), pltpu.roll(here, 1, 1))
        return here, mate, jnp.where(even, right, left), jnp.where(even, left, right)

    s, s_mate, s_fore, s_back = shifted(ext_s)
    x, x_mate, x_fore, x_back = shifted(ext_x)
    col[0] = s
    col[1] = x
    col[2] = d
    col[3] = 1.0 + s + 0.5 * (s * s + x * x_mate + d * d * near)
    col[4] = x + 0.5 * x * (s + s_mate)
    col[5] = d + 0.5 * d * (s + s_fore)
    col[6] = d + 0.5 * d * (s + s_back)
    col[7] = 0.5 * d * d
    col[8] = 0.5 * (x * other_d + d * x_fore)
    col[9] = 0.5 * (x * other_d + d * x_back)
    ab = a * b
    same, cross = STEP * (jnp.where(even, 2.0 * a, 0.0) + 2.0 * ab), STEP * (-2.0 * ab)
    col[10] = jnp.where(even, same, cross)
    col[11] = jnp.where(even, cross, same)

    load(0).wait()
    load(panels - 1).wait()
    lane8 = iota((8, LANES), 1)
    sub8 = iota((8, LANES), 0)
    lane16 = iota((16, LANES), 1)
    for side, panel, start in ((0, 1, 0), (1, panels, LANES - 4)):
        packed = jnp.zeros((16, LANES), F32)
        for g in range(groups):
            piece = vx[panel, PAD + 16 * g : PAD + 16 * g + 16, :]
            turn = (4 * g - start) % LANES
            piece = pltpu.roll(piece, turn, 1) if turn else piece
            packed = jnp.where((lane16 >= 4 * g) & (lane16 < 4 * g + 4), piece, packed)
        send_col[side] = packed

    small[4].wait()
    small[5].wait()
    for k in range(panels // 2):
        one, two = (slice(LANES * (2 * k + t), LANES * (2 * k + t + 1)) for t in (0, 1))
        send_row[0, 8 * k : 8 * k + 8, :] = jnp.where(sub8 < 4, edge[0, :, one], pltpu.roll(edge[0, :, two], 4, 0))
        send_row[1, 8 * k : 8 * k + 8, :] = jnp.where(sub8 < 4, pltpu.roll(edge[1, :, one], 4, 0), edge[1, :, two])

    tile_rows = 4 * panels

    def landing(i):
        dr, dc = SIDES[i]
        if dc == 0:
            return got_row.at[0 if dr > 0 else 1, pl.ds(8, tile_rows), :]
        if dr == 0:
            return got_col.at[0 if dc > 0 else 1]
        return got_corner.at[(2 if dr < 0 else 0) + (1 if dc < 0 else 0)]

    def remote(i):
        dr, dc = SIDES[i]
        if dc == 0:
            source = send_row.at[0 if dr < 0 else 1]
        elif dr == 0:
            source = send_col.at[0 if dc < 0 else 1]
        else:
            source = edge.at[0 if dr < 0 else 1, :, pl.ds(0 if dc < 0 else (panels - 1) * LANES, LANES)]
        return pltpu.make_async_remote_copy(
            src_ref=source, dst_ref=landing(i), send_sem=send_sem.at[i], recv_sem=recv_sem.at[i],
            device_id=(row + dr, cols_at + dc), device_id_type=MESH,
        )

    def send():
        pl.semaphore_wait(barrier, count)
        each_side(lambda dr, dc: remote(SIDES.index((dr, dc))).start())

    at16 = iota((16, LANES), 1)
    in16 = iota((16, LANES), 0)
    owner = (at16 + 4) // 32, (at16 + 20) // 32
    codes = [
        (16 * tile + in16 - at16) * (1 - 2 * (at16 % 2)) for tile in (2 * owner[0], 2 * owner[1] - 1)
    ]
    wide_at = iota((16, 2 * LANES), 1) % LANES
    wide_owner = (wide_at + 4) // 32, (wide_at + 20) // 32
    blank = jnp.zeros((16, 2 * LANES), BF16)

    def weights(p, _):
        c = [jnp.broadcast_to(col[i, pl.ds(p, 1), :], (16, LANES)) for i in range(10)]
        none = jnp.zeros((16, LANES), F32)
        pairs = []
        for k in codes:
            z = k == 0, k == 1, k == 2, k == -2
            u = jnp.where(jnp.abs(k) == 4, c[7], none)
            u = jnp.where(k == 3, c[8], u)
            u = jnp.where(k == -1, c[9], u)
            u = jnp.where(z[0], c[3], jnp.where(z[1], c[4], jnp.where(z[2], c[5], jnp.where(z[3], c[6], u))))
            w = jnp.where(z[0], c[0], jnp.where(z[1], c[1], jnp.where(z[2] | z[3], c[2], none)))
            pairs.append(split(jnp.concatenate([u, w], axis=1)))

        def tile(i, part):
            odd = i % 2
            return jnp.where(wide_owner[odd] == (i + odd) // 2, pairs[odd][part], blank)

        for i in range(8):
            whi[p, 16 * i : 16 * i + 16, :] = tile(i, 0)
            wlo[p, 16 * i : 16 * i + 16, :] = tile(i, 1)
        before, after = [tile(-1, part) for part in (0, 1)], [tile(8, part) for part in (0, 1)]
        for i, value in enumerate((after[0], before[0], after[0], before[1], after[1], blank, blank, before[0])):
            wlo[p, LANES + 16 * i : LANES + 16 * i + 16, :] = value
        return 0

    lax.fori_loop(0, panels, weights, 0)

    def split_panel(p):
        for g in range(groups):
            e = vx[p, pl.ds(PAD + 16 * g, 8, stride=2), :]
            o = vx[p, pl.ds(PAD + 16 * g + 1, 8, stride=2), :]
            hi, lo = split(jnp.concatenate([e, o], axis=0))
            high[p, 16 * g : 16 * g + 16, :] = hi
            low[p, 16 * g : 16 * g + 16, :] = lo

    split_panel(1)
    split_panel(panels)

    def next_panel(p, _):
        load(p - 1).wait()
        split_panel(p)
        return 0

    lax.fori_loop(2, panels, next_panel, 0)
    odd = cols_at % 2 == 1
    pl.when(jnp.logical_not(distant | odd))(send)

    at_rows = iota((rows, LANES), 1)
    next_lanes = at_rows < LANES // 2
    low_lanes = (at_rows >= 16) & (at_rows < 48)
    again_lanes = (at_rows >= 48) & (at_rows < 80)

    def columns(p, w_ref):
        hi, lo = high[p], low[p]
        edge_hi = jnp.where(next_lanes, high[p + 1], high[p - 1])
        edge_lo = jnp.where(next_lanes, low[p + 1], low[p - 1])
        edges = jnp.where(
            low_lanes, pltpu.roll(edge_lo, 32, 1), jnp.where(again_lanes, pltpu.roll(edge_hi, 64, 1), edge_hi)
        )
        lhs = jnp.concatenate([hi, lo, hi, edges], axis=1)
        rhs = jnp.concatenate([whi[p - 1], whi[p - 1], wlo[p - 1]], axis=0)
        both = jnp.dot(lhs, rhs, preferred_element_type=F32)
        w_ref[...] = both
        u_edge[p - 1, 0:16, :] = both[0:16, :LANES]
        u_edge[p - 1, 16:32, :] = both[rows - 16 :, :LANES]

    def own_rows(p, w_ref):
        for g in range(groups):
            at = PAD + 16 * g
            e, o = vx[p, pl.ds(at, 8, stride=2), :], vx[p, pl.ds(at + 1, 8, stride=2), :]
            e_sum = vx[p, pl.ds(at - 2, 8, stride=2), :] + vx[p, pl.ds(at + 2, 8, stride=2), :]
            o_sum = vx[p, pl.ds(at - 1, 8, stride=2), :] + vx[p, pl.ds(at + 3, 8, stride=2), :]
            c = [half[n, 8 * g : 8 * g + 8, :] for n in range(4)]
            ge[p - 1, PAD + 8 * g : PAD + 8 * g + 8, :] = (
                e + w_ref[16 * g : 16 * g + 8, LANES:] + ((c[0] * e + c[2] * o) + (0.5 * d0) * e_sum)
            )
            go[p - 1, PAD + 8 * g : PAD + 8 * g + 8, :] = (
                o + w_ref[16 * g + 8 : 16 * g + 16, LANES:] + ((c[1] * o + c[3] * e) + (0.5 * d1) * o_sum)
            )
        for g in range(1, groups - 1):
            at = PAD + 8 * g
            e, o = ge[p - 1, at : at + 8, :], go[p - 1, at : at + 8, :]
            e_sum = ge[p - 1, at - 1 : at + 7, :] + ge[p - 1, at + 1 : at + 9, :]
            o_sum = go[p - 1, at - 1 : at + 7, :] + go[p - 1, at + 1 : at + 9, :]
            c = [full[n, 8 * g : 8 * g + 8, :] for n in range(4)]
            stage[p - 1, pl.ds(16 * g, 8, stride=2), :] = (
                w_ref[16 * g : 16 * g + 8, :LANES] + ((c[0] * e + c[2] * o) + d0 * e_sum)
            )
            stage[p - 1, pl.ds(16 * g + 1, 8, stride=2), :] = (
                w_ref[16 * g + 8 : 16 * g + 16, :LANES] + ((c[1] * o + c[3] * e) + d1 * o_sum)
            )

    columns(2, w_one)

    steps = (panels - 4) // 2
    early = 1

    def middle(i, _):
        pl.when((distant | odd) & (i == early))(send)
        p = 3 + 2 * i
        own_rows(p - 1, w_one)
        columns(p, w_two)
        own_rows(p, w_two)
        columns(p + 1, w_one)
        return 0

    lax.fori_loop(0, steps, middle, 0)
    own_rows(panels - 2, w_one)
    columns(panels - 1, w_two)

    def wait_recv(dr, dc):
        @pl.when(there(-dr, -dc))
        def _():
            remote(SIDES.index((dr, dc))).wait_recv()

    wait_recv(0, 1)
    wait_recv(0, -1)
    for side, panel, start in ((0, 0, LANES - 4), (1, panels + 1, 0)):
        packed = got_col[side]
        for g in range(groups):
            turn = (start - 4 * g) % LANES
            vx[panel, PAD + 16 * g : PAD + 16 * g + 16, :] = pltpu.roll(packed, turn, 1) if turn else packed
        split_panel(panel)

    own_rows(panels - 1, w_two)
    columns(1, w_one)
    own_rows(1, w_one)
    columns(panels, w_two)
    own_rows(panels, w_two)

    per_panel = LANES // 16
    even_lane = lane8 % 2 == 0

    def add_noise(g, t, move):
        c = [col[i, pl.ds(t, 1), :] for i in (0, 1, 2, 10, 11)]
        here = slice(8 * g, 8 * g + 8)
        f = [full[i, here, :] for i in range(4)]
        n_e, n_o, n_x = (noise[i, here, :] for i in range(3))
        gap = (move * (LANES // 2) + lane8 // 2) - (8 * (g % per_panel) + sub8)
        on, beside = gap == 0, jnp.abs(gap) == 1
        for odd, s_r, x_r, d_r, one, two, mine, mate in (
            (0, f[0], f[2], d0, c[3], c[4], jnp.where(even_lane, n_e, n_x), jnp.where(even_lane, n_x, n_e)),
            (1, f[1], f[3], d1, c[4], c[3], jnp.where(even_lane, n_x, n_o), jnp.where(even_lane, n_o, n_x)),
        ):
            centre = mine + 0.5 * ((s_r * one + x_r * two) + (c[0] * mine + c[1] * mate))
            side = 0.5 * (d_r * one + c[2] * mine)
            value = jnp.where(on, centre, jnp.where(beside, side, 0.0))
            if g in (0, groups - 1):
                at = 8 * odd + (16 if g else 0)
                u_edge[t, at : at + 8, :] += value
            else:
                stage[t, pl.ds(16 * g + odd, 8, stride=2), :] += value

    ratio = panels * LANES // rows
    first_panel = (row - cols_at * ratio) * (rows // LANES)

    @pl.when((first_panel >= 0) & (first_panel < panels))
    def _():
        for g in range(groups):
            t = first_panel + g // per_panel
            add_noise(g, t, 0)
            if g % per_panel == 0 and g:
                add_noise(g, t - 1, -1)
            if g % per_panel == per_panel - 1 and g < groups - 1:
                add_noise(g, t + 1, 1)

    @pl.when((first_panel >= 1) & (first_panel <= panels))
    def _():
        add_noise(0, first_panel - 1, -1)

    @pl.when((first_panel + rows // LANES >= 0) & (first_panel + rows // LANES < panels))
    def _():
        add_noise(groups - 1, first_panel + rows // LANES, 1)

    upper = sub8 < 4
    species = sub8 % 2 == 0
    for k in range(panels // 2):
        here = slice(8 * k, 8 * k + 8)
        one, two = 2 * k + 1, 2 * k + 2
        e = PAD + rows
        inner[0, here, :] = jnp.where(upper, vx[one, PAD - 2 : PAD + 6, :], vx[two, PAD - 6 : PAD + 2, :])
        inner[1, here, :] = jnp.where(upper, vx[one, e - 2 : e + 6, :], vx[two, e - 6 : e + 2, :])
        for i in range(3):
            halo_col[i, here, :] = jnp.where(upper, col[i, 2 * k : 2 * k + 1, :], col[i, 2 * k + 1 : 2 * k + 2, :])
    for side in (0, 1):
        voxel = jnp.clip(row * half_rows + (-1 if side == 0 else half_rows), 0, voxels - 1)
        pick = lane8 * 0 + voxel % LANES
        a = jnp.broadcast_to(feed_of[pl.ds(voxel // LANES, 1), :], (8, LANES))
        b = jnp.broadcast_to(conv_of[pl.ds(voxel // LANES, 1), :], (8, LANES))
        a = jnp.sum(jnp.where(lane8 == pick, a, 0.0), axis=1, keepdims=True)
        b = jnp.sum(jnp.where(lane8 == pick, b, 0.0), axis=1, keepdims=True)
        end = (voxel == 0) | (voxel == voxels - 1)
        near = jnp.where(end, 1.0, 2.0)
        d_r = jnp.where(species, d0, d1)
        halo_row[side, 0] = jnp.broadcast_to(STEP * jnp.where(species, b - 1.0, -a * a) - d_r * near, (8, LANES))
        halo_row[side, 1] = jnp.broadcast_to(STEP * jnp.where(species, a * a, -b), (8, LANES))
        halo_row[side, 2] = jnp.broadcast_to(d_r, (8, LANES))
        ok = there(-1, 0) if side == 0 else there(1, 0)
        halo_row[side, 3] = jnp.full((8, LANES), ok.astype(F32))

    for dr, dc in SIDES:
        if dr:
            wait_recv(dr, dc)
    for side in (0, 1):
        halo[side, 8 : 8 + tile_rows, :] = got_row[side, 8 : 8 + tile_rows, :]
        halo[side, 0:8, :] = got_corner[2 * side] if side == 0 else pltpu.roll(got_corner[2 * side], 4, 0)
        right = got_corner[2 * side + 1]
        halo[side, 8 + tile_rows : 16 + tile_rows, :] = pltpu.roll(right, 4, 0) if side == 0 else right

    for i, (dr, dc) in enumerate(SIDES):
        @pl.when(there(dr, dc))
        def _(i=i):
            remote(i).wait_send()


def finish_kernel(
    rows, panels,
    stage, u_edge, ge, go, full, spread, halo, inner, halo_col, halo_row,
    out, tile_g, near_g, ends, wide, sem,
):
    d0, d1 = spread[0], spread[1]
    groups = rows // 16
    half_rows = rows // 2

    def store(p):
        return pltpu.make_async_copy(
            stage.at[p, pl.ds(16, rows - 32), :],
            out.at[pl.ds(16, rows - 32), pl.ds(p * LANES, LANES)],
            sem.at[p],
        )

    def store_end(side):
        return pltpu.make_async_copy(
            wide.at[side], out.at[pl.ds(side * (rows - 16), 16), :], sem.at[panels + side]
        )

    for p in range(panels):
        store(p).start()

    lane8 = iota((8, LANES), 1)
    sub8 = iota((8, LANES), 0)
    even8 = lane8 % 2 == 0
    species = sub8 % 2 == 0
    for side in (0, 1):
        s_r, x_r, d_r = halo_row[side, 0], halo_row[side, 1], halo_row[side, 2]
        ok = halo_row[side, 3] > 0.5
        for k in range(panels // 2):
            at = 8 + 8 * k
            here = slice(8 * k, 8 * k + 8)
            tile, left, right = (halo[side, at + t : at + t + 8, :] for t in (0, -4, 4))
            mate = jnp.where(even8, pltpu.roll(tile, LANES - 1, 1), pltpu.roll(tile, 1, 1))
            beside = pltpu.roll(jnp.where(lane8 >= LANES - 2, left, tile), 2, 1) + pltpu.roll(
                jnp.where(lane8 < 2, right, tile), LANES - 2, 1
            )
            w = halo_col[0, here, :] * tile + halo_col[1, here, :] * mate + halo_col[2, here, :] * beside
            row_mate = jnp.where(species, halo[side, at + 1 : at + 9, :], halo[side, at - 1 : at + 7, :])
            away = halo[side, at - 2 : at + 6, :] if side == 0 else halo[side, at + 2 : at + 10, :]
            g = tile + w + 0.5 * (s_r * tile + x_r * row_mate + d_r * (away + inner[side, here, :]))
            tile_g[side, at : at + 8, :] = jnp.where(ok, g, 0.0)

        first = 0 if side == 0 else half_rows - 8
        c = [full[i, first : first + 8, :] for i in range(4)]
        for p in range(panels):
            at = 8 + 8 * (p // 2) + 4 * (p % 2)
            for o, ref, dd in ((0, ge, d0), (1, go, d1)):
                mine = ref[p, PAD + first : PAD + first + 8, :]
                if side == 0:
                    fix = halo[side, at + 2 + o : at + 10 + o, :]
                    near_g[o, 0:8, :] = tile_g[side, at + o - 5 : at + o + 3, :]
                    near_g[o, 16:24, :] = ref[p, PAD + 8 : PAD + 16, :]
                else:
                    fix = halo[side, at + o - 7 : at + o + 1, :]
                    near_g[o, 0:8, :] = ref[p, PAD + first - 8 : PAD + first, :]
                    near_g[o, 16:24, :] = tile_g[side, at + o : at + o + 8, :]
                fix = jnp.where(ok & (sub8 == (0 if side == 0 else 7)), (0.5 * dd) * fix, 0.0)
                near_g[o, 8:16, :] = mine + fix
            e, o = near_g[0, 8:16, :], near_g[1, 8:16, :]
            e_sum = near_g[0, 7:15, :] + near_g[0, 9:17, :]
            o_sum = near_g[1, 7:15, :] + near_g[1, 9:17, :]
            u = 16 * side
            ends[p, pl.ds(0, 8, stride=2), :] = u_edge[p, u : u + 8, :] + ((c[0] * e + c[2] * o) + d0 * e_sum)
            ends[p, pl.ds(1, 8, stride=2), :] = u_edge[p, u + 8 : u + 16, :] + ((c[1] * o + c[3] * e) + d1 * o_sum)
            wide[side, :, LANES * p : LANES * p + LANES] = ends[p]
        store_end(side).start()

    for p in range(panels):
        store(p).wait()
    for side in (0, 1):
        store_end(side).wait()


def body(covariance, classes, feed_rate, conversion_rate, diffusion):
    rows, cols = covariance.shape
    panels = cols // LANES
    voxels = classes.shape[0]
    half_rows = rows // 2
    vmem = pl.BlockSpec(memory_space=pltpu.VMEM)
    hbm = pl.BlockSpec(memory_space=pl.ANY)
    sizes = (lax.axis_size("row"), lax.axis_size("col"))
    inputs = (covariance, classes.reshape(voxels // LANES, LANES), feed_rate, conversion_rate, diffusion)
    results = pl.pallas_call(
        functools.partial(advance_kernel, rows, panels, voxels, *sizes),
        out_shape=[
            pltpu.VMEM((panels, rows, LANES), F32),
            pltpu.VMEM((panels, 32, LANES), F32),
            pltpu.VMEM((panels, half_rows + 2 * PAD, LANES), F32),
            pltpu.VMEM((panels, half_rows + 2 * PAD, LANES), F32),
            pltpu.VMEM((4, half_rows, LANES), F32),
            pltpu.VMEM((2, 8, LANES), F32),
            pltpu.VMEM((2, 4 * panels + 16, LANES), F32),
            pltpu.VMEM((2, 4 * panels, LANES), F32),
            pltpu.VMEM((3, 4 * panels, LANES), F32),
            pltpu.VMEM((2, 4, 8, LANES), F32),
        ],
        in_specs=[hbm] * 5,
        out_specs=[vmem] * 10,
        scratch_shapes=[
            pltpu.VMEM((panels + 2, rows + 2 * PAD, LANES), F32),
            pltpu.VMEM((panels + 2, rows, LANES), BF16),
            pltpu.VMEM((panels + 2, rows, LANES), BF16),
            pltpu.VMEM((panels, LANES, 2 * LANES), BF16),
            pltpu.VMEM((panels, 2 * LANES, 2 * LANES), BF16),
            pltpu.VMEM((rows, 2 * LANES), F32),
            pltpu.VMEM((rows, 2 * LANES), F32),
            pltpu.VMEM((4, half_rows, LANES), F32),
            pltpu.VMEM((3, half_rows, LANES), F32),
            pltpu.VMEM((voxels // LANES, LANES), F32),
            pltpu.VMEM((voxels // LANES, LANES), F32),
            pltpu.VMEM((panels + 16, LANES), F32),
            pltpu.VMEM((panels + 16, LANES), F32),
            pltpu.VMEM((panels + 16, LANES), F32),
            pltpu.VMEM((panels + 16, LANES), F32),
            pltpu.VMEM((12, panels, LANES), F32),
            pltpu.VMEM((voxels // LANES, LANES), jnp.int32),
            pltpu.SMEM(feed_rate.shape, F32),
            pltpu.SMEM(conversion_rate.shape, F32),
            pltpu.SMEM(diffusion.shape, F32),
            pltpu.VMEM((2, 8, cols), F32),
            pltpu.VMEM((2, 4 * panels, LANES), F32),
            pltpu.VMEM((2, 16, LANES), F32),
            pltpu.VMEM((2, 4 * panels + 16, LANES), F32),
            pltpu.VMEM((2, 16, LANES), F32),
            pltpu.VMEM((4, 8, LANES), F32),
            pltpu.SemaphoreType.DMA((panels,)),
            pltpu.SemaphoreType.DMA((6,)),
            pltpu.SemaphoreType.DMA((8,)),
            pltpu.SemaphoreType.DMA((8,)),
        ],
        compiler_params=pltpu.CompilerParams(
            collective_id=0, has_side_effects=True, vmem_limit_bytes=32 << 20
        ),
        name="halo_and_columns",
    )(*(pltpu.with_memory_space_constraint(x, pltpu.HBM) for x in inputs))
    return pl.pallas_call(
        functools.partial(finish_kernel, rows, panels),
        out_shape=jax.ShapeDtypeStruct((rows, cols), F32),
        in_specs=[vmem] * 10,
        out_specs=hbm,
        scratch_shapes=[
            pltpu.VMEM((2, 4 * panels + 16, LANES), F32),
            pltpu.VMEM((2, 24, LANES), F32),
            pltpu.VMEM((panels, 16, LANES), F32),
            pltpu.VMEM((2, 16, cols), F32),
            pltpu.SemaphoreType.DMA((panels + 2,)),
        ],
        compiler_params=pltpu.CompilerParams(vmem_limit_bytes=24 << 20),
        name="rows",
    )(*results)


def solution(mesh):
    in_specs = (P("row", "col"), P(), P(), P(), P())
    return jax.shard_map(body, mesh=mesh, in_specs=in_specs, out_specs=P("row", "col"), check_vma=False)
```

```python
import functools

import jax
import jax.numpy as jnp
from jax import lax
from jax.experimental import pallas as pl
from jax.experimental.pallas import tpu as pltpu
from jax.sharding import PartitionSpec as P

STEP = 0.04
LANES = 128
PAD = 8
F32, BF16 = jnp.float32, jnp.bfloat16
MESH = pl.DeviceIdType.MESH
SIDES = [(dr, dc) for dr in (-1, 0, 1) for dc in (-1, 0, 1) if (dr, dc) != (0, 0)]


def split(value):
    high = value.astype(BF16)
    return high, (value - high.astype(F32)).astype(BF16)


def iota(shape, dim):
    return lax.broadcasted_iota(jnp.int32, shape, dim)


def advance_kernel(
    rows, panels, voxels, grid_rows, grid_cols,
    cov, classes_in, feed_in, conv_in, diff_in,
    stage, u_edge, ge, go, full, spread, got_row, got_corner, inner, halo_col, halo_row,
    vx, high, low, whi, wlo, w_one, w_two, half, noise, feed_of, conv_of, ext_s, ext_x, ext_a, ext_b, col,
    classes, feed, conv, diff, edge, send_row, send_col, got_col,
    load_sem, small_sem, send_sem, recv_sem,
):
    row, cols_at = lax.axis_index("row"), lax.axis_index("col")
    groups = rows // 16
    half_rows = rows // 2
    def there(dr, dc):
        ok = None
        for at, step, size in ((row, dr, grid_rows), (cols_at, dc, grid_cols)):
            if step:
                one = (at + step >= 0) & (at + step < size)
                ok = one if ok is None else ok & one
        return ok

    barrier = pltpu.get_barrier_semaphore()
    count = jnp.int32(0)
    across = {1: row == grid_rows // 2 - 1, -1: row == grid_rows // 2}
    distant = across[1] | across[-1]

    def each_side(act):
        for dr in (1, -1):
            @pl.when(across[dr])
            def _(dr=dr):
                for dc in (-1, 0, 1):
                    pl.when(there(dr, dc))(lambda dc=dc: act(dr, dc))
        for dr, dc in SIDES:
            ok = there(dr, dc)
            pl.when(ok & jnp.logical_not(across[dr]) if dr else ok)(lambda dr=dr, dc=dc: act(dr, dc))

    for dr, dc in SIDES:
        count += there(dr, dc).astype(jnp.int32)
    each_side(lambda dr, dc: pl.semaphore_signal(
        barrier, inc=1, device_id=(row + dr, cols_at + dc), device_id_type=MESH
    ))

    small = [
        pltpu.make_async_copy(a, b, small_sem.at[n])
        for n, (a, b) in enumerate((
            (classes_in, classes), (feed_in, feed), (conv_in, conv), (diff_in, diff),
            (cov.at[pl.ds(0, 8), :], edge.at[0]), (cov.at[pl.ds(rows - 8, 8), :], edge.at[1]),
        ))
    ]
    for copy in small:
        copy.start()
    def load(p):
        return pltpu.make_async_copy(
            cov.at[:, pl.ds(pl.multiple_of(p * LANES, LANES), LANES)],
            vx.at[p + 1, pl.ds(PAD, rows), :],
            load_sem.at[p],
        )

    load(0).start()
    load(panels - 1).start()

    def start_load(p, _):
        load(p).start()
        return 0

    lax.fori_loop(1, panels - 1, start_load, 0)

    zero = jnp.zeros((8, LANES), F32)
    for p in range(panels):
        vx[p + 1, 0:PAD, :] = zero
        vx[p + 1, PAD + rows : 2 * PAD + rows, :] = zero
    for i, at in enumerate((0, grid_cols - 1)):
        @pl.when(cols_at == at)
        def _(i=i):
            got_col[i] = jnp.zeros(got_col.shape[1:], F32)
            got_corner[i] = zero
            got_corner[2 + i] = zero

    for copy in small[:4]:
        copy.wait()
    d0, d1 = diff[0] * STEP, diff[1] * STEP
    spread[0] = jnp.full((8, LANES), d0, F32)
    spread[1] = jnp.full((8, LANES), d1, F32)
    ids = classes[...]
    a_all, b_all = jnp.zeros(ids.shape, F32), jnp.zeros(ids.shape, F32)
    for k in range(feed.shape[0]):
        a_all = jnp.where(ids == k, feed[k], a_all)
        b_all = jnp.where(ids == k, conv[k], b_all)
    feed_of[...] = a_all
    conv_of[...] = b_all
    class_rows = voxels // LANES

    lane8 = iota((8, LANES), 1)
    row_at = row * (half_rows // LANES)
    for t in range(half_rows // LANES):
        a = jnp.broadcast_to(feed_of[pl.ds(row_at + t, 1), :], (LANES, LANES)).T
        b = jnp.broadcast_to(conv_of[pl.ds(row_at + t, 1), :], (LANES, LANES)).T
        voxel = row * half_rows + t * LANES + iota((LANES, LANES), 0)
        near = 2.0 - (voxel == 0).astype(F32) - (voxel == voxels - 1).astype(F32)
        here = pl.ds(t * LANES, LANES)
        a2, ab = a * a, a * b
        values = (
            STEP * (b - 1.0) - d0 * near, -STEP * a2 - d1 * near, STEP * a2, -STEP * b,
        )
        for i, value in enumerate(values):
            full[i, here, :] = value
            half[i, here, :] = 0.5 * value
        noise[0, here, :] = STEP * (2.0 * a + 2.0 * ab)
        noise[1, here, :] = STEP * (2.0 * ab)
        noise[2, here, :] = STEP * (-2.0 * ab)

    first = cols_at * (panels // 2)
    lane = iota((panels // 2, LANES), 1)
    for t in range(2):
        pick = lane // 2 + (LANES // 2) * t
        for source, target in ((feed_of, ext_a), (conv_of, ext_b)):
            value = source[pl.ds(pl.multiple_of(first, panels // 2), panels // 2), :]
            target[pl.ds(8 + t, panels // 2, stride=2), :] = jnp.take_along_axis(value, pick, axis=1)
    before, after = jnp.maximum(first - 1, 0), jnp.minimum(first + panels // 2, class_rows - 1)
    for source, target in ((feed_of, ext_a), (conv_of, ext_b)):
        value = jnp.broadcast_to(source[pl.ds(before, 1), :], (8, LANES))
        target[0:8, :] = jnp.take_along_axis(value, lane8 // 2 + LANES // 2, axis=1)
        value = jnp.broadcast_to(source[pl.ds(after, 1), :], (8, LANES))
        target[8 + panels : 16 + panels, :] = jnp.take_along_axis(value, lane8 // 2, axis=1)
    shape = ext_a.shape
    lane_e = iota(shape, 1)
    even_e = lane_e % 2 == 0
    a, b = ext_a[...], ext_b[...]
    voxel = cols_at * (panels * LANES // 2) + (iota(shape, 0) - 8) * (LANES // 2) + lane_e // 2
    near = 2.0 - (voxel == 0).astype(F32) - (voxel == voxels - 1).astype(F32)
    d_e = jnp.where(even_e, d0, d1)
    ext_s[...] = STEP * jnp.where(even_e, b - 1.0, -a * a) - d_e * near
    ext_x[...] = STEP * jnp.where(even_e, a * a, -b)

    mid = slice(8, 8 + panels)
    lane = iota((panels, LANES), 1)
    even = lane % 2 == 0
    near, a, b = near[mid], a[mid], b[mid]
    d = jnp.where(even, d0, d1)
    other_d = jnp.where(even, d1, d0)

    def shifted(ref):
        here = ref[mid, :]
        left = pltpu.roll(jnp.where(lane >= LANES - 2, ref[7 : 7 + panels, :], here), 2, 1)
        right = pltpu.roll(jnp.where(lane < 2, ref[9 : 9 + panels, :], here), LANES - 2, 1)
        mate = jnp.where(even, pltpu.roll(here, LANES - 1, 1), pltpu.roll(here, 1, 1))
        return here, mate, jnp.where(even, right, left), jnp.where(even, left, right)

    s, s_mate, s_fore, s_back = shifted(ext_s)
    x, x_mate, x_fore, x_back = shifted(ext_x)
    col[0] = s
    col[1] = x
    col[2] = d
    col[3] = 1.0 + s + 0.5 * (s * s + x * x_mate + d * d * near)
    col[4] = x + 0.5 * x * (s + s_mate)
    col[5] = d + 0.5 * d * (s + s_fore)
    col[6] = d + 0.5 * d * (s + s_back)
    col[7] = 0.5 * d * d
    col[8] = 0.5 * (x * other_d + d * x_fore)
    col[9] = 0.5 * (x * other_d + d * x_back)
    ab = a * b
    same, cross = STEP * (jnp.where(even, 2.0 * a, 0.0) + 2.0 * ab), STEP * (-2.0 * ab)
    col[10] = jnp.where(even, same, cross)
    col[11] = jnp.where(even, cross, same)

    load(0).wait()
    load(panels - 1).wait()
    lane8 = iota((8, LANES), 1)
    sub8 = iota((8, LANES), 0)
    lane16 = iota((16, LANES), 1)
    for side, panel, start in ((0, 1, 0), (1, panels, LANES - 4)):
        packed = jnp.zeros((16, LANES), F32)
        for g in range(groups):
            piece = vx[panel, PAD + 16 * g : PAD + 16 * g + 16, :]
            turn = (4 * g - start) % LANES
            piece = pltpu.roll(piece, turn, 1) if turn else piece
            packed = jnp.where((lane16 >= 4 * g) & (lane16 < 4 * g + 4), piece, packed)
        send_col[side] = packed

    small[4].wait()
    small[5].wait()
    for k in range(panels // 2):
        one, two = (slice(LANES * (2 * k + t), LANES * (2 * k + t + 1)) for t in (0, 1))
        send_row[0, 8 * k : 8 * k + 8, :] = jnp.where(sub8 < 4, edge[0, :, one], pltpu.roll(edge[0, :, two], 4, 0))
        send_row[1, 8 * k : 8 * k + 8, :] = jnp.where(sub8 < 4, pltpu.roll(edge[1, :, one], 4, 0), edge[1, :, two])

    tile_rows = 4 * panels

    def landing(i):
        dr, dc = SIDES[i]
        if dc == 0:
            return got_row.at[0 if dr > 0 else 1]
        if dr == 0:
            return got_col.at[0 if dc > 0 else 1]
        return got_corner.at[(2 if dr < 0 else 0) + (1 if dc < 0 else 0)]

    def remote(i):
        dr, dc = SIDES[i]
        if dc == 0:
            source = send_row.at[0 if dr < 0 else 1]
        elif dr == 0:
            source = send_col.at[0 if dc < 0 else 1]
        else:
            source = edge.at[0 if dr < 0 else 1, :, pl.ds(0 if dc < 0 else (panels - 1) * LANES, LANES)]
        return pltpu.make_async_remote_copy(
            src_ref=source, dst_ref=landing(i), send_sem=send_sem.at[i], recv_sem=recv_sem.at[i],
            device_id=(row + dr, cols_at + dc), device_id_type=MESH,
        )

    def send():
        pl.semaphore_wait(barrier, count)
        each_side(lambda dr, dc: remote(SIDES.index((dr, dc))).start())

    at16 = iota((16, LANES), 1)
    in16 = iota((16, LANES), 0)
    owner = (at16 + 4) // 32, (at16 + 20) // 32
    codes = [
        (16 * tile + in16 - at16) * (1 - 2 * (at16 % 2)) for tile in (2 * owner[0], 2 * owner[1] - 1)
    ]
    wide_at = iota((16, 2 * LANES), 1) % LANES
    wide_owner = (wide_at + 4) // 32, (wide_at + 20) // 32
    blank = jnp.zeros((16, 2 * LANES), BF16)

    def weights(p, _):
        c = [jnp.broadcast_to(col[i, pl.ds(p, 1), :], (16, LANES)) for i in range(10)]
        none = jnp.zeros((16, LANES), F32)
        pairs = []
        for k in codes:
            z = k == 0, k == 1, k == 2, k == -2
            u = jnp.where(jnp.abs(k) == 4, c[7], none)
            u = jnp.where(k == 3, c[8], u)
            u = jnp.where(k == -1, c[9], u)
            u = jnp.where(z[0], c[3], jnp.where(z[1], c[4], jnp.where(z[2], c[5], jnp.where(z[3], c[6], u))))
            w = jnp.where(z[0], c[0], jnp.where(z[1], c[1], jnp.where(z[2] | z[3], c[2], none)))
            pairs.append(split(jnp.concatenate([u, w], axis=1)))

        def tile(i, part):
            odd = i % 2
            return jnp.where(wide_owner[odd] == (i + odd) // 2, pairs[odd][part], blank)

        for i in range(8):
            whi[p, 16 * i : 16 * i + 16, :] = tile(i, 0)
            wlo[p, 16 * i : 16 * i + 16, :] = tile(i, 1)
        before, after = [tile(-1, part) for part in (0, 1)], [tile(8, part) for part in (0, 1)]
        for i, value in enumerate((after[0], before[0], after[0], before[1], after[1], blank, blank, before[0])):
            wlo[p, LANES + 16 * i : LANES + 16 * i + 16, :] = value
        return 0

    lax.fori_loop(0, panels, weights, 0)

    def split_panel(p):
        for g in range(groups):
            e = vx[p, pl.ds(PAD + 16 * g, 8, stride=2), :]
            o = vx[p, pl.ds(PAD + 16 * g + 1, 8, stride=2), :]
            hi, lo = split(jnp.concatenate([e, o], axis=0))
            high[p, 16 * g : 16 * g + 16, :] = hi
            low[p, 16 * g : 16 * g + 16, :] = lo

    split_panel(1)
    split_panel(panels)

    def next_panel(p, _):
        load(p - 1).wait()
        split_panel(p)
        return 0

    lax.fori_loop(2, panels, next_panel, 0)
    odd = cols_at % 2 == 1
    pl.when(jnp.logical_not(distant | odd))(send)

    at_rows = iota((rows, LANES), 1)
    next_lanes = at_rows < LANES // 2
    low_lanes = (at_rows >= 16) & (at_rows < 48)
    again_lanes = (at_rows >= 48) & (at_rows < 80)

    def columns(p, w_ref):
        hi, lo = high[p], low[p]
        edge_hi = jnp.where(next_lanes, high[p + 1], high[p - 1])
        edge_lo = jnp.where(next_lanes, low[p + 1], low[p - 1])
        edges = jnp.where(
            low_lanes, pltpu.roll(edge_lo, 32, 1), jnp.where(again_lanes, pltpu.roll(edge_hi, 64, 1), edge_hi)
        )
        lhs = jnp.concatenate([hi, lo, hi, edges], axis=1)
        rhs = jnp.concatenate([whi[p - 1], whi[p - 1], wlo[p - 1]], axis=0)
        both = jnp.dot(lhs, rhs, preferred_element_type=F32)
        w_ref[...] = both
        u_edge[p - 1, 0:16, :] = both[0:16, :LANES]
        u_edge[p - 1, 16:32, :] = both[rows - 16 :, :LANES]

    def own_rows(p, w_ref):
        for g in range(groups):
            at = PAD + 16 * g
            e, o = vx[p, pl.ds(at, 8, stride=2), :], vx[p, pl.ds(at + 1, 8, stride=2), :]
            e_sum = vx[p, pl.ds(at - 2, 8, stride=2), :] + vx[p, pl.ds(at + 2, 8, stride=2), :]
            o_sum = vx[p, pl.ds(at - 1, 8, stride=2), :] + vx[p, pl.ds(at + 3, 8, stride=2), :]
            c = [half[n, 8 * g : 8 * g + 8, :] for n in range(4)]
            ge[p - 1, PAD + 8 * g : PAD + 8 * g + 8, :] = (
                e + w_ref[16 * g : 16 * g + 8, LANES:] + ((c[0] * e + c[2] * o) + (0.5 * d0) * e_sum)
            )
            go[p - 1, PAD + 8 * g : PAD + 8 * g + 8, :] = (
                o + w_ref[16 * g + 8 : 16 * g + 16, LANES:] + ((c[1] * o + c[3] * e) + (0.5 * d1) * o_sum)
            )
        for g in range(1, groups - 1):
            at = PAD + 8 * g
            e, o = ge[p - 1, at : at + 8, :], go[p - 1, at : at + 8, :]
            e_sum = ge[p - 1, at - 1 : at + 7, :] + ge[p - 1, at + 1 : at + 9, :]
            o_sum = go[p - 1, at - 1 : at + 7, :] + go[p - 1, at + 1 : at + 9, :]
            c = [full[n, 8 * g : 8 * g + 8, :] for n in range(4)]
            stage[p - 1, pl.ds(16 * g, 8, stride=2), :] = (
                w_ref[16 * g : 16 * g + 8, :LANES] + ((c[0] * e + c[2] * o) + d0 * e_sum)
            )
            stage[p - 1, pl.ds(16 * g + 1, 8, stride=2), :] = (
                w_ref[16 * g + 8 : 16 * g + 16, :LANES] + ((c[1] * o + c[3] * e) + d1 * o_sum)
            )

    columns(2, w_one)

    steps = (panels - 4) // 2
    early = 1

    def middle(i, _):
        pl.when((distant | odd) & (i == early))(send)
        p = 3 + 2 * i
        own_rows(p - 1, w_one)
        columns(p, w_two)
        own_rows(p, w_two)
        columns(p + 1, w_one)
        return 0

    lax.fori_loop(0, steps, middle, 0)
    own_rows(panels - 2, w_one)
    columns(panels - 1, w_two)

    def wait_recv(dr, dc):
        @pl.when(there(-dr, -dc))
        def _():
            remote(SIDES.index((dr, dc))).wait_recv()

    wait_recv(0, 1)
    wait_recv(0, -1)
    for side, panel, start in ((0, 0, LANES - 4), (1, panels + 1, 0)):
        packed = got_col[side]
        for g in range(groups):
            turn = (start - 4 * g) % LANES
            vx[panel, PAD + 16 * g : PAD + 16 * g + 16, :] = pltpu.roll(packed, turn, 1) if turn else packed
        split_panel(panel)

    own_rows(panels - 1, w_two)
    columns(1, w_one)
    own_rows(1, w_one)
    columns(panels, w_two)
    own_rows(panels, w_two)

    per_panel = LANES // 16
    even_lane = lane8 % 2 == 0

    def add_noise(g, t, move):
        c = [col[i, pl.ds(t, 1), :] for i in (0, 1, 2, 10, 11)]
        here = slice(8 * g, 8 * g + 8)
        f = [full[i, here, :] for i in range(4)]
        n_e, n_o, n_x = (noise[i, here, :] for i in range(3))
        gap = (move * (LANES // 2) + lane8 // 2) - (8 * (g % per_panel) + sub8)
        on, beside = gap == 0, jnp.abs(gap) == 1
        for odd, s_r, x_r, d_r, one, two, mine, mate in (
            (0, f[0], f[2], d0, c[3], c[4], jnp.where(even_lane, n_e, n_x), jnp.where(even_lane, n_x, n_e)),
            (1, f[1], f[3], d1, c[4], c[3], jnp.where(even_lane, n_x, n_o), jnp.where(even_lane, n_o, n_x)),
        ):
            centre = mine + 0.5 * ((s_r * one + x_r * two) + (c[0] * mine + c[1] * mate))
            side = 0.5 * (d_r * one + c[2] * mine)
            value = jnp.where(on, centre, jnp.where(beside, side, 0.0))
            if g in (0, groups - 1):
                at = 8 * odd + (16 if g else 0)
                u_edge[t, at : at + 8, :] += value
            else:
                stage[t, pl.ds(16 * g + odd, 8, stride=2), :] += value

    ratio = panels * LANES // rows
    first_panel = (row - cols_at * ratio) * (rows // LANES)

    @pl.when((first_panel >= 0) & (first_panel < panels))
    def _():
        for g in range(groups):
            t = first_panel + g // per_panel
            add_noise(g, t, 0)
            if g % per_panel == 0 and g:
                add_noise(g, t - 1, -1)
            if g % per_panel == per_panel - 1 and g < groups - 1:
                add_noise(g, t + 1, 1)

    @pl.when((first_panel >= 1) & (first_panel <= panels))
    def _():
        add_noise(0, first_panel - 1, -1)

    @pl.when((first_panel + rows // LANES >= 0) & (first_panel + rows // LANES < panels))
    def _():
        add_noise(groups - 1, first_panel + rows // LANES, 1)

    upper = sub8 < 4
    species = sub8 % 2 == 0
    for k in range(panels // 2):
        here = slice(8 * k, 8 * k + 8)
        one, two = 2 * k + 1, 2 * k + 2
        e = PAD + rows
        inner[0, here, :] = jnp.where(upper, vx[one, PAD - 2 : PAD + 6, :], vx[two, PAD - 6 : PAD + 2, :])
        inner[1, here, :] = jnp.where(upper, vx[one, e - 2 : e + 6, :], vx[two, e - 6 : e + 2, :])
        for i in range(3):
            halo_col[i, here, :] = jnp.where(upper, col[i, 2 * k : 2 * k + 1, :], col[i, 2 * k + 1 : 2 * k + 2, :])
    for side in (0, 1):
        voxel = jnp.clip(row * half_rows + (-1 if side == 0 else half_rows), 0, voxels - 1)
        pick = lane8 * 0 + voxel % LANES
        a = jnp.broadcast_to(feed_of[pl.ds(voxel // LANES, 1), :], (8, LANES))
        b = jnp.broadcast_to(conv_of[pl.ds(voxel // LANES, 1), :], (8, LANES))
        a = jnp.sum(jnp.where(lane8 == pick, a, 0.0), axis=1, keepdims=True)
        b = jnp.sum(jnp.where(lane8 == pick, b, 0.0), axis=1, keepdims=True)
        end = (voxel == 0) | (voxel == voxels - 1)
        near = jnp.where(end, 1.0, 2.0)
        d_r = jnp.where(species, d0, d1)
        halo_row[side, 0] = jnp.broadcast_to(STEP * jnp.where(species, b - 1.0, -a * a) - d_r * near, (8, LANES))
        halo_row[side, 1] = jnp.broadcast_to(STEP * jnp.where(species, a * a, -b), (8, LANES))
        halo_row[side, 2] = jnp.broadcast_to(d_r, (8, LANES))
        ok = there(-1, 0) if side == 0 else there(1, 0)
        halo_row[side, 3] = jnp.full((8, LANES), ok.astype(F32))

    for i, (dr, dc) in enumerate(SIDES):
        @pl.when(there(dr, dc))
        def _(i=i):
            remote(i).wait_send()

    for dr, dc in SIDES:
        if dr:
            wait_recv(dr, dc)


def finish_kernel(
    rows, panels,
    stage, u_edge, ge, go, full, spread, got_row, got_corner, inner, halo_col, halo_row,
    out, halo, tile_g, near_g, ends, wide, sem,
):
    d0, d1 = spread[0], spread[1]
    groups = rows // 16
    half_rows = rows // 2

    def store(p):
        return pltpu.make_async_copy(
            stage.at[p, pl.ds(16, rows - 32), :],
            out.at[pl.ds(16, rows - 32), pl.ds(p * LANES, LANES)],
            sem.at[p],
        )

    def store_end(side):
        return pltpu.make_async_copy(
            wide.at[side], out.at[pl.ds(side * (rows - 16), 16), :], sem.at[panels + side]
        )

    for p in range(panels):
        store(p).start()

    tile_rows = 4 * panels
    for side in (0, 1):
        left, right = got_corner[2 * side], got_corner[2 * side + 1]
        halo[side, 8 : 8 + tile_rows, :] = got_row[side]
        halo[side, 0:8, :] = left if side == 0 else pltpu.roll(left, 4, 0)
        halo[side, 8 + tile_rows : 16 + tile_rows, :] = pltpu.roll(right, 4, 0) if side == 0 else right

    lane8 = iota((8, LANES), 1)
    sub8 = iota((8, LANES), 0)
    even8 = lane8 % 2 == 0
    species = sub8 % 2 == 0
    for side in (0, 1):
        s_r, x_r, d_r = halo_row[side, 0], halo_row[side, 1], halo_row[side, 2]
        ok = halo_row[side, 3] > 0.5
        for k in range(panels // 2):
            at = 8 + 8 * k
            here = slice(8 * k, 8 * k + 8)
            tile, left, right = (halo[side, at + t : at + t + 8, :] for t in (0, -4, 4))
            mate = jnp.where(even8, pltpu.roll(tile, LANES - 1, 1), pltpu.roll(tile, 1, 1))
            beside = pltpu.roll(jnp.where(lane8 >= LANES - 2, left, tile), 2, 1) + pltpu.roll(
                jnp.where(lane8 < 2, right, tile), LANES - 2, 1
            )
            w = halo_col[0, here, :] * tile + halo_col[1, here, :] * mate + halo_col[2, here, :] * beside
            row_mate = jnp.where(species, halo[side, at + 1 : at + 9, :], halo[side, at - 1 : at + 7, :])
            away = halo[side, at - 2 : at + 6, :] if side == 0 else halo[side, at + 2 : at + 10, :]
            g = tile + w + 0.5 * (s_r * tile + x_r * row_mate + d_r * (away + inner[side, here, :]))
            tile_g[side, at : at + 8, :] = jnp.where(ok, g, 0.0)

        first = 0 if side == 0 else half_rows - 8
        c = [full[i, first : first + 8, :] for i in range(4)]
        for p in range(panels):
            at = 8 + 8 * (p // 2) + 4 * (p % 2)
            for o, ref, dd in ((0, ge, d0), (1, go, d1)):
                mine = ref[p, PAD + first : PAD + first + 8, :]
                if side == 0:
                    fix = halo[side, at + 2 + o : at + 10 + o, :]
                    near_g[o, 0:8, :] = tile_g[side, at + o - 5 : at + o + 3, :]
                    near_g[o, 16:24, :] = ref[p, PAD + 8 : PAD + 16, :]
                else:
                    fix = halo[side, at + o - 7 : at + o + 1, :]
                    near_g[o, 0:8, :] = ref[p, PAD + first - 8 : PAD + first, :]
                    near_g[o, 16:24, :] = tile_g[side, at + o : at + o + 8, :]
                fix = jnp.where(ok & (sub8 == (0 if side == 0 else 7)), (0.5 * dd) * fix, 0.0)
                near_g[o, 8:16, :] = mine + fix
            e, o = near_g[0, 8:16, :], near_g[1, 8:16, :]
            e_sum = near_g[0, 7:15, :] + near_g[0, 9:17, :]
            o_sum = near_g[1, 7:15, :] + near_g[1, 9:17, :]
            u = 16 * side
            ends[p, pl.ds(0, 8, stride=2), :] = u_edge[p, u : u + 8, :] + ((c[0] * e + c[2] * o) + d0 * e_sum)
            ends[p, pl.ds(1, 8, stride=2), :] = u_edge[p, u + 8 : u + 16, :] + ((c[1] * o + c[3] * e) + d1 * o_sum)
            wide[side, :, LANES * p : LANES * p + LANES] = ends[p]
        store_end(side).start()

    for p in range(panels):
        store(p).wait()
    for side in (0, 1):
        store_end(side).wait()


def body(covariance, classes, feed_rate, conversion_rate, diffusion):
    rows, cols = covariance.shape
    panels = cols // LANES
    voxels = classes.shape[0]
    half_rows = rows // 2
    vmem = pl.BlockSpec(memory_space=pltpu.VMEM)
    hbm = pl.BlockSpec(memory_space=pl.ANY)
    sizes = (lax.axis_size("row"), lax.axis_size("col"))
    inputs = (covariance, classes.reshape(voxels // LANES, LANES), feed_rate, conversion_rate, diffusion)
    results = pl.pallas_call(
        functools.partial(advance_kernel, rows, panels, voxels, *sizes),
        out_shape=[
            pltpu.VMEM((panels, rows, LANES), F32),
            pltpu.VMEM((panels, 32, LANES), F32),
            pltpu.VMEM((panels, half_rows + 2 * PAD, LANES), F32),
            pltpu.VMEM((panels, half_rows + 2 * PAD, LANES), F32),
            pltpu.VMEM((4, half_rows, LANES), F32),
            pltpu.VMEM((2, 8, LANES), F32),
            pltpu.VMEM((2, 4 * panels, LANES), F32),
            pltpu.VMEM((4, 8, LANES), F32),
            pltpu.VMEM((2, 4 * panels, LANES), F32),
            pltpu.VMEM((3, 4 * panels, LANES), F32),
            pltpu.VMEM((2, 4, 8, LANES), F32),
        ],
        in_specs=[hbm] * 5,
        out_specs=[vmem] * 11,
        scratch_shapes=[
            pltpu.VMEM((panels + 2, rows + 2 * PAD, LANES), F32),
            pltpu.VMEM((panels + 2, rows, LANES), BF16),
            pltpu.VMEM((panels + 2, rows, LANES), BF16),
            pltpu.VMEM((panels, LANES, 2 * LANES), BF16),
            pltpu.VMEM((panels, 2 * LANES, 2 * LANES), BF16),
            pltpu.VMEM((rows, 2 * LANES), F32),
            pltpu.VMEM((rows, 2 * LANES), F32),
            pltpu.VMEM((4, half_rows, LANES), F32),
            pltpu.VMEM((3, half_rows, LANES), F32),
            pltpu.VMEM((voxels // LANES, LANES), F32),
            pltpu.VMEM((voxels // LANES, LANES), F32),
            pltpu.VMEM((panels + 16, LANES), F32),
            pltpu.VMEM((panels + 16, LANES), F32),
            pltpu.VMEM((panels + 16, LANES), F32),
            pltpu.VMEM((panels + 16, LANES), F32),
            pltpu.VMEM((12, panels, LANES), F32),
            pltpu.VMEM((voxels // LANES, LANES), jnp.int32),
            pltpu.SMEM(feed_rate.shape, F32),
            pltpu.SMEM(conversion_rate.shape, F32),
            pltpu.SMEM(diffusion.shape, F32),
            pltpu.VMEM((2, 8, cols), F32),
            pltpu.VMEM((2, 4 * panels, LANES), F32),
            pltpu.VMEM((2, 16, LANES), F32),
            pltpu.VMEM((2, 16, LANES), F32),
            pltpu.SemaphoreType.DMA((panels,)),
            pltpu.SemaphoreType.DMA((6,)),
            pltpu.SemaphoreType.DMA((8,)),
            pltpu.SemaphoreType.DMA((8,)),
        ],
        compiler_params=pltpu.CompilerParams(
            collective_id=0, has_side_effects=True, vmem_limit_bytes=32 << 20
        ),
        name="halo_and_columns",
    )(*(pltpu.with_memory_space_constraint(x, pltpu.HBM) for x in inputs))
    return pl.pallas_call(
        functools.partial(finish_kernel, rows, panels),
        out_shape=jax.ShapeDtypeStruct((rows, cols), F32),
        in_specs=[vmem] * 11,
        out_specs=hbm,
        scratch_shapes=[
            pltpu.VMEM((2, 4 * panels + 16, LANES), F32),
            pltpu.VMEM((2, 4 * panels + 16, LANES), F32),
            pltpu.VMEM((2, 24, LANES), F32),
            pltpu.VMEM((panels, 16, LANES), F32),
            pltpu.VMEM((2, 16, cols), F32),
            pltpu.SemaphoreType.DMA((panels + 2,)),
        ],
        compiler_params=pltpu.CompilerParams(vmem_limit_bytes=24 << 20),
        name="rows",
    )(*results)


def solution(mesh):
    in_specs = (P("row", "col"), P(), P(), P(), P())
    return jax.shard_map(body, mesh=mesh, in_specs=in_specs, out_specs=P("row", "col"), check_vma=False)
```

```python
import functools

import jax
import jax.numpy as jnp
from jax import lax
from jax.experimental import pallas as pl
from jax.experimental.pallas import tpu as pltpu
from jax.sharding import PartitionSpec as P

STEP = 0.04
LANES = 128
PAD = 8
F32, BF16 = jnp.float32, jnp.bfloat16
MESH = pl.DeviceIdType.MESH
SIDES = [(dr, dc) for dr in (-1, 0, 1) for dc in (-1, 0, 1) if (dr, dc) != (0, 0)]


def split(value):
    high = value.astype(BF16)
    return high, (value - high.astype(F32)).astype(BF16)


def iota(shape, dim):
    return lax.broadcasted_iota(jnp.int32, shape, dim)


def advance_kernel(
    rows, panels, voxels, grid_rows, grid_cols,
    cov, classes_in, feed_in, conv_in, diff_in,
    stage, u_edge, ge, go, full, spread, got_row, got_corner, inner, halo_col, halo_row,
    vx, high, low, whi, wlo, w_one, w_two, half, noise, feed_of, conv_of, ext_s, ext_x, ext_a, ext_b, col,
    classes, feed, conv, diff, edge, send_row, send_col, got_col,
    load_sem, small_sem, send_sem, recv_sem,
):
    row, cols_at = lax.axis_index("row"), lax.axis_index("col")
    groups = rows // 16
    half_rows = rows // 2
    def there(dr, dc):
        ok = None
        for at, step, size in ((row, dr, grid_rows), (cols_at, dc, grid_cols)):
            if step:
                one = (at + step >= 0) & (at + step < size)
                ok = one if ok is None else ok & one
        return ok

    barrier = pltpu.get_barrier_semaphore()
    count = jnp.int32(0)
    across = {1: row == grid_rows // 2 - 1, -1: row == grid_rows // 2}
    distant = across[1] | across[-1]

    def each_side(act):
        for dr in (1, -1):
            @pl.when(across[dr])
            def _(dr=dr):
                for dc in (-1, 0, 1):
                    pl.when(there(dr, dc))(lambda dc=dc: act(dr, dc))
        for dr, dc in SIDES:
            ok = there(dr, dc)
            pl.when(ok & jnp.logical_not(across[dr]) if dr else ok)(lambda dr=dr, dc=dc: act(dr, dc))

    for dr, dc in SIDES:
        count += there(dr, dc).astype(jnp.int32)
    each_side(lambda dr, dc: pl.semaphore_signal(
        barrier, inc=1, device_id=(row + dr, cols_at + dc), device_id_type=MESH
    ))

    small = [
        pltpu.make_async_copy(a, b, small_sem.at[n])
        for n, (a, b) in enumerate((
            (classes_in, classes), (feed_in, feed), (conv_in, conv), (diff_in, diff),
            (cov.at[pl.ds(0, 8), :], edge.at[0]), (cov.at[pl.ds(rows - 8, 8), :], edge.at[1]),
        ))
    ]
    for copy in small:
        copy.start()
    def load(p):
        return pltpu.make_async_copy(
            cov.at[:, pl.ds(pl.multiple_of(p * LANES, LANES), LANES)],
            vx.at[p + 1, pl.ds(PAD, rows), :],
            load_sem.at[p],
        )

    load(0).start()
    load(panels - 1).start()

    def start_load(p, _):
        load(p).start()
        return 0

    lax.fori_loop(1, panels - 1, start_load, 0)

    zero = jnp.zeros((8, LANES), F32)
    for p in range(panels):
        vx[p + 1, 0:PAD, :] = zero
        vx[p + 1, PAD + rows : 2 * PAD + rows, :] = zero
    for i, at in enumerate((0, grid_cols - 1)):
        @pl.when(cols_at == at)
        def _(i=i):
            got_col[i] = jnp.zeros(got_col.shape[1:], F32)
            got_corner[i] = zero
            got_corner[2 + i] = zero

    for copy in small[:4]:
        copy.wait()
    d0, d1 = diff[0] * STEP, diff[1] * STEP
    spread[0] = jnp.full((8, LANES), d0, F32)
    spread[1] = jnp.full((8, LANES), d1, F32)
    ids = classes[...]
    a_all, b_all = jnp.zeros(ids.shape, F32), jnp.zeros(ids.shape, F32)
    for k in range(feed.shape[0]):
        a_all = jnp.where(ids == k, feed[k], a_all)
        b_all = jnp.where(ids == k, conv[k], b_all)
    feed_of[...] = a_all
    conv_of[...] = b_all
    class_rows = voxels // LANES

    lane8 = iota((8, LANES), 1)
    row_at = row * (half_rows // LANES)
    for t in range(half_rows // LANES):
        a = jnp.broadcast_to(feed_of[pl.ds(row_at + t, 1), :], (LANES, LANES)).T
        b = jnp.broadcast_to(conv_of[pl.ds(row_at + t, 1), :], (LANES, LANES)).T
        voxel = row * half_rows + t * LANES + iota((LANES, LANES), 0)
        near = 2.0 - (voxel == 0).astype(F32) - (voxel == voxels - 1).astype(F32)
        here = pl.ds(t * LANES, LANES)
        a2, ab = a * a, a * b
        values = (
            STEP * (b - 1.0) - d0 * near, -STEP * a2 - d1 * near, STEP * a2, -STEP * b,
        )
        for i, value in enumerate(values):
            full[i, here, :] = value
            half[i, here, :] = 0.5 * value
        noise[0, here, :] = STEP * (2.0 * a + 2.0 * ab)
        noise[1, here, :] = STEP * (2.0 * ab)
        noise[2, here, :] = STEP * (-2.0 * ab)

    first = cols_at * (panels // 2)
    lane = iota((panels // 2, LANES), 1)
    for t in range(2):
        pick = lane // 2 + (LANES // 2) * t
        for source, target in ((feed_of, ext_a), (conv_of, ext_b)):
            value = source[pl.ds(pl.multiple_of(first, panels // 2), panels // 2), :]
            target[pl.ds(8 + t, panels // 2, stride=2), :] = jnp.take_along_axis(value, pick, axis=1)
    before, after = jnp.maximum(first - 1, 0), jnp.minimum(first + panels // 2, class_rows - 1)
    for source, target in ((feed_of, ext_a), (conv_of, ext_b)):
        value = jnp.broadcast_to(source[pl.ds(before, 1), :], (8, LANES))
        target[0:8, :] = jnp.take_along_axis(value, lane8 // 2 + LANES // 2, axis=1)
        value = jnp.broadcast_to(source[pl.ds(after, 1), :], (8, LANES))
        target[8 + panels : 16 + panels, :] = jnp.take_along_axis(value, lane8 // 2, axis=1)
    shape = ext_a.shape
    lane_e = iota(shape, 1)
    even_e = lane_e % 2 == 0
    a, b = ext_a[...], ext_b[...]
    voxel = cols_at * (panels * LANES // 2) + (iota(shape, 0) - 8) * (LANES // 2) + lane_e // 2
    near = 2.0 - (voxel == 0).astype(F32) - (voxel == voxels - 1).astype(F32)
    d_e = jnp.where(even_e, d0, d1)
    ext_s[...] = STEP * jnp.where(even_e, b - 1.0, -a * a) - d_e * near
    ext_x[...] = STEP * jnp.where(even_e, a * a, -b)

    mid = slice(8, 8 + panels)
    lane = iota((panels, LANES), 1)
    even = lane % 2 == 0
    near, a, b = near[mid], a[mid], b[mid]
    d = jnp.where(even, d0, d1)
    other_d = jnp.where(even, d1, d0)

    def shifted(ref):
        here = ref[mid, :]
        left = pltpu.roll(jnp.where(lane >= LANES - 2, ref[7 : 7 + panels, :], here), 2, 1)
        right = pltpu.roll(jnp.where(lane < 2, ref[9 : 9 + panels, :], here), LANES - 2, 1)
        mate = jnp.where(even, pltpu.roll(here, LANES - 1, 1), pltpu.roll(here, 1, 1))
        return here, mate, jnp.where(even, right, left), jnp.where(even, left, right)

    s, s_mate, s_fore, s_back = shifted(ext_s)
    x, x_mate, x_fore, x_back = shifted(ext_x)
    col[0] = s
    col[1] = x
    col[2] = d
    col[3] = 1.0 + s + 0.5 * (s * s + x * x_mate + d * d * near)
    col[4] = x + 0.5 * x * (s + s_mate)
    col[5] = d + 0.5 * d * (s + s_fore)
    col[6] = d + 0.5 * d * (s + s_back)
    col[7] = 0.5 * d * d
    col[8] = 0.5 * (x * other_d + d * x_fore)
    col[9] = 0.5 * (x * other_d + d * x_back)
    ab = a * b
    same, cross = STEP * (jnp.where(even, 2.0 * a, 0.0) + 2.0 * ab), STEP * (-2.0 * ab)
    col[10] = jnp.where(even, same, cross)
    col[11] = jnp.where(even, cross, same)

    load(0).wait()
    load(panels - 1).wait()
    lane8 = iota((8, LANES), 1)
    sub8 = iota((8, LANES), 0)
    lane16 = iota((16, LANES), 1)
    for side, panel, start in ((0, 1, 0), (1, panels, LANES - 4)):
        packed = jnp.zeros((16, LANES), F32)
        for g in range(groups):
            piece = vx[panel, PAD + 16 * g : PAD + 16 * g + 16, :]
            turn = (4 * g - start) % LANES
            piece = pltpu.roll(piece, turn, 1) if turn else piece
            packed = jnp.where((lane16 >= 4 * g) & (lane16 < 4 * g + 4), piece, packed)
        send_col[side] = packed

    small[4].wait()
    small[5].wait()
    for k in range(panels // 2):
        one, two = (slice(LANES * (2 * k + t), LANES * (2 * k + t + 1)) for t in (0, 1))
        send_row[0, 8 * k : 8 * k + 8, :] = jnp.where(sub8 < 4, edge[0, :, one], pltpu.roll(edge[0, :, two], 4, 0))
        send_row[1, 8 * k : 8 * k + 8, :] = jnp.where(sub8 < 4, pltpu.roll(edge[1, :, one], 4, 0), edge[1, :, two])

    tile_rows = 4 * panels

    def landing(i):
        dr, dc = SIDES[i]
        if dc == 0:
            return got_row.at[0 if dr > 0 else 1]
        if dr == 0:
            return got_col.at[0 if dc > 0 else 1]
        return got_corner.at[(2 if dr < 0 else 0) + (1 if dc < 0 else 0)]

    def remote(i):
        dr, dc = SIDES[i]
        if dc == 0:
            source = send_row.at[0 if dr < 0 else 1]
        elif dr == 0:
            source = send_col.at[0 if dc < 0 else 1]
        else:
            source = edge.at[0 if dr < 0 else 1, :, pl.ds(0 if dc < 0 else (panels - 1) * LANES, LANES)]
        return pltpu.make_async_remote_copy(
            src_ref=source, dst_ref=landing(i), send_sem=send_sem.at[i], recv_sem=recv_sem.at[i],
            device_id=(row + dr, cols_at + dc), device_id_type=MESH,
        )

    def send():
        pl.semaphore_wait(barrier, count)
        each_side(lambda dr, dc: remote(SIDES.index((dr, dc))).start())

    at16 = iota((16, LANES), 1)
    in16 = iota((16, LANES), 0)
    owner = (at16 + 4) // 32, (at16 + 20) // 32
    codes = [
        (16 * tile + in16 - at16) * (1 - 2 * (at16 % 2)) for tile in (2 * owner[0], 2 * owner[1] - 1)
    ]
    wide_at = iota((16, 2 * LANES), 1) % LANES
    wide_owner = (wide_at + 4) // 32, (wide_at + 20) // 32
    blank = jnp.zeros((16, 2 * LANES), BF16)

    def weights(p, _):
        c = [jnp.broadcast_to(col[i, pl.ds(p, 1), :], (16, LANES)) for i in range(10)]
        none = jnp.zeros((16, LANES), F32)
        pairs = []
        for k in codes:
            z = k == 0, k == 1, k == 2, k == -2
            u = jnp.where(jnp.abs(k) == 4, c[7], none)
            u = jnp.where(k == 3, c[8], u)
            u = jnp.where(k == -1, c[9], u)
            u = jnp.where(z[0], c[3], jnp.where(z[1], c[4], jnp.where(z[2], c[5], jnp.where(z[3], c[6], u))))
            w = jnp.where(z[0], c[0], jnp.where(z[1], c[1], jnp.where(z[2] | z[3], c[2], none)))
            pairs.append(split(jnp.concatenate([u, w], axis=1)))

        def tile(i, part):
            odd = i % 2
            return jnp.where(wide_owner[odd] == (i + odd) // 2, pairs[odd][part], blank)

        for i in range(8):
            whi[p, 16 * i : 16 * i + 16, :] = tile(i, 0)
            wlo[p, 16 * i : 16 * i + 16, :] = tile(i, 1)
        before, after = [tile(-1, part) for part in (0, 1)], [tile(8, part) for part in (0, 1)]
        for i, value in enumerate((after[0], before[0], after[0], before[1], after[1], blank, blank, before[0])):
            wlo[p, LANES + 16 * i : LANES + 16 * i + 16, :] = value
        return 0

    lax.fori_loop(0, panels, weights, 0)

    def split_panel(p):
        for g in range(groups):
            e = vx[p, pl.ds(PAD + 16 * g, 8, stride=2), :]
            o = vx[p, pl.ds(PAD + 16 * g + 1, 8, stride=2), :]
            hi, lo = split(jnp.concatenate([e, o], axis=0))
            high[p, 16 * g : 16 * g + 16, :] = hi
            low[p, 16 * g : 16 * g + 16, :] = lo

    split_panel(1)
    split_panel(panels)

    def next_panel(p, _):
        load(p - 1).wait()
        split_panel(p)
        return 0

    lax.fori_loop(2, panels, next_panel, 0)
    odd = cols_at % 2 == 1
    pl.when(jnp.logical_not(distant | odd))(send)

    at_rows = iota((rows, LANES), 1)
    next_lanes = at_rows < LANES // 2
    low_lanes = (at_rows >= 16) & (at_rows < 48)
    again_lanes = (at_rows >= 48) & (at_rows < 80)

    def columns(p, w_ref):
        hi, lo = high[p], low[p]
        edge_hi = jnp.where(next_lanes, high[p + 1], high[p - 1])
        edge_lo = jnp.where(next_lanes, low[p + 1], low[p - 1])
        edges = jnp.where(
            low_lanes, pltpu.roll(edge_lo, 32, 1), jnp.where(again_lanes, pltpu.roll(edge_hi, 64, 1), edge_hi)
        )
        lhs = jnp.concatenate([hi, lo, hi, edges], axis=1)
        rhs = jnp.concatenate([whi[p - 1], whi[p - 1], wlo[p - 1]], axis=0)
        both = jnp.dot(lhs, rhs, preferred_element_type=F32)
        w_ref[...] = both
        u_edge[p - 1, 0:16, :] = both[0:16, :LANES]
        u_edge[p - 1, 16:32, :] = both[rows - 16 :, :LANES]

    def own_rows(p, w_ref):
        for g in range(groups):
            at = PAD + 16 * g
            e, o = vx[p, pl.ds(at, 8, stride=2), :], vx[p, pl.ds(at + 1, 8, stride=2), :]
            e_sum = vx[p, pl.ds(at - 2, 8, stride=2), :] + vx[p, pl.ds(at + 2, 8, stride=2), :]
            o_sum = vx[p, pl.ds(at - 1, 8, stride=2), :] + vx[p, pl.ds(at + 3, 8, stride=2), :]
            c = [half[n, 8 * g : 8 * g + 8, :] for n in range(4)]
            ge[p - 1, PAD + 8 * g : PAD + 8 * g + 8, :] = (
                e + w_ref[16 * g : 16 * g + 8, LANES:] + ((c[0] * e + c[2] * o) + (0.5 * d0) * e_sum)
            )
            go[p - 1, PAD + 8 * g : PAD + 8 * g + 8, :] = (
                o + w_ref[16 * g + 8 : 16 * g + 16, LANES:] + ((c[1] * o + c[3] * e) + (0.5 * d1) * o_sum)
            )
        for g in range(1, groups - 1):
            at = PAD + 8 * g
            e, o = ge[p - 1, at : at + 8, :], go[p - 1, at : at + 8, :]
            e_sum = ge[p - 1, at - 1 : at + 7, :] + ge[p - 1, at + 1 : at + 9, :]
            o_sum = go[p - 1, at - 1 : at + 7, :] + go[p - 1, at + 1 : at + 9, :]
            c = [full[n, 8 * g : 8 * g + 8, :] for n in range(4)]
            stage[p - 1, pl.ds(16 * g, 8, stride=2), :] = (
                w_ref[16 * g : 16 * g + 8, :LANES] + ((c[0] * e + c[2] * o) + d0 * e_sum)
            )
            stage[p - 1, pl.ds(16 * g + 1, 8, stride=2), :] = (
                w_ref[16 * g + 8 : 16 * g + 16, :LANES] + ((c[1] * o + c[3] * e) + d1 * o_sum)
            )

    columns(2, w_one)

    steps = (panels - 4) // 2
    early = 1

    def middle(i, _):
        pl.when((distant | odd) & (i == early))(send)
        p = 3 + 2 * i
        own_rows(p - 1, w_one)
        columns(p, w_two)
        own_rows(p, w_two)
        columns(p + 1, w_one)
        return 0

    lax.fori_loop(0, steps, middle, 0)
    own_rows(panels - 2, w_one)
    columns(panels - 1, w_two)

    def wait_recv(dr, dc):
        @pl.when(there(-dr, -dc))
        def _():
            remote(SIDES.index((dr, dc))).wait_recv()

    wait_recv(0, 1)
    wait_recv(0, -1)
    for side, panel, start in ((0, 0, LANES - 4), (1, panels + 1, 0)):
        packed = got_col[side]
        for g in range(groups):
            turn = (start - 4 * g) % LANES
            vx[panel, PAD + 16 * g : PAD + 16 * g + 16, :] = pltpu.roll(packed, turn, 1) if turn else packed
        split_panel(panel)

    own_rows(panels - 1, w_two)
    columns(1, w_one)
    own_rows(1, w_one)
    columns(panels, w_two)
    own_rows(panels, w_two)

    per_panel = LANES // 16
    even_lane = lane8 % 2 == 0

    def add_noise(g, t, move):
        c = [col[i, pl.ds(t, 1), :] for i in (0, 1, 2, 10, 11)]
        here = slice(8 * g, 8 * g + 8)
        f = [full[i, here, :] for i in range(4)]
        n_e, n_o, n_x = (noise[i, here, :] for i in range(3))
        gap = (move * (LANES // 2) + lane8 // 2) - (8 * (g % per_panel) + sub8)
        on, beside = gap == 0, jnp.abs(gap) == 1
        for odd, s_r, x_r, d_r, one, two, mine, mate in (
            (0, f[0], f[2], d0, c[3], c[4], jnp.where(even_lane, n_e, n_x), jnp.where(even_lane, n_x, n_e)),
            (1, f[1], f[3], d1, c[4], c[3], jnp.where(even_lane, n_x, n_o), jnp.where(even_lane, n_o, n_x)),
        ):
            centre = mine + 0.5 * ((s_r * one + x_r * two) + (c[0] * mine + c[1] * mate))
            side = 0.5 * (d_r * one + c[2] * mine)
            value = jnp.where(on, centre, jnp.where(beside, side, 0.0))
            if g in (0, groups - 1):
                at = 8 * odd + (16 if g else 0)
                u_edge[t, at : at + 8, :] += value
            else:
                stage[t, pl.ds(16 * g + odd, 8, stride=2), :] += value

    ratio = panels * LANES // rows
    first_panel = (row - cols_at * ratio) * (rows // LANES)

    @pl.when((first_panel >= 0) & (first_panel < panels))
    def _():
        for g in range(groups):
            t = first_panel + g // per_panel
            add_noise(g, t, 0)
            if g % per_panel == 0 and g:
                add_noise(g, t - 1, -1)
            if g % per_panel == per_panel - 1 and g < groups - 1:
                add_noise(g, t + 1, 1)

    @pl.when((first_panel >= 1) & (first_panel <= panels))
    def _():
        add_noise(0, first_panel - 1, -1)

    @pl.when((first_panel + rows // LANES >= 0) & (first_panel + rows // LANES < panels))
    def _():
        add_noise(groups - 1, first_panel + rows // LANES, 1)

    upper = sub8 < 4
    species = sub8 % 2 == 0
    for k in range(panels // 2):
        here = slice(8 * k, 8 * k + 8)
        one, two = 2 * k + 1, 2 * k + 2
        e = PAD + rows
        inner[0, here, :] = jnp.where(upper, vx[one, PAD - 2 : PAD + 6, :], vx[two, PAD - 6 : PAD + 2, :])
        inner[1, here, :] = jnp.where(upper, vx[one, e - 2 : e + 6, :], vx[two, e - 6 : e + 2, :])
        for i in range(3):
            halo_col[i, here, :] = jnp.where(upper, col[i, 2 * k : 2 * k + 1, :], col[i, 2 * k + 1 : 2 * k + 2, :])
    for side in (0, 1):
        voxel = jnp.clip(row * half_rows + (-1 if side == 0 else half_rows), 0, voxels - 1)
        pick = lane8 * 0 + voxel % LANES
        a = jnp.broadcast_to(feed_of[pl.ds(voxel // LANES, 1), :], (8, LANES))
        b = jnp.broadcast_to(conv_of[pl.ds(voxel // LANES, 1), :], (8, LANES))
        a = jnp.sum(jnp.where(lane8 == pick, a, 0.0), axis=1, keepdims=True)
        b = jnp.sum(jnp.where(lane8 == pick, b, 0.0), axis=1, keepdims=True)
        end = (voxel == 0) | (voxel == voxels - 1)
        near = jnp.where(end, 1.0, 2.0)
        d_r = jnp.where(species, d0, d1)
        halo_row[side, 0] = jnp.broadcast_to(STEP * jnp.where(species, b - 1.0, -a * a) - d_r * near, (8, LANES))
        halo_row[side, 1] = jnp.broadcast_to(STEP * jnp.where(species, a * a, -b), (8, LANES))
        halo_row[side, 2] = jnp.broadcast_to(d_r, (8, LANES))
        ok = there(-1, 0) if side == 0 else there(1, 0)
        halo_row[side, 3] = jnp.full((8, LANES), ok.astype(F32))

    for i, (dr, dc) in enumerate(SIDES):
        @pl.when(there(dr, dc))
        def _(i=i):
            remote(i).wait_send()

    for dr, dc in SIDES:
        if dr:
            wait_recv(dr, dc)


def finish_kernel(
    rows, panels,
    stage, u_edge, ge, go, full, spread, got_row, got_corner, inner, halo_col, halo_row,
    out, halo, tile_g, near_g, ends, wide, sem,
):
    d0, d1 = spread[0], spread[1]
    groups = rows // 16
    half_rows = rows // 2

    def store(p):
        return pltpu.make_async_copy(
            stage.at[p, pl.ds(16, rows - 32), :],
            out.at[pl.ds(16, rows - 32), pl.ds(p * LANES, LANES)],
            sem.at[p],
        )

    def store_end(side):
        return pltpu.make_async_copy(
            wide.at[side], out.at[pl.ds(side * (rows - 16), 16), :], sem.at[panels + side]
        )

    for p in range(panels):
        store(p).start()

    tile_rows = 4 * panels
    for side in (0, 1):
        left, right = got_corner[2 * side], got_corner[2 * side + 1]
        halo[side, 8 : 8 + tile_rows, :] = got_row[side]
        halo[side, 0:8, :] = left if side == 0 else pltpu.roll(left, 4, 0)
        halo[side, 8 + tile_rows : 16 + tile_rows, :] = pltpu.roll(right, 4, 0) if side == 0 else right

    lane8 = iota((8, LANES), 1)
    sub8 = iota((8, LANES), 0)
    even8 = lane8 % 2 == 0
    species = sub8 % 2 == 0
    for side in (0, 1):
        s_r, x_r, d_r = halo_row[side, 0], halo_row[side, 1], halo_row[side, 2]
        ok = halo_row[side, 3] > 0.5
        for k in range(panels // 2):
            at = 8 + 8 * k
            here = slice(8 * k, 8 * k + 8)
            tile, left, right = (halo[side, at + t : at + t + 8, :] for t in (0, -4, 4))
            mate = jnp.where(even8, pltpu.roll(tile, LANES - 1, 1), pltpu.roll(tile, 1, 1))
            beside = pltpu.roll(jnp.where(lane8 >= LANES - 2, left, tile), 2, 1) + pltpu.roll(
                jnp.where(lane8 < 2, right, tile), LANES - 2, 1
            )
            w = halo_col[0, here, :] * tile + halo_col[1, here, :] * mate + halo_col[2, here, :] * beside
            row_mate = jnp.where(species, halo[side, at + 1 : at + 9, :], halo[side, at - 1 : at + 7, :])
            away = halo[side, at - 2 : at + 6, :] if side == 0 else halo[side, at + 2 : at + 10, :]
            g = tile + w + 0.5 * (s_r * tile + x_r * row_mate + d_r * (away + inner[side, here, :]))
            tile_g[side, at : at + 8, :] = jnp.where(ok, g, 0.0)

        first = 0 if side == 0 else half_rows - 8
        c = [full[i, first : first + 8, :] for i in range(4)]
        for p in range(panels):
            at = 8 + 8 * (p // 2) + 4 * (p % 2)
            for o, ref, dd in ((0, ge, d0), (1, go, d1)):
                mine = ref[p, PAD + first : PAD + first + 8, :]
                if side == 0:
                    fix = halo[side, at + 2 + o : at + 10 + o, :]
                    near_g[o, 0:8, :] = tile_g[side, at + o - 5 : at + o + 3, :]
                    near_g[o, 16:24, :] = ref[p, PAD + 8 : PAD + 16, :]
                else:
                    fix = halo[side, at + o - 7 : at + o + 1, :]
                    near_g[o, 0:8, :] = ref[p, PAD + first - 8 : PAD + first, :]
                    near_g[o, 16:24, :] = tile_g[side, at + o : at + o + 8, :]
                fix = jnp.where(ok & (sub8 == (0 if side == 0 else 7)), (0.5 * dd) * fix, 0.0)
                near_g[o, 8:16, :] = mine + fix
            e, o = near_g[0, 8:16, :], near_g[1, 8:16, :]
            e_sum = near_g[0, 7:15, :] + near_g[0, 9:17, :]
            o_sum = near_g[1, 7:15, :] + near_g[1, 9:17, :]
            u = 16 * side
            ends[p, pl.ds(0, 8, stride=2), :] = u_edge[p, u : u + 8, :] + ((c[0] * e + c[2] * o) + d0 * e_sum)
            ends[p, pl.ds(1, 8, stride=2), :] = u_edge[p, u + 8 : u + 16, :] + ((c[1] * o + c[3] * e) + d1 * o_sum)
            wide[side, :, LANES * p : LANES * p + LANES] = ends[p, 0:16, :]
        store_end(side).start()

    for p in range(panels):
        store(p).wait()
    for side in (0, 1):
        store_end(side).wait()


def body(covariance, classes, feed_rate, conversion_rate, diffusion):
    rows, cols = covariance.shape
    panels = cols // LANES
    voxels = classes.shape[0]
    half_rows = rows // 2
    vmem = pl.BlockSpec(memory_space=pltpu.VMEM)
    hbm = pl.BlockSpec(memory_space=pl.ANY)
    sizes = (lax.axis_size("row"), lax.axis_size("col"))
    inputs = (covariance, classes.reshape(voxels // LANES, LANES), feed_rate, conversion_rate, diffusion)
    results = pl.pallas_call(
        functools.partial(advance_kernel, rows, panels, voxels, *sizes),
        out_shape=[
            pltpu.VMEM((panels, rows, LANES), F32),
            pltpu.VMEM((panels, 32, LANES), F32),
            pltpu.VMEM((panels, half_rows + 2 * PAD, LANES), F32),
            pltpu.VMEM((panels, half_rows + 2 * PAD, LANES), F32),
            pltpu.VMEM((4, half_rows, LANES), F32),
            pltpu.VMEM((2, 8, LANES), F32),
            pltpu.VMEM((2, 4 * panels, LANES), F32),
            pltpu.VMEM((4, 8, LANES), F32),
            pltpu.VMEM((2, 4 * panels, LANES), F32),
            pltpu.VMEM((3, 4 * panels, LANES), F32),
            pltpu.VMEM((2, 4, 8, LANES), F32),
        ],
        in_specs=[hbm] * 5,
        out_specs=[vmem] * 11,
        scratch_shapes=[
            pltpu.VMEM((panels + 2, rows + 2 * PAD, LANES), F32),
            pltpu.VMEM((panels + 2, rows, LANES), BF16),
            pltpu.VMEM((panels + 2, rows, LANES), BF16),
            pltpu.VMEM((panels, LANES, 2 * LANES), BF16),
            pltpu.VMEM((panels, 2 * LANES, 2 * LANES), BF16),
            pltpu.VMEM((rows, 2 * LANES), F32),
            pltpu.VMEM((rows, 2 * LANES), F32),
            pltpu.VMEM((4, half_rows, LANES), F32),
            pltpu.VMEM((3, half_rows, LANES), F32),
            pltpu.VMEM((voxels // LANES, LANES), F32),
            pltpu.VMEM((voxels // LANES, LANES), F32),
            pltpu.VMEM((panels + 16, LANES), F32),
            pltpu.VMEM((panels + 16, LANES), F32),
            pltpu.VMEM((panels + 16, LANES), F32),
            pltpu.VMEM((panels + 16, LANES), F32),
            pltpu.VMEM((12, panels, LANES), F32),
            pltpu.VMEM((voxels // LANES, LANES), jnp.int32),
            pltpu.SMEM(feed_rate.shape, F32),
            pltpu.SMEM(conversion_rate.shape, F32),
            pltpu.SMEM(diffusion.shape, F32),
            pltpu.VMEM((2, 8, cols), F32),
            pltpu.VMEM((2, 4 * panels, LANES), F32),
            pltpu.VMEM((2, 16, LANES), F32),
            pltpu.VMEM((2, 16, LANES), F32),
            pltpu.SemaphoreType.DMA((panels,)),
            pltpu.SemaphoreType.DMA((6,)),
            pltpu.SemaphoreType.DMA((8,)),
            pltpu.SemaphoreType.DMA((8,)),
        ],
        compiler_params=pltpu.CompilerParams(
            collective_id=0, has_side_effects=True, vmem_limit_bytes=32 << 20
        ),
        name="halo_and_columns",
    )(*(pltpu.with_memory_space_constraint(x, pltpu.HBM) for x in inputs))
    return pl.pallas_call(
        functools.partial(finish_kernel, rows, panels),
        out_shape=jax.ShapeDtypeStruct((rows, cols), F32),
        in_specs=[vmem] * 11,
        out_specs=hbm,
        scratch_shapes=[
            pltpu.VMEM((2, 4 * panels + 16, LANES), F32),
            pltpu.VMEM((2, 4 * panels + 16, LANES), F32),
            pltpu.VMEM((2, 24, LANES), F32),
            pltpu.VMEM((panels, 24, LANES), F32),
            pltpu.VMEM((2, 16, cols), F32),
            pltpu.SemaphoreType.DMA((panels + 2,)),
        ],
        compiler_params=pltpu.CompilerParams(vmem_limit_bytes=24 << 20),
        name="rows",
    )(*results)


def solution(mesh):
    in_specs = (P("row", "col"), P(), P(), P(), P())
    return jax.shard_map(body, mesh=mesh, in_specs=in_specs, out_specs=P("row", "col"), check_vma=False)
```

```python
import functools

import jax
import jax.numpy as jnp
from jax import lax
from jax.experimental import pallas as pl
from jax.experimental.pallas import tpu as pltpu
from jax.sharding import PartitionSpec as P

STEP = 0.04
LANES = 128
PAD = 8
F32, BF16 = jnp.float32, jnp.bfloat16
MESH = pl.DeviceIdType.MESH
SIDES = [(dr, dc) for dr in (-1, 0, 1) for dc in (-1, 0, 1) if (dr, dc) != (0, 0)]


def split(value):
    high = value.astype(BF16)
    return high, (value - high.astype(F32)).astype(BF16)


def iota(shape, dim):
    return lax.broadcasted_iota(jnp.int32, shape, dim)


def advance_kernel(
    rows, panels, voxels, grid_rows, grid_cols,
    cov, classes_in, feed_in, conv_in, diff_in,
    stage, u_edge, ge, go, full, spread, got_row, got_corner, inner, halo_col, halo_row,
    vx, high, low, whi, wlo, w_one, w_two, half, noise, feed_of, conv_of, ext_s, ext_x, ext_a, ext_b, col,
    classes, feed, conv, diff, edge, send_row, send_col, got_col,
    load_sem, small_sem, send_sem, recv_sem,
):
    row, cols_at = lax.axis_index("row"), lax.axis_index("col")
    groups = rows // 16
    half_rows = rows // 2
    def there(dr, dc):
        ok = None
        for at, step, size in ((row, dr, grid_rows), (cols_at, dc, grid_cols)):
            if step:
                one = (at + step >= 0) & (at + step < size)
                ok = one if ok is None else ok & one
        return ok

    barrier = pltpu.get_barrier_semaphore()
    count = jnp.int32(0)
    across = {1: row == grid_rows // 2 - 1, -1: row == grid_rows // 2}
    distant = across[1] | across[-1]

    def each_side(act):
        for dr in (1, -1):
            @pl.when(across[dr])
            def _(dr=dr):
                for dc in (-1, 0, 1):
                    pl.when(there(dr, dc))(lambda dc=dc: act(dr, dc))
        for dr, dc in SIDES:
            ok = there(dr, dc)
            pl.when(ok & jnp.logical_not(across[dr]) if dr else ok)(lambda dr=dr, dc=dc: act(dr, dc))

    for dr, dc in SIDES:
        count += there(dr, dc).astype(jnp.int32)
    each_side(lambda dr, dc: pl.semaphore_signal(
        barrier, inc=1, device_id=(row + dr, cols_at + dc), device_id_type=MESH
    ))

    small = [
        pltpu.make_async_copy(a, b, small_sem.at[n])
        for n, (a, b) in enumerate((
            (classes_in, classes), (feed_in, feed), (conv_in, conv), (diff_in, diff),
            (cov.at[pl.ds(0, 8), :], edge.at[0]), (cov.at[pl.ds(rows - 8, 8), :], edge.at[1]),
        ))
    ]
    for copy in small:
        copy.start()
    def load(p):
        return pltpu.make_async_copy(
            cov.at[:, pl.ds(pl.multiple_of(p * LANES, LANES), LANES)],
            vx.at[p + 1, pl.ds(PAD, rows), :],
            load_sem.at[p],
        )

    load(0).start()
    load(panels - 1).start()

    def start_load(p, _):
        load(p).start()
        return 0

    lax.fori_loop(1, panels - 1, start_load, 0)

    zero = jnp.zeros((8, LANES), F32)
    for p in range(panels):
        vx[p + 1, 0:PAD, :] = zero
        vx[p + 1, PAD + rows : 2 * PAD + rows, :] = zero
    for i, at in enumerate((0, grid_cols - 1)):
        @pl.when(cols_at == at)
        def _(i=i):
            got_col[i] = jnp.zeros(got_col.shape[1:], F32)
            got_corner[i] = zero
            got_corner[2 + i] = zero

    for copy in small[:4]:
        copy.wait()
    d0, d1 = diff[0] * STEP, diff[1] * STEP
    spread[0] = jnp.full((8, LANES), d0, F32)
    spread[1] = jnp.full((8, LANES), d1, F32)
    ids = classes[...]
    a_all, b_all = jnp.zeros(ids.shape, F32), jnp.zeros(ids.shape, F32)
    for k in range(feed.shape[0]):
        a_all = jnp.where(ids == k, feed[k], a_all)
        b_all = jnp.where(ids == k, conv[k], b_all)
    feed_of[...] = a_all
    conv_of[...] = b_all
    class_rows = voxels // LANES

    lane8 = iota((8, LANES), 1)
    row_at = row * (half_rows // LANES)
    for t in range(half_rows // LANES):
        a = jnp.broadcast_to(feed_of[pl.ds(row_at + t, 1), :], (LANES, LANES)).T
        b = jnp.broadcast_to(conv_of[pl.ds(row_at + t, 1), :], (LANES, LANES)).T
        voxel = row * half_rows + t * LANES + iota((LANES, LANES), 0)
        near = 2.0 - (voxel == 0).astype(F32) - (voxel == voxels - 1).astype(F32)
        here = pl.ds(t * LANES, LANES)
        a2, ab = a * a, a * b
        values = (
            STEP * (b - 1.0) - d0 * near, -STEP * a2 - d1 * near, STEP * a2, -STEP * b,
        )
        for i, value in enumerate(values):
            full[i, here, :] = value
            half[i, here, :] = 0.5 * value
        noise[0, here, :] = STEP * (2.0 * a + 2.0 * ab)
        noise[1, here, :] = STEP * (2.0 * ab)
        noise[2, here, :] = STEP * (-2.0 * ab)

    first = cols_at * (panels // 2)
    lane = iota((panels // 2, LANES), 1)
    for t in range(2):
        pick = lane // 2 + (LANES // 2) * t
        for source, target in ((feed_of, ext_a), (conv_of, ext_b)):
            value = source[pl.ds(pl.multiple_of(first, panels // 2), panels // 2), :]
            target[pl.ds(8 + t, panels // 2, stride=2), :] = jnp.take_along_axis(value, pick, axis=1)
    before, after = jnp.maximum(first - 1, 0), jnp.minimum(first + panels // 2, class_rows - 1)
    for source, target in ((feed_of, ext_a), (conv_of, ext_b)):
        value = jnp.broadcast_to(source[pl.ds(before, 1), :], (8, LANES))
        target[0:8, :] = jnp.take_along_axis(value, lane8 // 2 + LANES // 2, axis=1)
        value = jnp.broadcast_to(source[pl.ds(after, 1), :], (8, LANES))
        target[8 + panels : 16 + panels, :] = jnp.take_along_axis(value, lane8 // 2, axis=1)
    shape = ext_a.shape
    lane_e = iota(shape, 1)
    even_e = lane_e % 2 == 0
    a, b = ext_a[...], ext_b[...]
    voxel = cols_at * (panels * LANES // 2) + (iota(shape, 0) - 8) * (LANES // 2) + lane_e // 2
    near = 2.0 - (voxel == 0).astype(F32) - (voxel == voxels - 1).astype(F32)
    d_e = jnp.where(even_e, d0, d1)
    ext_s[...] = STEP * jnp.where(even_e, b - 1.0, -a * a) - d_e * near
    ext_x[...] = STEP * jnp.where(even_e, a * a, -b)

    mid = slice(8, 8 + panels)
    lane = iota((panels, LANES), 1)
    even = lane % 2 == 0
    near, a, b = near[mid], a[mid], b[mid]
    d = jnp.where(even, d0, d1)
    other_d = jnp.where(even, d1, d0)

    def shifted(ref):
        here = ref[mid, :]
        left = pltpu.roll(jnp.where(lane >= LANES - 2, ref[7 : 7 + panels, :], here), 2, 1)
        right = pltpu.roll(jnp.where(lane < 2, ref[9 : 9 + panels, :], here), LANES - 2, 1)
        mate = jnp.where(even, pltpu.roll(here, LANES - 1, 1), pltpu.roll(here, 1, 1))
        return here, mate, jnp.where(even, right, left), jnp.where(even, left, right)

    s, s_mate, s_fore, s_back = shifted(ext_s)
    x, x_mate, x_fore, x_back = shifted(ext_x)
    col[0] = s
    col[1] = x
    col[2] = d
    col[3] = 1.0 + s + 0.5 * (s * s + x * x_mate + d * d * near)
    col[4] = x + 0.5 * x * (s + s_mate)
    col[5] = d + 0.5 * d * (s + s_fore)
    col[6] = d + 0.5 * d * (s + s_back)
    col[7] = 0.5 * d * d
    col[8] = 0.5 * (x * other_d + d * x_fore)
    col[9] = 0.5 * (x * other_d + d * x_back)
    ab = a * b
    same, cross = STEP * (jnp.where(even, 2.0 * a, 0.0) + 2.0 * ab), STEP * (-2.0 * ab)
    col[10] = jnp.where(even, same, cross)
    col[11] = jnp.where(even, cross, same)

    load(0).wait()
    load(panels - 1).wait()
    lane8 = iota((8, LANES), 1)
    sub8 = iota((8, LANES), 0)
    lane16 = iota((16, LANES), 1)
    for side, panel, start in ((0, 1, 0), (1, panels, LANES - 4)):
        packed = jnp.zeros((16, LANES), F32)
        for g in range(groups):
            piece = vx[panel, PAD + 16 * g : PAD + 16 * g + 16, :]
            turn = (4 * g - start) % LANES
            piece = pltpu.roll(piece, turn, 1) if turn else piece
            packed = jnp.where((lane16 >= 4 * g) & (lane16 < 4 * g + 4), piece, packed)
        send_col[side] = packed

    small[4].wait()
    small[5].wait()
    for k in range(panels // 2):
        one, two = (slice(LANES * (2 * k + t), LANES * (2 * k + t + 1)) for t in (0, 1))
        send_row[0, 8 * k : 8 * k + 8, :] = jnp.where(sub8 < 4, edge[0, :, one], pltpu.roll(edge[0, :, two], 4, 0))
        send_row[1, 8 * k : 8 * k + 8, :] = jnp.where(sub8 < 4, pltpu.roll(edge[1, :, one], 4, 0), edge[1, :, two])

    tile_rows = 4 * panels

    def landing(i):
        dr, dc = SIDES[i]
        if dc == 0:
            return got_row.at[0 if dr > 0 else 1]
        if dr == 0:
            return got_col.at[0 if dc > 0 else 1]
        return got_corner.at[(2 if dr < 0 else 0) + (1 if dc < 0 else 0)]

    def remote(i):
        dr, dc = SIDES[i]
        if dc == 0:
            source = send_row.at[0 if dr < 0 else 1]
        elif dr == 0:
            source = send_col.at[0 if dc < 0 else 1]
        else:
            source = edge.at[0 if dr < 0 else 1, :, pl.ds(0 if dc < 0 else (panels - 1) * LANES, LANES)]
        return pltpu.make_async_remote_copy(
            src_ref=source, dst_ref=landing(i), send_sem=send_sem.at[i], recv_sem=recv_sem.at[i],
            device_id=(row + dr, cols_at + dc), device_id_type=MESH,
        )

    def send():
        pl.semaphore_wait(barrier, count)
        each_side(lambda dr, dc: remote(SIDES.index((dr, dc))).start())

    at16 = iota((16, LANES), 1)
    in16 = iota((16, LANES), 0)
    owner = (at16 + 4) // 32, (at16 + 20) // 32
    codes = [
        (16 * tile + in16 - at16) * (1 - 2 * (at16 % 2)) for tile in (2 * owner[0], 2 * owner[1] - 1)
    ]
    wide_at = iota((16, 2 * LANES), 1) % LANES
    wide_owner = (wide_at + 4) // 32, (wide_at + 20) // 32
    blank = jnp.zeros((16, 2 * LANES), BF16)

    def weights(p, _):
        c = [jnp.broadcast_to(col[i, pl.ds(p, 1), :], (16, LANES)) for i in range(10)]
        none = jnp.zeros((16, LANES), F32)
        pairs = []
        for k in codes:
            z = k == 0, k == 1, k == 2, k == -2
            u = jnp.where(jnp.abs(k) == 4, c[7], none)
            u = jnp.where(k == 3, c[8], u)
            u = jnp.where(k == -1, c[9], u)
            u = jnp.where(z[0], c[3], jnp.where(z[1], c[4], jnp.where(z[2], c[5], jnp.where(z[3], c[6], u))))
            w = jnp.where(z[0], c[0], jnp.where(z[1], c[1], jnp.where(z[2] | z[3], c[2], none)))
            pairs.append(split(jnp.concatenate([u, w], axis=1)))

        def tile(i, part):
            odd = i % 2
            return jnp.where(wide_owner[odd] == (i + odd) // 2, pairs[odd][part], blank)

        for i in range(8):
            whi[p, 16 * i : 16 * i + 16, :] = tile(i, 0)
            wlo[p, 16 * i : 16 * i + 16, :] = tile(i, 1)
        before, after = [tile(-1, part) for part in (0, 1)], [tile(8, part) for part in (0, 1)]
        for i, value in enumerate((after[0], before[0], after[0], before[1], after[1], blank, blank, before[0])):
            wlo[p, LANES + 16 * i : LANES + 16 * i + 16, :] = value
        return 0

    lax.fori_loop(0, panels, weights, 0)

    def split_panel(p):
        for g in range(groups):
            e = vx[p, pl.ds(PAD + 16 * g, 8, stride=2), :]
            o = vx[p, pl.ds(PAD + 16 * g + 1, 8, stride=2), :]
            hi, lo = split(jnp.concatenate([e, o], axis=0))
            high[p, 16 * g : 16 * g + 16, :] = hi
            low[p, 16 * g : 16 * g + 16, :] = lo

    split_panel(1)
    split_panel(panels)

    def next_panel(p, _):
        load(p - 1).wait()
        split_panel(p)
        return 0

    lax.fori_loop(2, panels, next_panel, 0)
    odd = cols_at % 2 == 1
    pl.when(jnp.logical_not(distant | odd))(send)

    at_rows = iota((rows, LANES), 1)
    next_lanes = at_rows < LANES // 2
    low_lanes = (at_rows >= 16) & (at_rows < 48)
    again_lanes = (at_rows >= 48) & (at_rows < 80)

    def columns(p, w_ref):
        hi, lo = high[p], low[p]
        edge_hi = jnp.where(next_lanes, high[p + 1], high[p - 1])
        edge_lo = jnp.where(next_lanes, low[p + 1], low[p - 1])
        edges = jnp.where(
            low_lanes, pltpu.roll(edge_lo, 32, 1), jnp.where(again_lanes, pltpu.roll(edge_hi, 64, 1), edge_hi)
        )
        lhs = jnp.concatenate([hi, lo, hi, edges], axis=1)
        rhs = jnp.concatenate([whi[p - 1], whi[p - 1], wlo[p - 1]], axis=0)
        both = jnp.dot(lhs, rhs, preferred_element_type=F32)
        w_ref[...] = both
        u_edge[p - 1, 0:16, :] = both[0:16, :LANES]
        u_edge[p - 1, 16:32, :] = both[rows - 16 :, :LANES]

    def own_rows(p, w_ref):
        for g in range(groups):
            at = PAD + 16 * g
            e, o = vx[p, pl.ds(at, 8, stride=2), :], vx[p, pl.ds(at + 1, 8, stride=2), :]
            e_sum = vx[p, pl.ds(at - 2, 8, stride=2), :] + vx[p, pl.ds(at + 2, 8, stride=2), :]
            o_sum = vx[p, pl.ds(at - 1, 8, stride=2), :] + vx[p, pl.ds(at + 3, 8, stride=2), :]
            c = [half[n, 8 * g : 8 * g + 8, :] for n in range(4)]
            ge[p - 1, PAD + 8 * g : PAD + 8 * g + 8, :] = (
                e + w_ref[16 * g : 16 * g + 8, LANES:] + ((c[0] * e + c[2] * o) + (0.5 * d0) * e_sum)
            )
            go[p - 1, PAD + 8 * g : PAD + 8 * g + 8, :] = (
                o + w_ref[16 * g + 8 : 16 * g + 16, LANES:] + ((c[1] * o + c[3] * e) + (0.5 * d1) * o_sum)
            )
        for g in range(1, groups - 1):
            at = PAD + 8 * g
            e, o = ge[p - 1, at : at + 8, :], go[p - 1, at : at + 8, :]
            e_sum = ge[p - 1, at - 1 : at + 7, :] + ge[p - 1, at + 1 : at + 9, :]
            o_sum = go[p - 1, at - 1 : at + 7, :] + go[p - 1, at + 1 : at + 9, :]
            c = [full[n, 8 * g : 8 * g + 8, :] for n in range(4)]
            stage[p - 1, pl.ds(16 * g, 8, stride=2), :] = (
                w_ref[16 * g : 16 * g + 8, :LANES] + ((c[0] * e + c[2] * o) + d0 * e_sum)
            )
            stage[p - 1, pl.ds(16 * g + 1, 8, stride=2), :] = (
                w_ref[16 * g + 8 : 16 * g + 16, :LANES] + ((c[1] * o + c[3] * e) + d1 * o_sum)
            )

    columns(2, w_one)

    steps = (panels - 4) // 2
    early = 1

    def middle(i, _):
        pl.when((distant | odd) & (i == early))(send)
        p = 3 + 2 * i
        own_rows(p - 1, w_one)
        columns(p, w_two)
        own_rows(p, w_two)
        columns(p + 1, w_one)
        return 0

    lax.fori_loop(0, steps, middle, 0)
    own_rows(panels - 2, w_one)
    columns(panels - 1, w_two)

    def wait_recv(dr, dc):
        @pl.when(there(-dr, -dc))
        def _():
            remote(SIDES.index((dr, dc))).wait_recv()

    wait_recv(0, 1)
    wait_recv(0, -1)
    for side, panel, start in ((0, 0, LANES - 4), (1, panels + 1, 0)):
        packed = got_col[side]
        for g in range(groups):
            turn = (start - 4 * g) % LANES
            vx[panel, PAD + 16 * g : PAD + 16 * g + 16, :] = pltpu.roll(packed, turn, 1) if turn else packed
        split_panel(panel)

    own_rows(panels - 1, w_two)
    columns(1, w_one)
    own_rows(1, w_one)
    columns(panels, w_two)
    own_rows(panels, w_two)

    for dr in (1, -1):
        @pl.when(jnp.logical_not(across[-dr]))
        def _(dr=dr):
            for dc in (0, 1, -1):
                wait_recv(dr, dc)

    per_panel = LANES // 16
    even_lane = lane8 % 2 == 0

    def add_noise(g, t, move):
        c = [col[i, pl.ds(t, 1), :] for i in (0, 1, 2, 10, 11)]
        here = slice(8 * g, 8 * g + 8)
        f = [full[i, here, :] for i in range(4)]
        n_e, n_o, n_x = (noise[i, here, :] for i in range(3))
        gap = (move * (LANES // 2) + lane8 // 2) - (8 * (g % per_panel) + sub8)
        on, beside = gap == 0, jnp.abs(gap) == 1
        for odd, s_r, x_r, d_r, one, two, mine, mate in (
            (0, f[0], f[2], d0, c[3], c[4], jnp.where(even_lane, n_e, n_x), jnp.where(even_lane, n_x, n_e)),
            (1, f[1], f[3], d1, c[4], c[3], jnp.where(even_lane, n_x, n_o), jnp.where(even_lane, n_o, n_x)),
        ):
            centre = mine + 0.5 * ((s_r * one + x_r * two) + (c[0] * mine + c[1] * mate))
            side = 0.5 * (d_r * one + c[2] * mine)
            value = jnp.where(on, centre, jnp.where(beside, side, 0.0))
            if g in (0, groups - 1):
                at = 8 * odd + (16 if g else 0)
                u_edge[t, at : at + 8, :] += value
            else:
                stage[t, pl.ds(16 * g + odd, 8, stride=2), :] += value

    ratio = panels * LANES // rows
    first_panel = (row - cols_at * ratio) * (rows // LANES)

    @pl.when((first_panel >= 0) & (first_panel < panels))
    def _():
        for g in range(groups):
            t = first_panel + g // per_panel
            add_noise(g, t, 0)
            if g % per_panel == 0 and g:
                add_noise(g, t - 1, -1)
            if g % per_panel == per_panel - 1 and g < groups - 1:
                add_noise(g, t + 1, 1)

    @pl.when((first_panel >= 1) & (first_panel <= panels))
    def _():
        add_noise(0, first_panel - 1, -1)

    @pl.when((first_panel + rows // LANES >= 0) & (first_panel + rows // LANES < panels))
    def _():
        add_noise(groups - 1, first_panel + rows // LANES, 1)

    upper = sub8 < 4
    species = sub8 % 2 == 0
    for k in range(panels // 2):
        here = slice(8 * k, 8 * k + 8)
        one, two = 2 * k + 1, 2 * k + 2
        e = PAD + rows
        inner[0, here, :] = jnp.where(upper, vx[one, PAD - 2 : PAD + 6, :], vx[two, PAD - 6 : PAD + 2, :])
        inner[1, here, :] = jnp.where(upper, vx[one, e - 2 : e + 6, :], vx[two, e - 6 : e + 2, :])
        for i in range(3):
            halo_col[i, here, :] = jnp.where(upper, col[i, 2 * k : 2 * k + 1, :], col[i, 2 * k + 1 : 2 * k + 2, :])
    for side in (0, 1):
        voxel = jnp.clip(row * half_rows + (-1 if side == 0 else half_rows), 0, voxels - 1)
        pick = lane8 * 0 + voxel % LANES
        a = jnp.broadcast_to(feed_of[pl.ds(voxel // LANES, 1), :], (8, LANES))
        b = jnp.broadcast_to(conv_of[pl.ds(voxel // LANES, 1), :], (8, LANES))
        a = jnp.sum(jnp.where(lane8 == pick, a, 0.0), axis=1, keepdims=True)
        b = jnp.sum(jnp.where(lane8 == pick, b, 0.0), axis=1, keepdims=True)
        end = (voxel == 0) | (voxel == voxels - 1)
        near = jnp.where(end, 1.0, 2.0)
        d_r = jnp.where(species, d0, d1)
        halo_row[side, 0] = jnp.broadcast_to(STEP * jnp.where(species, b - 1.0, -a * a) - d_r * near, (8, LANES))
        halo_row[side, 1] = jnp.broadcast_to(STEP * jnp.where(species, a * a, -b), (8, LANES))
        halo_row[side, 2] = jnp.broadcast_to(d_r, (8, LANES))
        ok = there(-1, 0) if side == 0 else there(1, 0)
        halo_row[side, 3] = jnp.full((8, LANES), ok.astype(F32))

    for i, (dr, dc) in enumerate(SIDES):
        @pl.when(there(dr, dc))
        def _(i=i):
            remote(i).wait_send()

    for dr in (1, -1):
        @pl.when(across[-dr])
        def _(dr=dr):
            for dc in (0, 1, -1):
                wait_recv(dr, dc)


def finish_kernel(
    rows, panels,
    stage, u_edge, ge, go, full, spread, got_row, got_corner, inner, halo_col, halo_row,
    out, halo, tile_g, near_g, ends, wide, sem,
):
    d0, d1 = spread[0], spread[1]
    groups = rows // 16
    half_rows = rows // 2

    def store(p):
        return pltpu.make_async_copy(
            stage.at[p, pl.ds(16, rows - 32), :],
            out.at[pl.ds(16, rows - 32), pl.ds(p * LANES, LANES)],
            sem.at[p],
        )

    def store_end(side):
        return pltpu.make_async_copy(
            wide.at[side], out.at[pl.ds(side * (rows - 16), 16), :], sem.at[panels + side]
        )

    for p in range(panels):
        store(p).start()

    tile_rows = 4 * panels
    for side in (0, 1):
        left, right = got_corner[2 * side], got_corner[2 * side + 1]
        halo[side, 8 : 8 + tile_rows, :] = got_row[side]
        halo[side, 0:8, :] = left if side == 0 else pltpu.roll(left, 4, 0)
        halo[side, 8 + tile_rows : 16 + tile_rows, :] = pltpu.roll(right, 4, 0) if side == 0 else right

    lane8 = iota((8, LANES), 1)
    sub8 = iota((8, LANES), 0)
    even8 = lane8 % 2 == 0
    species = sub8 % 2 == 0
    for side in (0, 1):
        s_r, x_r, d_r = halo_row[side, 0], halo_row[side, 1], halo_row[side, 2]
        ok = halo_row[side, 3] > 0.5
        for k in range(panels // 2):
            at = 8 + 8 * k
            here = slice(8 * k, 8 * k + 8)
            tile, left, right = (halo[side, at + t : at + t + 8, :] for t in (0, -4, 4))
            mate = jnp.where(even8, pltpu.roll(tile, LANES - 1, 1), pltpu.roll(tile, 1, 1))
            beside = pltpu.roll(jnp.where(lane8 >= LANES - 2, left, tile), 2, 1) + pltpu.roll(
                jnp.where(lane8 < 2, right, tile), LANES - 2, 1
            )
            w = halo_col[0, here, :] * tile + halo_col[1, here, :] * mate + halo_col[2, here, :] * beside
            row_mate = jnp.where(species, halo[side, at + 1 : at + 9, :], halo[side, at - 1 : at + 7, :])
            away = halo[side, at - 2 : at + 6, :] if side == 0 else halo[side, at + 2 : at + 10, :]
            g = tile + w + 0.5 * (s_r * tile + x_r * row_mate + d_r * (away + inner[side, here, :]))
            tile_g[side, at : at + 8, :] = jnp.where(ok, g, 0.0)

        first = 0 if side == 0 else half_rows - 8
        c = [full[i, first : first + 8, :] for i in range(4)]
        for p in range(panels):
            at = 8 + 8 * (p // 2) + 4 * (p % 2)
            for o, ref, dd in ((0, ge, d0), (1, go, d1)):
                mine = ref[p, PAD + first : PAD + first + 8, :]
                if side == 0:
                    fix = halo[side, at + 2 + o : at + 10 + o, :]
                    near_g[o, 0:8, :] = tile_g[side, at + o - 5 : at + o + 3, :]
                    near_g[o, 16:24, :] = ref[p, PAD + 8 : PAD + 16, :]
                else:
                    fix = halo[side, at + o - 7 : at + o + 1, :]
                    near_g[o, 0:8, :] = ref[p, PAD + first - 8 : PAD + first, :]
                    near_g[o, 16:24, :] = tile_g[side, at + o : at + o + 8, :]
                fix = jnp.where(ok & (sub8 == (0 if side == 0 else 7)), (0.5 * dd) * fix, 0.0)
                near_g[o, 8:16, :] = mine + fix
            e, o = near_g[0, 8:16, :], near_g[1, 8:16, :]
            e_sum = near_g[0, 7:15, :] + near_g[0, 9:17, :]
            o_sum = near_g[1, 7:15, :] + near_g[1, 9:17, :]
            u = 16 * side
            ends[p, pl.ds(0, 8, stride=2), :] = u_edge[p, u : u + 8, :] + ((c[0] * e + c[2] * o) + d0 * e_sum)
            ends[p, pl.ds(1, 8, stride=2), :] = u_edge[p, u + 8 : u + 16, :] + ((c[1] * o + c[3] * e) + d1 * o_sum)
            wide[side, :, LANES * p : LANES * p + LANES] = ends[p, 0:16, :]
        store_end(side).start()

    for p in range(panels):
        store(p).wait()
    for side in (0, 1):
        store_end(side).wait()


def body(covariance, classes, feed_rate, conversion_rate, diffusion):
    rows, cols = covariance.shape
    panels = cols // LANES
    voxels = classes.shape[0]
    half_rows = rows // 2
    vmem = pl.BlockSpec(memory_space=pltpu.VMEM)
    hbm = pl.BlockSpec(memory_space=pl.ANY)
    sizes = (lax.axis_size("row"), lax.axis_size("col"))
    inputs = (covariance, classes.reshape(voxels // LANES, LANES), feed_rate, conversion_rate, diffusion)
    results = pl.pallas_call(
        functools.partial(advance_kernel, rows, panels, voxels, *sizes),
        out_shape=[
            pltpu.VMEM((panels, rows, LANES), F32),
            pltpu.VMEM((panels, 32, LANES), F32),
            pltpu.VMEM((panels, half_rows + 2 * PAD, LANES), F32),
            pltpu.VMEM((panels, half_rows + 2 * PAD, LANES), F32),
            pltpu.VMEM((4, half_rows, LANES), F32),
            pltpu.VMEM((2, 8, LANES), F32),
            pltpu.VMEM((2, 4 * panels, LANES), F32),
            pltpu.VMEM((4, 8, LANES), F32),
            pltpu.VMEM((2, 4 * panels, LANES), F32),
            pltpu.VMEM((3, 4 * panels, LANES), F32),
            pltpu.VMEM((2, 4, 8, LANES), F32),
        ],
        in_specs=[hbm] * 5,
        out_specs=[vmem] * 11,
        scratch_shapes=[
            pltpu.VMEM((panels + 2, rows + 2 * PAD, LANES), F32),
            pltpu.VMEM((panels + 2, rows, LANES), BF16),
            pltpu.VMEM((panels + 2, rows, LANES), BF16),
            pltpu.VMEM((panels, LANES, 2 * LANES), BF16),
            pltpu.VMEM((panels, 2 * LANES, 2 * LANES), BF16),
            pltpu.VMEM((rows, 2 * LANES), F32),
            pltpu.VMEM((rows, 2 * LANES), F32),
            pltpu.VMEM((4, half_rows, LANES), F32),
            pltpu.VMEM((3, half_rows, LANES), F32),
            pltpu.VMEM((voxels // LANES, LANES), F32),
            pltpu.VMEM((voxels // LANES, LANES), F32),
            pltpu.VMEM((panels + 16, LANES), F32),
            pltpu.VMEM((panels + 16, LANES), F32),
            pltpu.VMEM((panels + 16, LANES), F32),
            pltpu.VMEM((panels + 16, LANES), F32),
            pltpu.VMEM((12, panels, LANES), F32),
            pltpu.VMEM((voxels // LANES, LANES), jnp.int32),
            pltpu.SMEM(feed_rate.shape, F32),
            pltpu.SMEM(conversion_rate.shape, F32),
            pltpu.SMEM(diffusion.shape, F32),
            pltpu.VMEM((2, 8, cols), F32),
            pltpu.VMEM((2, 4 * panels, LANES), F32),
            pltpu.VMEM((2, 16, LANES), F32),
            pltpu.VMEM((2, 16, LANES), F32),
            pltpu.SemaphoreType.DMA((panels,)),
            pltpu.SemaphoreType.DMA((6,)),
            pltpu.SemaphoreType.DMA((8,)),
            pltpu.SemaphoreType.DMA((8,)),
        ],
        compiler_params=pltpu.CompilerParams(
            collective_id=0, has_side_effects=True, vmem_limit_bytes=32 << 20
        ),
        name="halo_and_columns",
    )(*(pltpu.with_memory_space_constraint(x, pltpu.HBM) for x in inputs))
    return pl.pallas_call(
        functools.partial(finish_kernel, rows, panels),
        out_shape=jax.ShapeDtypeStruct((rows, cols), F32),
        in_specs=[vmem] * 11,
        out_specs=hbm,
        scratch_shapes=[
            pltpu.VMEM((2, 4 * panels + 16, LANES), F32),
            pltpu.VMEM((2, 4 * panels + 16, LANES), F32),
            pltpu.VMEM((2, 24, LANES), F32),
            pltpu.VMEM((panels, 24, LANES), F32),
            pltpu.VMEM((2, 16, cols), F32),
            pltpu.SemaphoreType.DMA((panels + 2,)),
        ],
        compiler_params=pltpu.CompilerParams(vmem_limit_bytes=24 << 20),
        name="rows",
    )(*results)


def solution(mesh):
    in_specs = (P("row", "col"), P(), P(), P(), P())
    return jax.shard_map(body, mesh=mesh, in_specs=in_specs, out_specs=P("row", "col"), check_vma=False)
```

```python
import functools

import jax
import jax.numpy as jnp
from jax import lax
from jax.experimental import pallas as pl
from jax.experimental.pallas import tpu as pltpu
from jax.sharding import PartitionSpec as P

STEP = 0.04
LANES = 128
PAD = 8
F32, BF16 = jnp.float32, jnp.bfloat16
MESH = pl.DeviceIdType.MESH
SIDES = [(dr, dc) for dr in (-1, 0, 1) for dc in (-1, 0, 1) if (dr, dc) != (0, 0)]


def split(value):
    high = value.astype(BF16)
    return high, (value - high.astype(F32)).astype(BF16)


def iota(shape, dim):
    return lax.broadcasted_iota(jnp.int32, shape, dim)


def advance_kernel(
    rows, panels, voxels, grid_rows, grid_cols,
    cov, classes_in, feed_in, conv_in, diff_in,
    stage, u_edge, ge, go, full, spread, got_row, got_corner, inner, halo_col, halo_row,
    vx, high, low, whi, wlo, w_one, w_two, half, noise, feed_of, conv_of, ext_s, ext_x, ext_a, ext_b, col,
    classes, feed, conv, diff, edge, send_row, send_col, got_col,
    load_sem, small_sem, send_sem, recv_sem,
):
    row, cols_at = lax.axis_index("row"), lax.axis_index("col")
    groups = rows // 16
    half_rows = rows // 2
    def there(dr, dc):
        ok = None
        for at, step, size in ((row, dr, grid_rows), (cols_at, dc, grid_cols)):
            if step:
                one = (at + step >= 0) & (at + step < size)
                ok = one if ok is None else ok & one
        return ok

    barrier = pltpu.get_barrier_semaphore()
    count = jnp.int32(0)
    across = {1: row == grid_rows // 2 - 1, -1: row == grid_rows // 2}
    distant = across[1] | across[-1]

    def each_side(act):
        for dr in (1, -1):
            @pl.when(across[dr])
            def _(dr=dr):
                for dc in (-1, 0, 1):
                    pl.when(there(dr, dc))(lambda dc=dc: act(dr, dc))
        for dr, dc in SIDES:
            ok = there(dr, dc)
            pl.when(ok & jnp.logical_not(across[dr]) if dr else ok)(lambda dr=dr, dc=dc: act(dr, dc))

    for dr, dc in SIDES:
        count += there(dr, dc).astype(jnp.int32)
    each_side(lambda dr, dc: pl.semaphore_signal(
        barrier, inc=1, device_id=(row + dr, cols_at + dc), device_id_type=MESH
    ))

    small = [
        pltpu.make_async_copy(a, b, small_sem.at[n])
        for n, (a, b) in enumerate((
            (classes_in, classes), (feed_in, feed), (conv_in, conv), (diff_in, diff),
            (cov.at[pl.ds(0, 8), :], edge.at[0]), (cov.at[pl.ds(rows - 8, 8), :], edge.at[1]),
        ))
    ]
    for copy in small:
        copy.start()
    def load(p):
        return pltpu.make_async_copy(
            cov.at[:, pl.ds(pl.multiple_of(p * LANES, LANES), LANES)],
            vx.at[p + 1, pl.ds(PAD, rows), :],
            load_sem.at[p],
        )

    load(0).start()
    load(panels - 1).start()

    def start_load(p, _):
        load(p).start()
        return 0

    lax.fori_loop(1, panels - 1, start_load, 0)

    zero = jnp.zeros((8, LANES), F32)
    for p in range(panels):
        vx[p + 1, 0:PAD, :] = zero
        vx[p + 1, PAD + rows : 2 * PAD + rows, :] = zero
    for i, at in enumerate((0, grid_cols - 1)):
        @pl.when(cols_at == at)
        def _(i=i):
            got_col[i] = jnp.zeros(got_col.shape[1:], F32)
            got_corner[i] = zero
            got_corner[2 + i] = zero

    for copy in small[:4]:
        copy.wait()
    d0, d1 = diff[0] * STEP, diff[1] * STEP
    spread[0] = jnp.full((8, LANES), d0, F32)
    spread[1] = jnp.full((8, LANES), d1, F32)
    ids = classes[...]
    a_all, b_all = jnp.zeros(ids.shape, F32), jnp.zeros(ids.shape, F32)
    for k in range(feed.shape[0]):
        a_all = jnp.where(ids == k, feed[k], a_all)
        b_all = jnp.where(ids == k, conv[k], b_all)
    feed_of[...] = a_all
    conv_of[...] = b_all
    class_rows = voxels // LANES

    lane8 = iota((8, LANES), 1)
    row_at = row * (half_rows // LANES)
    for t in range(half_rows // LANES):
        a = jnp.broadcast_to(feed_of[pl.ds(row_at + t, 1), :], (LANES, LANES)).T
        b = jnp.broadcast_to(conv_of[pl.ds(row_at + t, 1), :], (LANES, LANES)).T
        voxel = row * half_rows + t * LANES + iota((LANES, LANES), 0)
        near = 2.0 - (voxel == 0).astype(F32) - (voxel == voxels - 1).astype(F32)
        here = pl.ds(t * LANES, LANES)
        a2, ab = a * a, a * b
        values = (
            STEP * (b - 1.0) - d0 * near, -STEP * a2 - d1 * near, STEP * a2, -STEP * b,
        )
        for i, value in enumerate(values):
            full[i, here, :] = value
            half[i, here, :] = 0.5 * value
        noise[0, here, :] = STEP * (2.0 * a + 2.0 * ab)
        noise[1, here, :] = STEP * (2.0 * ab)
        noise[2, here, :] = STEP * (-2.0 * ab)

    first = cols_at * (panels // 2)
    lane = iota((panels // 2, LANES), 1)
    for t in range(2):
        pick = lane // 2 + (LANES // 2) * t
        for source, target in ((feed_of, ext_a), (conv_of, ext_b)):
            value = source[pl.ds(pl.multiple_of(first, panels // 2), panels // 2), :]
            target[pl.ds(8 + t, panels // 2, stride=2), :] = jnp.take_along_axis(value, pick, axis=1)
    before, after = jnp.maximum(first - 1, 0), jnp.minimum(first + panels // 2, class_rows - 1)
    for source, target in ((feed_of, ext_a), (conv_of, ext_b)):
        value = jnp.broadcast_to(source[pl.ds(before, 1), :], (8, LANES))
        target[0:8, :] = jnp.take_along_axis(value, lane8 // 2 + LANES // 2, axis=1)
        value = jnp.broadcast_to(source[pl.ds(after, 1), :], (8, LANES))
        target[8 + panels : 16 + panels, :] = jnp.take_along_axis(value, lane8 // 2, axis=1)
    shape = ext_a.shape
    lane_e = iota(shape, 1)
    even_e = lane_e % 2 == 0
    a, b = ext_a[...], ext_b[...]
    voxel = cols_at * (panels * LANES // 2) + (iota(shape, 0) - 8) * (LANES // 2) + lane_e // 2
    near = 2.0 - (voxel == 0).astype(F32) - (voxel == voxels - 1).astype(F32)
    d_e = jnp.where(even_e, d0, d1)
    ext_s[...] = STEP * jnp.where(even_e, b - 1.0, -a * a) - d_e * near
    ext_x[...] = STEP * jnp.where(even_e, a * a, -b)

    mid = slice(8, 8 + panels)
    lane = iota((panels, LANES), 1)
    even = lane % 2 == 0
    near, a, b = near[mid], a[mid], b[mid]
    d = jnp.where(even, d0, d1)
    other_d = jnp.where(even, d1, d0)

    def shifted(ref):
        here = ref[mid, :]
        left = pltpu.roll(jnp.where(lane >= LANES - 2, ref[7 : 7 + panels, :], here), 2, 1)
        right = pltpu.roll(jnp.where(lane < 2, ref[9 : 9 + panels, :], here), LANES - 2, 1)
        mate = jnp.where(even, pltpu.roll(here, LANES - 1, 1), pltpu.roll(here, 1, 1))
        return here, mate, jnp.where(even, right, left), jnp.where(even, left, right)

    s, s_mate, s_fore, s_back = shifted(ext_s)
    x, x_mate, x_fore, x_back = shifted(ext_x)
    col[0] = s
    col[1] = x
    col[2] = d
    col[3] = 1.0 + s + 0.5 * (s * s + x * x_mate + d * d * near)
    col[4] = x + 0.5 * x * (s + s_mate)
    col[5] = d + 0.5 * d * (s + s_fore)
    col[6] = d + 0.5 * d * (s + s_back)
    col[7] = 0.5 * d * d
    col[8] = 0.5 * (x * other_d + d * x_fore)
    col[9] = 0.5 * (x * other_d + d * x_back)
    ab = a * b
    same, cross = STEP * (jnp.where(even, 2.0 * a, 0.0) + 2.0 * ab), STEP * (-2.0 * ab)
    col[10] = jnp.where(even, same, cross)
    col[11] = jnp.where(even, cross, same)

    load(0).wait()
    load(panels - 1).wait()
    lane8 = iota((8, LANES), 1)
    sub8 = iota((8, LANES), 0)
    lane16 = iota((16, LANES), 1)
    for side, panel, start in ((0, 1, 0), (1, panels, LANES - 4)):
        packed = jnp.zeros((16, LANES), F32)
        for g in range(groups):
            piece = vx[panel, PAD + 16 * g : PAD + 16 * g + 16, :]
            turn = (4 * g - start) % LANES
            piece = pltpu.roll(piece, turn, 1) if turn else piece
            packed = jnp.where((lane16 >= 4 * g) & (lane16 < 4 * g + 4), piece, packed)
        send_col[side] = packed

    small[4].wait()
    small[5].wait()
    for k in range(panels // 2):
        one, two = (slice(LANES * (2 * k + t), LANES * (2 * k + t + 1)) for t in (0, 1))
        send_row[0, 8 * k : 8 * k + 8, :] = jnp.where(sub8 < 4, edge[0, :, one], pltpu.roll(edge[0, :, two], 4, 0))
        send_row[1, 8 * k : 8 * k + 8, :] = jnp.where(sub8 < 4, pltpu.roll(edge[1, :, one], 4, 0), edge[1, :, two])

    tile_rows = 4 * panels

    def landing(i):
        dr, dc = SIDES[i]
        if dc == 0:
            return got_row.at[0 if dr > 0 else 1]
        if dr == 0:
            return got_col.at[0 if dc > 0 else 1]
        return got_corner.at[(2 if dr < 0 else 0) + (1 if dc < 0 else 0)]

    def remote(i):
        dr, dc = SIDES[i]
        if dc == 0:
            source = send_row.at[0 if dr < 0 else 1]
        elif dr == 0:
            source = send_col.at[0 if dc < 0 else 1]
        else:
            source = edge.at[0 if dr < 0 else 1, :, pl.ds(0 if dc < 0 else (panels - 1) * LANES, LANES)]
        return pltpu.make_async_remote_copy(
            src_ref=source, dst_ref=landing(i), send_sem=send_sem.at[i], recv_sem=recv_sem.at[i],
            device_id=(row + dr, cols_at + dc), device_id_type=MESH,
        )

    def send():
        pl.semaphore_wait(barrier, count)
        each_side(lambda dr, dc: remote(SIDES.index((dr, dc))).start())

    at16 = iota((16, LANES), 1)
    in16 = iota((16, LANES), 0)
    owner = (at16 + 4) // 32, (at16 + 20) // 32
    codes = [
        (16 * tile + in16 - at16) * (1 - 2 * (at16 % 2)) for tile in (2 * owner[0], 2 * owner[1] - 1)
    ]
    wide_at = iota((16, 2 * LANES), 1) % LANES
    wide_owner = (wide_at + 4) // 32, (wide_at + 20) // 32
    blank = jnp.zeros((16, 2 * LANES), BF16)

    def weights(p, _):
        c = [jnp.broadcast_to(col[i, pl.ds(p, 1), :], (16, LANES)) for i in range(10)]
        none = jnp.zeros((16, LANES), F32)
        pairs = []
        for k in codes:
            z = k == 0, k == 1, k == 2, k == -2
            u = jnp.where(jnp.abs(k) == 4, c[7], none)
            u = jnp.where(k == 3, c[8], u)
            u = jnp.where(k == -1, c[9], u)
            u = jnp.where(z[0], c[3], jnp.where(z[1], c[4], jnp.where(z[2], c[5], jnp.where(z[3], c[6], u))))
            w = jnp.where(z[0], c[0], jnp.where(z[1], c[1], jnp.where(z[2] | z[3], c[2], none)))
            pairs.append(split(jnp.concatenate([u, w], axis=1)))

        def tile(i, part):
            odd = i % 2
            return jnp.where(wide_owner[odd] == (i + odd) // 2, pairs[odd][part], blank)

        for i in range(8):
            whi[p, 16 * i : 16 * i + 16, :] = tile(i, 0)
            wlo[p, 16 * i : 16 * i + 16, :] = tile(i, 1)
        before, after = [tile(-1, part) for part in (0, 1)], [tile(8, part) for part in (0, 1)]
        for i, value in enumerate((after[0], before[0], after[0], before[1], after[1], blank, blank, before[0])):
            wlo[p, LANES + 16 * i : LANES + 16 * i + 16, :] = value
        return 0

    lax.fori_loop(0, panels, weights, 0)

    def split_panel(p):
        for g in range(groups):
            e = vx[p, pl.ds(PAD + 16 * g, 8, stride=2), :]
            o = vx[p, pl.ds(PAD + 16 * g + 1, 8, stride=2), :]
            hi, lo = split(jnp.concatenate([e, o], axis=0))
            high[p, 16 * g : 16 * g + 16, :] = hi
            low[p, 16 * g : 16 * g + 16, :] = lo

    split_panel(1)
    split_panel(panels)

    def next_panel(p, _):
        load(p - 1).wait()
        split_panel(p)
        return 0

    lax.fori_loop(2, panels, next_panel, 0)
    odd = cols_at % 2 == 1
    pl.when(jnp.logical_not(distant | odd))(send)

    at_rows = iota((rows, LANES), 1)
    next_lanes = at_rows < LANES // 2
    low_lanes = (at_rows >= 16) & (at_rows < 48)
    again_lanes = (at_rows >= 48) & (at_rows < 80)

    def columns(p, w_ref):
        hi, lo = high[p], low[p]
        edge_hi = jnp.where(next_lanes, high[p + 1], high[p - 1])
        edge_lo = jnp.where(next_lanes, low[p + 1], low[p - 1])
        edges = jnp.where(
            low_lanes, pltpu.roll(edge_lo, 32, 1), jnp.where(again_lanes, pltpu.roll(edge_hi, 64, 1), edge_hi)
        )
        lhs = jnp.concatenate([hi, lo, hi, edges], axis=1)
        rhs = jnp.concatenate([whi[p - 1], whi[p - 1], wlo[p - 1]], axis=0)
        both = jnp.dot(lhs, rhs, preferred_element_type=F32)
        w_ref[...] = both
        u_edge[p - 1, 0:16, :] = both[0:16, :LANES]
        u_edge[p - 1, 16:32, :] = both[rows - 16 :, :LANES]

    def own_rows(p, w_ref):
        for g in range(groups):
            at = PAD + 16 * g
            e, o = vx[p, pl.ds(at, 8, stride=2), :], vx[p, pl.ds(at + 1, 8, stride=2), :]
            e_sum = vx[p, pl.ds(at - 2, 8, stride=2), :] + vx[p, pl.ds(at + 2, 8, stride=2), :]
            o_sum = vx[p, pl.ds(at - 1, 8, stride=2), :] + vx[p, pl.ds(at + 3, 8, stride=2), :]
            c = [half[n, 8 * g : 8 * g + 8, :] for n in range(4)]
            ge[p - 1, PAD + 8 * g : PAD + 8 * g + 8, :] = (
                e + w_ref[16 * g : 16 * g + 8, LANES:] + ((c[0] * e + c[2] * o) + (0.5 * d0) * e_sum)
            )
            go[p - 1, PAD + 8 * g : PAD + 8 * g + 8, :] = (
                o + w_ref[16 * g + 8 : 16 * g + 16, LANES:] + ((c[1] * o + c[3] * e) + (0.5 * d1) * o_sum)
            )
        for g in range(1, groups - 1):
            at = PAD + 8 * g
            e, o = ge[p - 1, at : at + 8, :], go[p - 1, at : at + 8, :]
            e_sum = ge[p - 1, at - 1 : at + 7, :] + ge[p - 1, at + 1 : at + 9, :]
            o_sum = go[p - 1, at - 1 : at + 7, :] + go[p - 1, at + 1 : at + 9, :]
            c = [full[n, 8 * g : 8 * g + 8, :] for n in range(4)]
            stage[p - 1, pl.ds(16 * g, 8, stride=2), :] = (
                w_ref[16 * g : 16 * g + 8, :LANES] + ((c[0] * e + c[2] * o) + d0 * e_sum)
            )
            stage[p - 1, pl.ds(16 * g + 1, 8, stride=2), :] = (
                w_ref[16 * g + 8 : 16 * g + 16, :LANES] + ((c[1] * o + c[3] * e) + d1 * o_sum)
            )

    columns(2, w_one)

    steps = (panels - 4) // 2
    place = cols_at // 2
    turn = jnp.clip(jnp.where(across[1], 4 - place, jnp.where(across[-1], 1 + place, 1)), 0, steps - 1)

    def middle(i, _):
        pl.when((distant | odd) & (i == turn))(send)
        p = 3 + 2 * i
        own_rows(p - 1, w_one)
        columns(p, w_two)
        own_rows(p, w_two)
        columns(p + 1, w_one)
        return 0

    lax.fori_loop(0, steps, middle, 0)
    own_rows(panels - 2, w_one)
    columns(panels - 1, w_two)

    def wait_recv(dr, dc):
        @pl.when(there(-dr, -dc))
        def _():
            remote(SIDES.index((dr, dc))).wait_recv()

    wait_recv(0, 1)
    wait_recv(0, -1)
    for side, panel, start in ((0, 0, LANES - 4), (1, panels + 1, 0)):
        packed = got_col[side]
        for g in range(groups):
            turn = (start - 4 * g) % LANES
            vx[panel, PAD + 16 * g : PAD + 16 * g + 16, :] = pltpu.roll(packed, turn, 1) if turn else packed
        split_panel(panel)

    own_rows(panels - 1, w_two)
    columns(1, w_one)
    own_rows(1, w_one)
    columns(panels, w_two)
    own_rows(panels, w_two)

    per_panel = LANES // 16
    even_lane = lane8 % 2 == 0

    def add_noise(g, t, move):
        c = [col[i, pl.ds(t, 1), :] for i in (0, 1, 2, 10, 11)]
        here = slice(8 * g, 8 * g + 8)
        f = [full[i, here, :] for i in range(4)]
        n_e, n_o, n_x = (noise[i, here, :] for i in range(3))
        gap = (move * (LANES // 2) + lane8 // 2) - (8 * (g % per_panel) + sub8)
        on, beside = gap == 0, jnp.abs(gap) == 1
        for odd, s_r, x_r, d_r, one, two, mine, mate in (
            (0, f[0], f[2], d0, c[3], c[4], jnp.where(even_lane, n_e, n_x), jnp.where(even_lane, n_x, n_e)),
            (1, f[1], f[3], d1, c[4], c[3], jnp.where(even_lane, n_x, n_o), jnp.where(even_lane, n_o, n_x)),
        ):
            centre = mine + 0.5 * ((s_r * one + x_r * two) + (c[0] * mine + c[1] * mate))
            side = 0.5 * (d_r * one + c[2] * mine)
            value = jnp.where(on, centre, jnp.where(beside, side, 0.0))
            if g in (0, groups - 1):
                at = 8 * odd + (16 if g else 0)
                u_edge[t, at : at + 8, :] += value
            else:
                stage[t, pl.ds(16 * g + odd, 8, stride=2), :] += value

    ratio = panels * LANES // rows
    first_panel = (row - cols_at * ratio) * (rows // LANES)

    @pl.when((first_panel >= 0) & (first_panel < panels))
    def _():
        for g in range(groups):
            t = first_panel + g // per_panel
            add_noise(g, t, 0)
            if g % per_panel == 0 and g:
                add_noise(g, t - 1, -1)
            if g % per_panel == per_panel - 1 and g < groups - 1:
                add_noise(g, t + 1, 1)

    @pl.when((first_panel >= 1) & (first_panel <= panels))
    def _():
        add_noise(0, first_panel - 1, -1)

    @pl.when((first_panel + rows // LANES >= 0) & (first_panel + rows // LANES < panels))
    def _():
        add_noise(groups - 1, first_panel + rows // LANES, 1)

    upper = sub8 < 4
    species = sub8 % 2 == 0
    for k in range(panels // 2):
        here = slice(8 * k, 8 * k + 8)
        one, two = 2 * k + 1, 2 * k + 2
        e = PAD + rows
        inner[0, here, :] = jnp.where(upper, vx[one, PAD - 2 : PAD + 6, :], vx[two, PAD - 6 : PAD + 2, :])
        inner[1, here, :] = jnp.where(upper, vx[one, e - 2 : e + 6, :], vx[two, e - 6 : e + 2, :])
        for i in range(3):
            halo_col[i, here, :] = jnp.where(upper, col[i, 2 * k : 2 * k + 1, :], col[i, 2 * k + 1 : 2 * k + 2, :])
    for side in (0, 1):
        voxel = jnp.clip(row * half_rows + (-1 if side == 0 else half_rows), 0, voxels - 1)
        pick = lane8 * 0 + voxel % LANES
        a = jnp.broadcast_to(feed_of[pl.ds(voxel // LANES, 1), :], (8, LANES))
        b = jnp.broadcast_to(conv_of[pl.ds(voxel // LANES, 1), :], (8, LANES))
        a = jnp.sum(jnp.where(lane8 == pick, a, 0.0), axis=1, keepdims=True)
        b = jnp.sum(jnp.where(lane8 == pick, b, 0.0), axis=1, keepdims=True)
        end = (voxel == 0) | (voxel == voxels - 1)
        near = jnp.where(end, 1.0, 2.0)
        d_r = jnp.where(species, d0, d1)
        halo_row[side, 0] = jnp.broadcast_to(STEP * jnp.where(species, b - 1.0, -a * a) - d_r * near, (8, LANES))
        halo_row[side, 1] = jnp.broadcast_to(STEP * jnp.where(species, a * a, -b), (8, LANES))
        halo_row[side, 2] = jnp.broadcast_to(d_r, (8, LANES))
        ok = there(-1, 0) if side == 0 else there(1, 0)
        halo_row[side, 3] = jnp.full((8, LANES), ok.astype(F32))

    for i, (dr, dc) in enumerate(SIDES):
        @pl.when(there(dr, dc))
        def _(i=i):
            remote(i).wait_send()

    for dr, dc in SIDES:
        if dr:
            wait_recv(dr, dc)


def finish_kernel(
    rows, panels,
    stage, u_edge, ge, go, full, spread, got_row, got_corner, inner, halo_col, halo_row,
    out, halo, tile_g, near_g, ends, wide, sem,
):
    d0, d1 = spread[0], spread[1]
    groups = rows // 16
    half_rows = rows // 2

    def store(p):
        return pltpu.make_async_copy(
            stage.at[p, pl.ds(16, rows - 32), :],
            out.at[pl.ds(16, rows - 32), pl.ds(p * LANES, LANES)],
            sem.at[p],
        )

    def store_end(side):
        return pltpu.make_async_copy(
            wide.at[side], out.at[pl.ds(side * (rows - 16), 16), :], sem.at[panels + side]
        )

    for p in range(panels):
        store(p).start()

    tile_rows = 4 * panels
    for side in (0, 1):
        left, right = got_corner[2 * side], got_corner[2 * side + 1]
        halo[side, 8 : 8 + tile_rows, :] = got_row[side]
        halo[side, 0:8, :] = left if side == 0 else pltpu.roll(left, 4, 0)
        halo[side, 8 + tile_rows : 16 + tile_rows, :] = pltpu.roll(right, 4, 0) if side == 0 else right

    lane8 = iota((8, LANES), 1)
    sub8 = iota((8, LANES), 0)
    even8 = lane8 % 2 == 0
    species = sub8 % 2 == 0
    for side in (0, 1):
        s_r, x_r, d_r = halo_row[side, 0], halo_row[side, 1], halo_row[side, 2]
        ok = halo_row[side, 3] > 0.5
        for k in range(panels // 2):
            at = 8 + 8 * k
            here = slice(8 * k, 8 * k + 8)
            tile, left, right = (halo[side, at + t : at + t + 8, :] for t in (0, -4, 4))
            mate = jnp.where(even8, pltpu.roll(tile, LANES - 1, 1), pltpu.roll(tile, 1, 1))
            beside = pltpu.roll(jnp.where(lane8 >= LANES - 2, left, tile), 2, 1) + pltpu.roll(
                jnp.where(lane8 < 2, right, tile), LANES - 2, 1
            )
            w = halo_col[0, here, :] * tile + halo_col[1, here, :] * mate + halo_col[2, here, :] * beside
            row_mate = jnp.where(species, halo[side, at + 1 : at + 9, :], halo[side, at - 1 : at + 7, :])
            away = halo[side, at - 2 : at + 6, :] if side == 0 else halo[side, at + 2 : at + 10, :]
            g = tile + w + 0.5 * (s_r * tile + x_r * row_mate + d_r * (away + inner[side, here, :]))
            tile_g[side, at : at + 8, :] = jnp.where(ok, g, 0.0)

        first = 0 if side == 0 else half_rows - 8
        c = [full[i, first : first + 8, :] for i in range(4)]
        for p in range(panels):
            at = 8 + 8 * (p // 2) + 4 * (p % 2)
            for o, ref, dd in ((0, ge, d0), (1, go, d1)):
                mine = ref[p, PAD + first : PAD + first + 8, :]
                if side == 0:
                    fix = halo[side, at + 2 + o : at + 10 + o, :]
                    near_g[o, 0:8, :] = tile_g[side, at + o - 5 : at + o + 3, :]
                    near_g[o, 16:24, :] = ref[p, PAD + 8 : PAD + 16, :]
                else:
                    fix = halo[side, at + o - 7 : at + o + 1, :]
                    near_g[o, 0:8, :] = ref[p, PAD + first - 8 : PAD + first, :]
                    near_g[o, 16:24, :] = tile_g[side, at + o : at + o + 8, :]
                fix = jnp.where(ok & (sub8 == (0 if side == 0 else 7)), (0.5 * dd) * fix, 0.0)
                near_g[o, 8:16, :] = mine + fix
            e, o = near_g[0, 8:16, :], near_g[1, 8:16, :]
            e_sum = near_g[0, 7:15, :] + near_g[0, 9:17, :]
            o_sum = near_g[1, 7:15, :] + near_g[1, 9:17, :]
            u = 16 * side
            ends[p, pl.ds(0, 8, stride=2), :] = u_edge[p, u : u + 8, :] + ((c[0] * e + c[2] * o) + d0 * e_sum)
            ends[p, pl.ds(1, 8, stride=2), :] = u_edge[p, u + 8 : u + 16, :] + ((c[1] * o + c[3] * e) + d1 * o_sum)
            wide[side, :, LANES * p : LANES * p + LANES] = ends[p, 0:16, :]
        store_end(side).start()

    for p in range(panels):
        store(p).wait()
    for side in (0, 1):
        store_end(side).wait()


def body(covariance, classes, feed_rate, conversion_rate, diffusion):
    rows, cols = covariance.shape
    panels = cols // LANES
    voxels = classes.shape[0]
    half_rows = rows // 2
    vmem = pl.BlockSpec(memory_space=pltpu.VMEM)
    hbm = pl.BlockSpec(memory_space=pl.ANY)
    sizes = (lax.axis_size("row"), lax.axis_size("col"))
    inputs = (covariance, classes.reshape(voxels // LANES, LANES), feed_rate, conversion_rate, diffusion)
    results = pl.pallas_call(
        functools.partial(advance_kernel, rows, panels, voxels, *sizes),
        out_shape=[
            pltpu.VMEM((panels, rows, LANES), F32),
            pltpu.VMEM((panels, 32, LANES), F32),
            pltpu.VMEM((panels, half_rows + 2 * PAD, LANES), F32),
            pltpu.VMEM((panels, half_rows + 2 * PAD, LANES), F32),
            pltpu.VMEM((4, half_rows, LANES), F32),
            pltpu.VMEM((2, 8, LANES), F32),
            pltpu.VMEM((2, 4 * panels, LANES), F32),
            pltpu.VMEM((4, 8, LANES), F32),
            pltpu.VMEM((2, 4 * panels, LANES), F32),
            pltpu.VMEM((3, 4 * panels, LANES), F32),
            pltpu.VMEM((2, 4, 8, LANES), F32),
        ],
        in_specs=[hbm] * 5,
        out_specs=[vmem] * 11,
        scratch_shapes=[
            pltpu.VMEM((panels + 2, rows + 2 * PAD, LANES), F32),
            pltpu.VMEM((panels + 2, rows, LANES), BF16),
            pltpu.VMEM((panels + 2, rows, LANES), BF16),
            pltpu.VMEM((panels, LANES, 2 * LANES), BF16),
            pltpu.VMEM((panels, 2 * LANES, 2 * LANES), BF16),
            pltpu.VMEM((rows, 2 * LANES), F32),
            pltpu.VMEM((rows, 2 * LANES), F32),
            pltpu.VMEM((4, half_rows, LANES), F32),
            pltpu.VMEM((3, half_rows, LANES), F32),
            pltpu.VMEM((voxels // LANES, LANES), F32),
            pltpu.VMEM((voxels // LANES, LANES), F32),
            pltpu.VMEM((panels + 16, LANES), F32),
            pltpu.VMEM((panels + 16, LANES), F32),
            pltpu.VMEM((panels + 16, LANES), F32),
            pltpu.VMEM((panels + 16, LANES), F32),
            pltpu.VMEM((12, panels, LANES), F32),
            pltpu.VMEM((voxels // LANES, LANES), jnp.int32),
            pltpu.SMEM(feed_rate.shape, F32),
            pltpu.SMEM(conversion_rate.shape, F32),
            pltpu.SMEM(diffusion.shape, F32),
            pltpu.VMEM((2, 8, cols), F32),
            pltpu.VMEM((2, 4 * panels, LANES), F32),
            pltpu.VMEM((2, 16, LANES), F32),
            pltpu.VMEM((2, 16, LANES), F32),
            pltpu.SemaphoreType.DMA((panels,)),
            pltpu.SemaphoreType.DMA((6,)),
            pltpu.SemaphoreType.DMA((8,)),
            pltpu.SemaphoreType.DMA((8,)),
        ],
        compiler_params=pltpu.CompilerParams(
            collective_id=0, has_side_effects=True, vmem_limit_bytes=32 << 20
        ),
        name="halo_and_columns",
    )(*(pltpu.with_memory_space_constraint(x, pltpu.HBM) for x in inputs))
    return pl.pallas_call(
        functools.partial(finish_kernel, rows, panels),
        out_shape=jax.ShapeDtypeStruct((rows, cols), F32),
        in_specs=[vmem] * 11,
        out_specs=hbm,
        scratch_shapes=[
            pltpu.VMEM((2, 4 * panels + 16, LANES), F32),
            pltpu.VMEM((2, 4 * panels + 16, LANES), F32),
            pltpu.VMEM((2, 24, LANES), F32),
            pltpu.VMEM((panels, 24, LANES), F32),
            pltpu.VMEM((2, 16, cols), F32),
            pltpu.SemaphoreType.DMA((panels + 2,)),
        ],
        compiler_params=pltpu.CompilerParams(vmem_limit_bytes=24 << 20),
        name="rows",
    )(*results)


def solution(mesh):
    in_specs = (P("row", "col"), P(), P(), P(), P())
    return jax.shard_map(body, mesh=mesh, in_specs=in_specs, out_specs=P("row", "col"), check_vma=False)
```
